128 devices in a mesh: view: 4 (over z), tile: 32 (over x, y, core).
Axes of the slice: x: 4, y: 4, z: 4, core: 2. Of those that a mesh axis runs over, the one named last changes fastest.
Arguments:
- params: float32 [59, 1048576], P(None, ('view', 'tile')), may hold values from -16 to 16, as said below
- send_list: int32 [128, 8192], P(('view', 'tile')), may hold values from 0 to 8191, as said below
- send_counts: int32 [128, 128], P(('view', 'tile')), may hold values from 0 to 64, as said below
- camera: float32 [8, 6], replicated, may hold values from -0.2 to 0.2
- ground_truth: float32 [8, 3, 512, 512], P('view', None, 'tile'), may hold values from 0 to 1
- tile_lists: int32 [8, 32, 32, 128], P('view', 'tile'), may hold values from 0 to 8191, as said below
- list_lengths: int32 [8, 32, 32], P('view', 'tile'), may hold values from 0 to 128, as said below
Outputs:
- gradients: float32 [59, 1048576], P(None, ('view', 'tile'))
The draws below stay inside these ranges and needn't reach their ends.
Inputs may be any that keep to these rules, and one draw needn't show every extreme that they name: `params`: every Gaussian lies at camera depth 1 or more in every view. `send_list`: each row is an ordering of 0 to 8191. `send_counts`: each row sums to at most 8192; some destination gets 64 from every source. `tile_lists`: live entries name slots s * 64 + k with k < send_counts[s, d] of the tile's destination d; entries past the length name any slot. `list_lengths`: some tile's list is full in every draw.
All inputs are finite; a program needn't handle non-finite values.
Results may differ from the reference program's by a relative error of at most 0.0003.
Values sent between devices are 32-bit elements; how exact they have to be, the bound alone decides.
A program may use at most 128 MiB of HBM per device.

```python
import jax
import jax.numpy as jnp
import numpy as np
from jax import lax

TILE = 16
VIEWS_DEV = 2
PARAMS = 59
TILE_COLS = 32
LIST = 128
G_DEV = 8192
VIEWS = 8
CAP = 64
HEIGHT = 512
WIDTH = 512
N_VIEW = 4
N_TILE = 32
DEVICES = 128


FOCAL = 1000.0


def matrix_product_drawn(left_side, right_side):
    return [[left_side[row_idx][0] * right_side[0][col_idx] + left_side[row_idx][1] * right_side[1][col_idx] + left_side[row_idx][2] * right_side[2][col_idx] for col_idx in range(3)] for row_idx in range(3)]


def rotation_drawn(angles):
    cos_a, sin_a = (jnp.cos(angles[0]), jnp.sin(angles[0]))
    cos_b, sin_b = (jnp.cos(angles[1]), jnp.sin(angles[1]))
    cos_c, sin_c = (jnp.cos(angles[2]), jnp.sin(angles[2]))
    about_x = [[1.0, 0.0, 0.0], [0.0, cos_a, -sin_a], [0.0, sin_a, cos_a]]
    about_y = [[cos_b, 0.0, sin_b], [0.0, 1.0, 0.0], [-sin_b, 0.0, cos_b]]
    about_z = [[cos_c, -sin_c, 0.0], [sin_c, cos_c, 0.0], [0.0, 0.0, 1.0]]
    return matrix_product_drawn(about_z, matrix_product_drawn(about_y, about_x))


def camera_values(key):
    cam_key = jax.random.fold_in(key, 11)
    angle_key, move_key = jax.random.split(cam_key)
    angles = jax.random.uniform(angle_key, (VIEWS, 3), jnp.float32, -0.03, 0.03)
    moves = jax.random.uniform(move_key, (VIEWS, 3), jnp.float32, -0.2, 0.2)
    return jnp.concatenate([angles, moves], axis=1)


def slot_plan(key):
    plan_key = jax.random.fold_in(key, 23)
    subkeys = jax.random.split(plan_key, 8)
    heavy_dest = jax.random.randint(subkeys[0], (DEVICES,), 0, 4) == 3
    load_level = jnp.where(heavy_dest, 4, 1).astype(jnp.int32)
    jitter = jax.random.randint(subkeys[1], (DEVICES, DEVICES), 0, CAP // 16 + 1)
    counts = load_level[None, :] * CAP // 4 - jitter
    full_dest = jax.random.randint(subkeys[2], (), 0, DEVICES)
    counts = jnp.where(jnp.arange(DEVICES)[None, :] == full_dest, CAP, counts).astype(jnp.int32)
    orders = jax.vmap(lambda sub_key: jax.random.permutation(sub_key, G_DEV))(jax.random.split(subkeys[3], DEVICES))
    home_cols = jax.random.randint(subkeys[4], (DEVICES, G_DEV), 0, TILE_COLS)
    depth_rank = jax.vmap(lambda sub_key: jax.random.permutation(sub_key, G_DEV))(jax.random.split(subkeys[5], DEVICES))
    moved_by = jax.random.randint(subkeys[6], (DEVICES, G_DEV), -1, 2) * (jax.random.randint(subkeys[7], (DEVICES, G_DEV), 0, 4) == 0).astype(jnp.int32)
    home_cols_two = jnp.clip(home_cols + moved_by, 0, TILE_COLS - 1)
    return (counts, orders.astype(jnp.int32), home_cols.astype(jnp.int32), home_cols_two.astype(jnp.int32), depth_rank.astype(jnp.int32))


def list_plan(key):
    counts, orders, home_cols, home_cols_two, depth_rank = slot_plan(key)
    limit_key = jax.random.fold_in(key, 29)
    limits = jax.random.randint(limit_key, (DEVICES, 2, TILE_COLS), LIST // 2, LIST + 1).astype(jnp.int32)
    is_full = jnp.all(counts == CAP, axis=0)
    limits = jnp.where(is_full[:, None, None], LIST, limits).astype(jnp.int32)
    slot_ids = jnp.arange(G_DEV, dtype=jnp.int32)
    col_ids = jnp.arange(TILE_COLS, dtype=jnp.int32)
    list_ids = jnp.arange(LIST, dtype=jnp.int32)

    def per_dest(target_counts, home_first, home_second, rank_row, limit_rows):
        is_live = slot_ids % CAP < target_counts[slot_ids // CAP]

        def per_view(home_row, limit_row):
            placed = jnp.where(is_live, home_row, TILE_COLS)
            order_key = placed * G_DEV + rank_row
            sequence = jnp.argsort(order_key)
            per_col = jnp.sum((placed[None, :] == col_ids[:, None]).astype(jnp.int32), axis=1)
            col_start = jnp.cumsum(per_col) - per_col
            spot_ids = jnp.minimum(col_start[:, None] + list_ids[None, :], G_DEV - 1)
            return (sequence[spot_ids].astype(jnp.int32), jnp.minimum(jnp.minimum(per_col, LIST), limit_row).astype(jnp.int32))
        first_lists, first_lengths = per_view(home_first, limit_rows[0])
        second_lists, second_lengths = per_view(home_second, limit_rows[1])
        return (jnp.stack([first_lists, second_lists]), jnp.stack([first_lengths, second_lengths]))
    all_lists, all_lengths = jax.vmap(per_dest)(counts.T, home_cols, home_cols_two, depth_rank, limits)
    all_lists = all_lists.reshape(N_VIEW, N_TILE, VIEWS_DEV, TILE_COLS, LIST).transpose(0, 2, 1, 3, 4).reshape(VIEWS, N_TILE, TILE_COLS, LIST)
    all_lengths = all_lengths.reshape(N_VIEW, N_TILE, VIEWS_DEV, TILE_COLS).transpose(0, 2, 1, 3).reshape(VIEWS, N_TILE, TILE_COLS)
    return (all_lists, all_lengths)


def draw_camera(key, part):
    shared = camera_values(key)
    key = jax.random.fold_in(key, 1)
    return shared


def draw_send_counts(key, part):
    shared = slot_plan(key)[0]
    key = jax.random.fold_in(key, 2)
    return shared


def draw_send_list(key, part):
    shared = slot_plan(key)[1]
    key = jax.random.fold_in(key, 4)
    return shared


def draw_tile_lists(key, part):
    planned = list_plan(key)
    key = jax.random.fold_in(key, 5)
    return planned[0]


def draw_list_lengths(key, part):
    planned = list_plan(key)
    key = jax.random.fold_in(key, 6)
    return planned[1]


def draw_params(key, part):
    counts, orders, home_cols, home_cols_two, depth_rank = slot_plan(key)
    cams = camera_values(key)
    key = jax.random.fold_in(key, 3)
    subkeys = jax.random.split(key, 12)
    position = jnp.argsort(orders, axis=1).astype(jnp.int32)
    run_ends = jnp.cumsum(counts, axis=1)
    run_starts = run_ends - counts
    target = jax.vmap(lambda end_row, pos_row: jnp.searchsorted(end_row, pos_row, side='right'))(run_ends, position).astype(jnp.int32)
    is_sent = target < DEVICES
    clipped = jnp.minimum(target, DEVICES - 1)
    inside_slot = position - jnp.take_along_axis(run_starts, clipped, axis=1)
    source_ids = jnp.arange(DEVICES, dtype=jnp.int32)[:, None]
    slot_index = jnp.clip(source_ids * CAP + inside_slot, 0, G_DEV - 1)
    home_sent = home_cols[clipped, slot_index]
    rank_sent = depth_rank[clipped, slot_index]
    random_dest = jax.random.randint(subkeys[0], (DEVICES, G_DEV), 0, DEVICES)
    random_col = jax.random.randint(subkeys[1], (DEVICES, G_DEV), 0, TILE_COLS)
    random_rank = jax.random.randint(subkeys[2], (DEVICES, G_DEV), 0, G_DEV)
    dest_eff = jnp.where(is_sent, clipped, random_dest)
    col_eff = jnp.where(is_sent, home_sent, random_col)
    rank_eff = jnp.where(is_sent, rank_sent, random_rank)
    offset_u = jax.random.uniform(subkeys[3], (DEVICES, G_DEV), jnp.float32, -2.0, TILE + 2.0)
    offset_v = jax.random.uniform(subkeys[4], (DEVICES, G_DEV), jnp.float32, -2.0, TILE + 2.0)
    pix_u = (col_eff * TILE).astype(jnp.float32) + offset_u
    pix_v = (dest_eff % N_TILE * TILE).astype(jnp.float32) + offset_v
    depth_val = 3.0 + 9.0 * (rank_eff.astype(jnp.float32) + jax.random.uniform(subkeys[5], (DEVICES, G_DEV), jnp.float32)) / G_DEV
    cam_rows = cams[VIEWS_DEV * (dest_eff // N_TILE)]
    cam_rot = rotation_drawn([cam_rows[..., 0], cam_rows[..., 1], cam_rows[..., 2]])
    relative = [(pix_u - WIDTH / 2.0) * depth_val / FOCAL - cam_rows[..., 3], (pix_v - HEIGHT / 2.0) * depth_val / FOCAL - cam_rows[..., 4], depth_val - cam_rows[..., 5]]
    world = [cam_rot[0][col_idx] * relative[0] + cam_rot[1][col_idx] * relative[1] + cam_rot[2][col_idx] * relative[2] for col_idx in range(3)]
    log_scales = jax.random.uniform(subkeys[6], (3, DEVICES, G_DEV), jnp.float32, -5.5, -3.9)
    quat_w = jax.random.uniform(subkeys[7], (1, DEVICES, G_DEV), jnp.float32, 0.5, 1.5)
    quat_rest = jax.random.uniform(subkeys[8], (3, DEVICES, G_DEV), jnp.float32, -1.0, 1.0)
    opacity_logit = jax.random.uniform(subkeys[9], (1, DEVICES, G_DEV), jnp.float32, -4.5, -1.5)
    colour_dc = jax.random.truncated_normal(subkeys[10], -2.5, 2.5, (3, 1, DEVICES, G_DEV), jnp.float32)
    colour_rest = 0.3 * jax.random.truncated_normal(subkeys[11], -2.5, 2.5, (3, 15, DEVICES, G_DEV), jnp.float32)
    sh_coeffs = jnp.concatenate([colour_dc, colour_rest], axis=1).reshape(48, DEVICES, G_DEV)
    stacked = jnp.concatenate([jnp.stack(world), log_scales, quat_w, quat_rest, opacity_logit, sh_coeffs], axis=0)
    return stacked.reshape(PARAMS, DEVICES * G_DEV).astype(jnp.float32)


def block_levels(rng, shape, cuts, least, top_value):
    def one(dim, parts):
        steps = jax.random.uniform(jax.random.fold_in(jax.random.fold_in(rng, 6), dim), (parts,), jnp.float32, least / len(cuts), top_value / len(cuts))
        return jnp.repeat(jnp.exp(steps), shape[dim] // parts).reshape((-1,) + (1,) * (len(shape) - dim - 1))

    gain = one(*cuts[0])
    for cut in cuts[1:]:
        gain = gain * one(*cut)
    return gain


def setup_inputs(seed: int = 0) -> dict:
    key_of = jax.random.split(jax.random.key(seed), 8)
    return {
        "params": draw_params(jax.random.fold_in(key_of[7], 71), 0),
        "send_list": draw_send_list(jax.random.fold_in(key_of[7], 71), 0),
        "send_counts": draw_send_counts(jax.random.fold_in(key_of[7], 71), 0),
        "camera": draw_camera(jax.random.fold_in(key_of[7], 71), 0),
        "ground_truth": jnp.clip(1.0 * jax.random.uniform(key_of[4], (VIEWS, 3, HEIGHT, WIDTH), jnp.float32) ** block_levels(key_of[4], (VIEWS, 3, HEIGHT, WIDTH), ((0, 4), (2, 32)), -0.2, 0.2), 0.0, 1.0),
        "tile_lists": draw_tile_lists(jax.random.fold_in(key_of[7], 71), 0),
        "list_lengths": draw_list_lengths(jax.random.fold_in(key_of[7], 71), 0),
    }


FOCAL = 1000.0
LOW_PASS = 0.3
SSIM_SHARE = 0.2
SMOOTH_EPS = 1e-06
SSIM_ONE = 0.0001
SSIM_TWO = 0.0009
HARMONIC_ZERO = 0.28209479177387814
HARMONIC_ONE = 0.4886025119029199
HARMONIC_TWO = (1.0925484305920792, -1.0925484305920792, 0.31539156525252005, -1.0925484305920792, 0.5462742152960396)
HARMONIC_THREE = (-0.5900435899266435, 2.890611442640554, -0.4570457994644658, 0.3731763325901154, -0.4570457994644658, 1.445305721320277, -0.5900435899266435)

def window_taps():
    offsets_np = np.arange(11) - 5.0
    weights = np.exp(-offsets_np * offsets_np / 4.5)
    weights = weights / weights.sum()
    return [float(weight) for weight in weights]

def matrix_product(left_side, right_side):
    return [[left_side[row_idx][0] * right_side[0][col_idx] + left_side[row_idx][1] * right_side[1][col_idx] + left_side[row_idx][2] * right_side[2][col_idx] for col_idx in range(3)] for row_idx in range(3)]

def rotation(angles):
    cos_a, sin_a = (jnp.cos(angles[0]), jnp.sin(angles[0]))
    cos_b, sin_b = (jnp.cos(angles[1]), jnp.sin(angles[1]))
    cos_c, sin_c = (jnp.cos(angles[2]), jnp.sin(angles[2]))
    about_x = [[1.0, 0.0, 0.0], [0.0, cos_a, -sin_a], [0.0, sin_a, cos_a]]
    about_y = [[cos_b, 0.0, sin_b], [0.0, 1.0, 0.0], [-sin_b, 0.0, cos_b]]
    about_z = [[cos_c, -sin_c, 0.0], [sin_c, cos_c, 0.0], [0.0, 0.0, 1.0]]
    return matrix_product(about_z, matrix_product(about_y, about_x))

def harmonics(dir_x, dir_y, dir_z):
    sq_x, sq_y, sq_z = (dir_x * dir_x, dir_y * dir_y, dir_z * dir_z)
    prod_xy, prod_yz, prod_xz = (dir_x * dir_y, dir_y * dir_z, dir_x * dir_z)
    return [HARMONIC_ZERO + 0.0 * dir_x, -HARMONIC_ONE * dir_y, HARMONIC_ONE * dir_z, -HARMONIC_ONE * dir_x, HARMONIC_TWO[0] * prod_xy, HARMONIC_TWO[1] * prod_yz, HARMONIC_TWO[2] * (2.0 * sq_z - sq_x - sq_y), HARMONIC_TWO[3] * prod_xz, HARMONIC_TWO[4] * (sq_x - sq_y), HARMONIC_THREE[0] * dir_y * (3.0 * sq_x - sq_y), HARMONIC_THREE[1] * prod_xy * dir_z, HARMONIC_THREE[2] * dir_y * (4.0 * sq_z - sq_x - sq_y), HARMONIC_THREE[3] * dir_z * (2.0 * sq_z - 3.0 * sq_x - 3.0 * sq_y), HARMONIC_THREE[4] * dir_x * (4.0 * sq_z - sq_x - sq_y), HARMONIC_THREE[5] * dir_z * (sq_x - sq_y), HARMONIC_THREE[6] * dir_x * (sq_x - 3.0 * sq_y)]

def project(gaussians, camera_row, image_width, image_height):
    mean_x, mean_y, mean_z = (gaussians[0], gaussians[1], gaussians[2])
    scales = [jnp.exp(gaussians[3 + axis_num]) for axis_num in range(3)]
    quat_norm = jnp.sqrt(gaussians[6] * gaussians[6] + gaussians[7] * gaussians[7] + gaussians[8] * gaussians[8] + gaussians[9] * gaussians[9])
    quat_w, quat_x, quat_y, quat_z = (gaussians[6] / quat_norm, gaussians[7] / quat_norm, gaussians[8] / quat_norm, gaussians[9] / quat_norm)
    quat_rot = [[1.0 - 2.0 * (quat_y * quat_y + quat_z * quat_z), 2.0 * (quat_x * quat_y - quat_w * quat_z), 2.0 * (quat_x * quat_z + quat_w * quat_y)], [2.0 * (quat_x * quat_y + quat_w * quat_z), 1.0 - 2.0 * (quat_x * quat_x + quat_z * quat_z), 2.0 * (quat_y * quat_z - quat_w * quat_x)], [2.0 * (quat_x * quat_z - quat_w * quat_y), 2.0 * (quat_y * quat_z + quat_w * quat_x), 1.0 - 2.0 * (quat_x * quat_x + quat_y * quat_y)]]
    cam_rot = rotation(camera_row[0:3])
    translation = camera_row[3:6]
    point = [cam_rot[row_idx][0] * mean_x + cam_rot[row_idx][1] * mean_y + cam_rot[row_idx][2] * mean_z + translation[row_idx] for row_idx in range(3)]
    rotated = matrix_product(cam_rot, quat_rot)
    spread = [[rotated[row_idx][col_idx] * scales[col_idx] for col_idx in range(3)] for row_idx in range(3)]
    inv_depth = 1.0 / point[2]
    jac_xx = FOCAL * inv_depth
    jac_xz = -FOCAL * point[0] * inv_depth * inv_depth
    jac_yz = -FOCAL * point[1] * inv_depth * inv_depth
    proj_x = [jac_xx * spread[0][col_idx] + jac_xz * spread[2][col_idx] for col_idx in range(3)]
    proj_y = [jac_xx * spread[1][col_idx] + jac_yz * spread[2][col_idx] for col_idx in range(3)]
    cov_xx = proj_x[0] * proj_x[0] + proj_x[1] * proj_x[1] + proj_x[2] * proj_x[2] + LOW_PASS
    cov_xy = proj_x[0] * proj_y[0] + proj_x[1] * proj_y[1] + proj_x[2] * proj_y[2]
    cov_yy = proj_y[0] * proj_y[0] + proj_y[1] * proj_y[1] + proj_y[2] * proj_y[2] + LOW_PASS
    determinant = cov_xx * cov_yy - cov_xy * cov_xy
    centre_u = FOCAL * point[0] * inv_depth + image_width / 2.0
    centre_v = FOCAL * point[1] * inv_depth + image_height / 2.0
    opacity = 0.99 * jax.nn.sigmoid(gaussians[10])
    anchor = [-(cam_rot[0][col_idx] * translation[0] + cam_rot[1][col_idx] * translation[1] + cam_rot[2][col_idx] * translation[2]) for col_idx in range(3)]
    ray_x, ray_y, ray_z = (mean_x - anchor[0], mean_y - anchor[1], mean_z - anchor[2])
    ray_len = jnp.sqrt(ray_x * ray_x + ray_y * ray_y + ray_z * ray_z)
    basis_list = harmonics(ray_x / ray_len, ray_y / ray_len, ray_z / ray_len)
    colours = []
    for channel in range(3):
        summed = 0.5 + 0.0 * mean_x
        for harmonic in range(16):
            summed = summed + basis_list[harmonic] * gaussians[11 + 16 * channel + harmonic]
        colours.append(summed)
    return jnp.stack([centre_u, centre_v, cov_yy / determinant, -cov_xy / determinant, cov_xx / determinant, opacity] + colours)

def composite(pieces, lengths, columns, tile_row, start_at, span_len):
    pieces = lax.slice_in_dim(pieces, start_at, start_at + span_len, axis=2)
    pixel_ids = jnp.arange(TILE * TILE, dtype=jnp.int32)
    pix_x = (columns[:, None] * TILE + pixel_ids[None, :] % TILE).astype(jnp.float32)
    pix_y = (tile_row * TILE + pixel_ids // TILE).astype(jnp.float32)
    delta_x = pieces[0][:, None, :] - pix_x[:, :, None]
    delta_y = pieces[1][:, None, :] - pix_y[None, :, None]
    exponent = -0.5 * (pieces[2][:, None, :] * delta_x * delta_x + pieces[4][:, None, :] * delta_y * delta_y) - pieces[3][:, None, :] * delta_x * delta_y
    list_ranks = start_at + jnp.arange(span_len, dtype=jnp.int32)
    live_mask = list_ranks[None, :] < lengths[:, None]
    opacity_at = jnp.where(live_mask[:, None, :], pieces[5][:, None, :] * jnp.exp(exponent), 0.0)
    log_keep = jnp.log1p(-opacity_at)
    before = jnp.cumsum(log_keep, axis=2) - log_keep
    weights = jnp.exp(before) * opacity_at
    colour = jnp.einsum('npc,knc->nkp', weights, pieces[6:9], precision=lax.Precision.HIGHEST)
    return (colour, lax.optimization_barrier(jnp.sum(log_keep, axis=2)))

def render(features, tile_lists_in, lengths, tile_row):
    slot_count = features.shape[2]
    tile_cols = tile_lists_in.shape[1]
    list_len = tile_lists_in.shape[2]
    feature_table = jnp.transpose(features, (1, 0, 2)).reshape(9, 2 * slot_count)
    view_base = (jnp.arange(2, dtype=jnp.int32) * slot_count)[:, None, None]
    flat_lists = (tile_lists_in + view_base).reshape(-1, 8, list_len)
    flat_lengths = lengths.reshape(-1, 8)
    columns = jnp.tile(jnp.arange(tile_cols, dtype=jnp.int32), 2).reshape(-1, 8)

    def one_block(block_items):
        block_lists, block_lengths, block_columns = block_items
        pieces = feature_table[:, block_lists]
        return composite(pieces, block_lengths, block_columns, tile_row, 0, list_len)[0]
    colours = lax.map(one_block, (flat_lists, flat_lengths, columns))
    colours = colours.reshape(2, tile_cols, 3, TILE, TILE)
    return jnp.transpose(colours, (0, 2, 3, 1, 4)).reshape(2, 3, TILE, tile_cols * TILE)

def blur_columns(images):
    col_total = images.shape[-1]
    padded_cols = jnp.pad(images, [(0, 0)] * (images.ndim - 1) + [(5, 5)])
    result = 0.0
    for shift_num, weight in enumerate(window_taps()):
        result = result + weight * padded_cols[..., shift_num:shift_num + col_total]
    return result

def blur_rows(images):
    row_total = images.shape[-2] - 10
    result = 0.0
    for shift_num, weight in enumerate(window_taps()):
        result = result + weight * images[..., shift_num:shift_num + row_total, :]
    return result

def structure_map(images, targets):

    def blurred(values):
        return blur_rows(blur_columns(values))
    mean_one = blurred(images)
    mean_two = blurred(targets)
    var_one = blurred(images * images) - mean_one * mean_one
    var_two = blurred(targets * targets) - mean_two * mean_two
    cross_var = blurred(images * targets) - mean_one * mean_two
    numerator = (2.0 * mean_one * mean_two + SSIM_ONE) * (2.0 * cross_var + SSIM_TWO)
    denominator = (mean_one * mean_one + mean_two * mean_two + SSIM_ONE) * (var_one + var_two + SSIM_TWO)
    return numerator / denominator

def image_loss(images, targets):
    pad_rows = ((0, 0), (0, 0), (5, 5), (0, 0))
    similarity = structure_map(jnp.pad(images, pad_rows), jnp.pad(targets, pad_rows))
    difference = images - targets
    return SSIM_SHARE * jnp.sum(1.0 - similarity) + (1.0 - SSIM_SHARE) * jnp.sum(jnp.sqrt(difference * difference + SMOOTH_EPS))

def reference(params, send_list, send_counts, camera, ground_truth, tile_lists, list_lengths):
    starts = jnp.cumsum(send_counts, axis=1) - send_counts
    sources = jnp.arange(DEVICES, dtype=jnp.int32)
    slot_range = jnp.arange(CAP, dtype=jnp.int32)
    grouped_lists = tile_lists.reshape(N_VIEW, VIEWS_DEV, N_TILE, TILE_COLS, LIST)
    grouped_lengths = list_lengths.reshape(N_VIEW, VIEWS_DEV, N_TILE, TILE_COLS)
    grouped_cams = camera.reshape(N_VIEW, VIEWS_DEV, 6)

    def total_loss(weights_in):

        def one_band(target):
            view_group = target // N_TILE
            tile_row = target % N_TILE
            slot_pos = jnp.minimum(starts[:, target][:, None] + slot_range[None, :], G_DEV - 1).astype(jnp.int32)
            local_ids = jnp.take_along_axis(send_list, slot_pos, axis=1)
            global_ids = (sources[:, None] * G_DEV + local_ids).reshape(-1)
            arrived = weights_in[:, global_ids]
            cams_here = grouped_cams[view_group]
            features = jnp.stack([project(arrived, [cams_here[view_slot, entry_num] for entry_num in range(6)], float(WIDTH), float(HEIGHT)) for view_slot in range(VIEWS_DEV)])
            return render(features, grouped_lists[view_group][:, tile_row], grouped_lengths[view_group][:, tile_row], tile_row)
        all_bands = lax.map(jax.checkpoint(one_band), sources)
        images = all_bands.reshape(N_VIEW, N_TILE, VIEWS_DEV, 3, TILE, WIDTH).transpose(0, 2, 3, 1, 4, 5).reshape(VIEWS, 3, HEIGHT, WIDTH)
        return image_loss(images, ground_truth)
    return jax.grad(total_loss)(params)
```

```python
import jax
import jax.numpy as jnp
import numpy as np
from jax import lax
from jax.experimental import pallas as pl
from jax.experimental.pallas import tpu as pltpu
from jax.sharding import PartitionSpec as P

F32 = jnp.float32
BF16 = jnp.bfloat16
I32 = jnp.int32

TILE = 16
FOCAL = 1000.0
LOW_PASS = 0.3
SSIM_SHARE = 0.2
SMOOTH_EPS = 1e-06
SSIM_ONE = 0.0001
SSIM_TWO = 0.0009
LOG2E = 1.4426950408889634
HARMONIC_ZERO = 0.28209479177387814
HARMONIC_ONE = 0.4886025119029199
HARMONIC_TWO = (
    1.0925484305920792,
    -1.0925484305920792,
    0.31539156525252005,
    -1.0925484305920792,
    0.5462742152960396,
)
HARMONIC_THREE = (
    -0.5900435899266435,
    2.890611442640554,
    -0.4570457994644658,
    0.3731763325901154,
    -0.4570457994644658,
    1.445305721320277,
    -0.5900435899266435,
)
VMEM_BYTES = 56 * 1024 * 1024
NT = (((1,), (1,)), ((), ()))
NN = (((1,), (0,)), ((), ()))
TN = (((0,), (0,)), ((), ()))


def window_taps():
    offsets_np = np.arange(11) - 5.0
    weights = np.exp(-offsets_np * offsets_np / 4.5)
    weights = weights / weights.sum()
    return [float(weight) for weight in weights]


TAPS = window_taps()


def matrix_product(left_side, right_side):
    return [
        [
            left_side[row_idx][0] * right_side[0][col_idx]
            + left_side[row_idx][1] * right_side[1][col_idx]
            + left_side[row_idx][2] * right_side[2][col_idx]
            for col_idx in range(3)
        ]
        for row_idx in range(3)
    ]


def rotation(angles):
    cos_a, sin_a = (jnp.cos(angles[0]), jnp.sin(angles[0]))
    cos_b, sin_b = (jnp.cos(angles[1]), jnp.sin(angles[1]))
    cos_c, sin_c = (jnp.cos(angles[2]), jnp.sin(angles[2]))
    zero, one = jnp.zeros_like(cos_a), jnp.ones_like(cos_a)
    about_x = [[one, zero, zero], [zero, cos_a, -sin_a], [zero, sin_a, cos_a]]
    about_y = [[cos_b, zero, sin_b], [zero, one, zero], [-sin_b, zero, cos_b]]
    about_z = [[cos_c, -sin_c, zero], [sin_c, cos_c, zero], [zero, zero, one]]
    return matrix_product(about_z, matrix_product(about_y, about_x))


def camera_table(camera):
    rot = rotation([camera[:, 0], camera[:, 1], camera[:, 2]])
    move = [camera[:, 3], camera[:, 4], camera[:, 5]]
    anchor = [
        -(rot[0][c] * move[0] + rot[1][c] * move[1] + rot[2][c] * move[2]) for c in range(3)
    ]
    flat = rot[0] + rot[1] + rot[2] + move + anchor + [jnp.zeros_like(move[0])]
    return jnp.stack(flat, axis=1)


def harmonics(dir_x, dir_y, dir_z):
    sq_x, sq_y, sq_z = (dir_x * dir_x, dir_y * dir_y, dir_z * dir_z)
    prod_xy, prod_yz, prod_xz = (dir_x * dir_y, dir_y * dir_z, dir_x * dir_z)
    return [
        None,
        -HARMONIC_ONE * dir_y,
        HARMONIC_ONE * dir_z,
        -HARMONIC_ONE * dir_x,
        HARMONIC_TWO[0] * prod_xy,
        HARMONIC_TWO[1] * prod_yz,
        HARMONIC_TWO[2] * (2.0 * sq_z - sq_x - sq_y),
        HARMONIC_TWO[3] * prod_xz,
        HARMONIC_TWO[4] * (sq_x - sq_y),
        HARMONIC_THREE[0] * dir_y * (3.0 * sq_x - sq_y),
        HARMONIC_THREE[1] * prod_xy * dir_z,
        HARMONIC_THREE[2] * dir_y * (4.0 * sq_z - sq_x - sq_y),
        HARMONIC_THREE[3] * dir_z * (2.0 * sq_z - 3.0 * sq_x - 3.0 * sq_y),
        HARMONIC_THREE[4] * dir_x * (4.0 * sq_z - sq_x - sq_y),
        HARMONIC_THREE[5] * dir_z * (sq_x - sq_y),
        HARMONIC_THREE[6] * dir_x * (sq_x - 3.0 * sq_y),
    ]


def shape_values(gauss):
    scales = [jnp.exp(gauss[axis]) for axis in range(3)]
    norm_inv = 1.0 / jnp.sqrt(
        gauss[3] * gauss[3] + gauss[4] * gauss[4] + gauss[5] * gauss[5] + gauss[6] * gauss[6]
    )
    quat_w, quat_x, quat_y, quat_z = [gauss[3 + n] * norm_inv for n in range(4)]
    quat_rot = [
        [
            1.0 - 2.0 * (quat_y * quat_y + quat_z * quat_z),
            2.0 * (quat_x * quat_y - quat_w * quat_z),
            2.0 * (quat_x * quat_z + quat_w * quat_y),
        ],
        [
            2.0 * (quat_x * quat_y + quat_w * quat_z),
            1.0 - 2.0 * (quat_x * quat_x + quat_z * quat_z),
            2.0 * (quat_y * quat_z - quat_w * quat_x),
        ],
        [
            2.0 * (quat_x * quat_z - quat_w * quat_y),
            2.0 * (quat_y * quat_z + quat_w * quat_x),
            1.0 - 2.0 * (quat_x * quat_x + quat_y * quat_y),
        ],
    ]
    spread = [[quat_rot[r][c] * scales[c] for c in range(3)] for r in range(3)]

    def dot_rows(one, two):
        return (
            spread[one][0] * spread[two][0]
            + spread[one][1] * spread[two][1]
            + spread[one][2] * spread[two][2]
        )

    return [
        dot_rows(0, 0),
        dot_rows(0, 1),
        dot_rows(0, 2),
        dot_rows(1, 1),
        dot_rows(1, 2),
        dot_rows(2, 2),
    ]


def colour_basis(mean, anchor):
    ray_x, ray_y, ray_z = (mean[0] - anchor[0], mean[1] - anchor[1], mean[2] - anchor[2])
    len_inv = 1.0 / jnp.sqrt(ray_x * ray_x + ray_y * ray_y + ray_z * ray_z)
    return harmonics(ray_x * len_inv, ray_y * len_inv, ray_z * len_inv)


def image_values(gauss, cam):
    point = [
        cam[3 * r] * gauss[0] + cam[3 * r + 1] * gauss[1] + cam[3 * r + 2] * gauss[2] + cam[9 + r]
        for r in range(3)
    ]
    inv_depth = 1.0 / point[2]
    jac = FOCAL * inv_depth
    jac_xz = -FOCAL * point[0] * inv_depth * inv_depth
    jac_yz = -FOCAL * point[1] * inv_depth * inv_depth
    row_x = [jac * cam[c] + jac_xz * cam[6 + c] for c in range(3)]
    row_y = [jac * cam[3 + c] + jac_yz * cam[6 + c] for c in range(3)]
    s_xx, s_xy, s_xz, s_yy, s_yz, s_zz = gauss[3:9]
    by_x = [
        s_xx * row_x[0] + s_xy * row_x[1] + s_xz * row_x[2],
        s_xy * row_x[0] + s_yy * row_x[1] + s_yz * row_x[2],
        s_xz * row_x[0] + s_yz * row_x[1] + s_zz * row_x[2],
    ]
    by_y = [
        s_xx * row_y[0] + s_xy * row_y[1] + s_xz * row_y[2],
        s_xy * row_y[0] + s_yy * row_y[1] + s_yz * row_y[2],
        s_xz * row_y[0] + s_yz * row_y[1] + s_zz * row_y[2],
    ]
    cov_xx = row_x[0] * by_x[0] + row_x[1] * by_x[1] + row_x[2] * by_x[2] + LOW_PASS
    cov_xy = row_y[0] * by_x[0] + row_y[1] * by_x[1] + row_y[2] * by_x[2]
    cov_yy = row_y[0] * by_y[0] + row_y[1] * by_y[1] + row_y[2] * by_y[2] + LOW_PASS
    det_inv = 1.0 / (cov_xx * cov_yy - cov_xy * cov_xy)
    return [
        FOCAL * point[0] * inv_depth + 256.0,
        FOCAL * point[1] * inv_depth + 256.0,
        cov_yy * det_inv,
        -cov_xy * det_inv,
        cov_xx * det_inv,
    ]


def split3(value):
    one = value.astype(BF16)
    rest = value - one.astype(F32)
    two = rest.astype(BF16)
    three = (rest - two.astype(F32)).astype(BF16)
    return one, two, three


def split2(value):
    one = value.astype(BF16)
    return one, (value - one.astype(F32)).astype(BF16)


def dot(left, right, dims):
    return lax.dot_general(left, right, dims, preferred_element_type=F32)


def iota(shape, dim):
    return lax.broadcasted_iota(I32, shape, dim)


def high_onehot(idx):
    high = ((idx >> 12) << 7) | (idx & 127)
    return jnp.where(iota((256, idx.shape[1]), 0) == high, 1.0, 0.0).astype(BF16)


def low_mask(idx):
    return iota((32, idx.shape[1]), 0) == ((idx >> 7) & 31)


def pick(tables, onehot, mask, rows):
    total = dot(tables[0], onehot, NN)
    for table in tables[1:]:
        total = total + dot(table, onehot, NN)
    picked = jnp.where(mask[None], total.reshape(rows, 32, mask.shape[1]), 0.0)
    return jnp.sum(picked, axis=1)


def spread_rows(rows, mask):
    count = rows.shape[0]
    return jnp.where(mask[None], rows[:, None, :], 0.0).reshape(count * 32, rows.shape[1])


def half_roll(value):
    return pltpu.roll(value, 64, 1)


def first_half():
    return iota((8, 128), 1) < 64


def load_params(params, blocks):
    for row in range(64):
        blocks[pl.ds(row * 64, 59), :] = params[:, row * 128 : (row + 1) * 128]


def group_anchors(cam, group):
    anchors = []
    for slot in range(2):
        triple = []
        for c in range(3):
            value = jnp.full(group.shape, cam[slot, 12 + c], F32)
            for number in range(1, 4):
                value = jnp.where(group > number + 0.5, cam[2 * number + slot, 12 + c], value)
            triple.append(value)
        anchors.append(triple)
    return anchors


def send_kernel(cam, params, slist, counts, send, group_out, chosen, blocks, tab, t0, t1, t2, hot, stab, pos, val):
    cnt = counts[...].astype(F32)
    lanes = iota((32, 128), 1)
    first = iota((32, 128), 0) * 4
    slot_lane = iota((32, 256), 1)
    off = jnp.zeros((32, 256), F32)
    own = jnp.zeros((32, 256), F32)
    for j in range(4):
        off_j = jnp.sum(jnp.where(lanes < first + j, cnt, 0.0), axis=1, keepdims=True)
        own_j = jnp.sum(jnp.where(lanes == first + j, cnt, 0.0), axis=1, keepdims=True)
        here = (slot_lane >> 6) == j
        off = jnp.where(here, off_j, off)
        own = jnp.where(here, own_j, own)
    place = (slot_lane & 63).astype(F32)
    pos[...] = jnp.minimum(off + place, 8191.0).astype(I32)
    group = (iota((32, 256), 0) >> 3).astype(F32) + 1.0
    val[...] = jnp.where(place < own, group, 0.0)
    for row in range(64):
        piece = slist[:, row * 128 : (row + 1) * 128]
        half = slice((row // 32) * 128, (row // 32) * 128 + 128)
        stab[row % 32 : row % 32 + 1, half] = (piece >> 6).astype(F32)
        stab[32 + row % 32 : 33 + row % 32, half] = (piece & 63).astype(F32)
    load_params(params, blocks)
    group_out[...] = jnp.zeros((32, 256), F32)
    stab_b = stab[...].astype(BF16)

    def choose(p, carry):
        idx = pos[pl.ds(p, 1), :]
        found = dot(stab_b, high_onehot(idx), NN)
        both = found[0:32] * 64.0 + found[32:64]
        ids = jnp.sum(jnp.where(low_mask(idx), both, 0.0), axis=0, keepdims=True).astype(I32)
        chosen[pl.ds(p, 1), :] = ids
        onehot = high_onehot(ids)
        hot[pl.ds(pl.multiple_of(p * 256, 256), 256), :] = onehot
        left = jnp.where(low_mask(ids), val[pl.ds(p, 1), :], 0.0).astype(BF16)
        group_out[...] += dot(left, onehot, NT)
        return carry

    lax.fori_loop(0, 32, choose, 0)

    for high in range(2):
        lane_part = slice(high * 128, high * 128 + 128)

        def compute(low, carry):
            base = (high * 4 + low) * 512
            row0 = pl.multiple_of(low * 8, 8)

            def load(p):
                return blocks[pl.ds(base + p, 8, stride=64), :]

            anchors = group_anchors(cam, group_out[pl.ds(row0, 8), lane_part])
            mean = [load(0), load(1), load(2)]
            values = mean + [0.99 / (1.0 + jnp.exp(-load(10)))]
            values += shape_values([load(3 + n) for n in range(7)])
            bases = [colour_basis(mean, anchor) for anchor in anchors]
            sums = [[None] * 3, [None] * 3]
            for c in range(3):
                flat = 0.5 + HARMONIC_ZERO * load(11 + 16 * c)
                sums[0][c] = flat
                sums[1][c] = flat
                for k in range(1, 16):
                    coef = load(11 + 16 * c + k)
                    sums[0][c] = sums[0][c] + bases[0][k] * coef
                    sums[1][c] = sums[1][c] + bases[1][k] * coef
            values += sums[0] + sums[1]
            for f in range(16):
                tab[pl.ds(f * 32 + row0, 8), lane_part] = values[f]
            return carry

        lax.fori_loop(0, 4, compute, 0)

    t0[...], t1[...], t2[...] = split3(tab[...])
    is_first = first_half()

    def gather(p, carry):
        onehot = hot[pl.ds(pl.multiple_of(p * 256, 256), 256), :]
        mask = low_mask(chosen[pl.ds(p, 1), :])
        rows = []
        for part in range(2):
            cut = pl.ds(part * 256, 256)
            rows.append(pick([t0[cut, :], t1[cut, :], t2[cut, :]], onehot, mask, 8))
        for b in range(2):
            one = rows[0][:, b * 128 : b * 128 + 128]
            two = rows[1][:, b * 128 : b * 128 + 128]
            start = pl.multiple_of(p * 32 + b * 16, 16)
            send[pl.ds(start, 8), :] = jnp.where(is_first, one, half_roll(two))
            send[pl.ds(start + 8, 8), :] = jnp.where(is_first, half_roll(one), two)
        return carry

    lax.fori_loop(0, 32, gather, 0)


def unpack_slots(recv, q):
    is_first = first_half()
    low, high = [], []
    for f in range(8):
        even = recv[pl.ds(q * 128 + f, 8, stride=16), :]
        odd = recv[pl.ds(q * 128 + 8 + f, 8, stride=16), :]
        low.append(jnp.where(is_first, even, half_roll(odd)))
        high.append(jnp.where(is_first, half_roll(even), odd))
    return low + high


def block_transpose(value):
    turn = (iota((8, 128), 0) - (iota((8, 128), 1) >> 4)) & 7
    result = value
    for d in range(1, 8):
        moved = pltpu.roll(pltpu.roll(value, d, 0), 128 - 16 * d, 1)
        result = jnp.where(turn == d, moved, result)
    return result


def triangle(keep):
    return jnp.where(keep, 1.0, 0.0).astype(BF16)


def pixel_rows(feat, column, tile_row):
    def row(f):
        return jnp.broadcast_to(feat[f : f + 1, :], (16, 128))

    shift = iota((16, 128), 0).astype(F32) + (column * 16).astype(F32)
    delta_x = row(0) - shift
    square = (-0.5 * LOG2E) * row(2) * delta_x * delta_x
    cross = -LOG2E * row(3) * delta_x
    quad = (-0.5 * LOG2E) * row(4)
    delta_v = row(1) - (tile_row * 16).astype(F32)
    return delta_x, delta_v, square, cross, quad, row(5)


def tile_weights(feat, column, tile_row, tri, alpha, pair):
    delta_x, delta_v, square, cross, quad, opacity = pixel_rows(feat, column, tile_row)
    for j in range(16):
        delta_y = delta_v - float(j)
        value = opacity * jnp.exp2(square + delta_y * (cross + quad * delta_y))
        rows = slice(j * 16, j * 16 + 16)
        alpha[rows, :] = value
        one, two = split2(jnp.log(1.0 - value))
        pair[rows, 0:128] = one
        pair[rows, 128:256] = two
    return jnp.exp(dot(pair[...], tri, NN)) * alpha[...], delta_x, delta_v


def stack_splits(value, order):
    one, two, three = split3(value)
    parts = [one.astype(F32), two.astype(F32), three.astype(F32)]
    return jnp.concatenate([parts[n] for n in order], axis=0).astype(BF16)


def render_kernel(own, place, lens, recv, lists, image, feats, tab, t0, t1, t2, alpha, pair, left, right, frame):
    for high in range(2):
        lane_part = slice(high * 128, high * 128 + 128)

        def compute(low, carry):
            row0 = pl.multiple_of(low * 8, 8)
            values = unpack_slots(recv, high * 4 + low)
            gauss = values[0:3] + values[4:10]
            for w in range(2):
                seen = image_values(gauss, [own[w, n] for n in range(12)])
                seen = seen + [values[3]] + values[10 + 3 * w : 13 + 3 * w]
                for f in range(9):
                    tab[pl.ds((w * 9 + f) * 32 + row0, 8), lane_part] = seen[f]
            return carry

        lax.fori_loop(0, 4, compute, 0)
    t0[...], t1[...], t2[...] = split3(tab[...])
    lane = iota((1, 256), 1)

    for w in range(2):
        cut = slice(w * 288, w * 288 + 288)

        def look_up(pair_no, carry):
            tile = w * 32 + pair_no * 2
            idx = jnp.concatenate([lists[pl.ds(tile, 1), :], lists[pl.ds(tile + 1, 1), :]], axis=1)
            rows = pick([t0[cut, :], t1[cut, :], t2[cut, :]], high_onehot(idx), low_mask(idx), 9)
            length = jnp.where(lane < 128, lens[tile], lens[tile + 1])
            rows = jnp.where((lane & 127) < length, rows, 0.0)
            start = pl.multiple_of(tile * 16, 32)
            for b in range(2):
                part = rows[:, b * 128 : b * 128 + 128]
                feats[pl.ds(start + b * 16, 6), :] = part[0:6]
                feats[pl.ds(start + b * 16 + 6, 2), :] = jnp.zeros((2, 128), F32)
                feats[pl.ds(start + b * 16 + 8, 3), :] = part[6:9]
                feats[pl.ds(start + b * 16 + 11, 5), :] = jnp.zeros((5, 128), F32)
            return carry

        lax.fori_loop(0, 16, look_up, 0)

    tri = triangle((iota((256, 128), 0) & 127) < iota((256, 128), 1))
    tile_row = place[0]

    def composite(tile, carry):
        feat = feats[pl.ds(pl.multiple_of(tile * 16, 16), 16), :]
        weights, _, _ = tile_weights(feat, tile & 31, tile_row, tri, alpha, pair)
        one, two = split2(weights)
        colours = stack_splits(feat[8:16], (0, 1, 2))
        big = dot(colours, one, NT)
        small = dot(colours, two, NT)
        result = (big[0:8] + big[8:16]) + (small[0:8] + small[8:16]) + big[16:24]
        start = pl.multiple_of(tile * 8, 8)
        left[pl.ds(start, 8), :] = result[:, 0:128]
        right[pl.ds(start, 8), :] = result[:, 128:256]
        return carry

    lax.fori_loop(0, 64, composite, 0)
    frame[...] = jnp.zeros((512, 128), F32)
    for w in range(2):
        for c in range(3):
            for b in range(4):
                for half, source in enumerate((left, right)):
                    block = source[pl.ds((w * 32 + b * 8) * 8 + c, 8, stride=8), :]
                    start = b * 128 + half * 64 + w * 3 + c
                    frame[pl.ds(start, 8, stride=8), :] = block_transpose(block)
    for b in range(4):
        image[:, b * 128 : b * 128 + 128] = frame[b * 128 : b * 128 + 128, :]


def blur_lanes(value):
    padded = jnp.concatenate([value, jnp.zeros((8, 128), F32)], axis=1)
    total = TAPS[5] * padded
    for k in range(1, 6):
        total = total + TAPS[5 + k] * (pltpu.roll(padded, k, 1) + pltpu.roll(padded, 640 - k, 1))
    return total[:, 0:512]


def blur_rows(rows):
    total = TAPS[5] * rows[5]
    for k in range(1, 6):
        total = total + TAPS[5 + k] * (rows[5 - k] + rows[5 + k])
    return total


def grad_kernel(
    own, place, shown, truth, feats, lists, recv, back,
    map_m, map_q, map_x, grads, left, right, frame, acc, alpha, pair, share, rows_out,
):
    tile_row = place[0]

    def similarity(y, carry):
        ones = [shown[y + k] for k in range(11)]
        twos = [truth[y + k] for k in range(11)]
        mean_one = blur_lanes(blur_rows(ones))
        mean_two = blur_lanes(blur_rows(twos))
        sq_one = blur_lanes(blur_rows([a * a for a in ones]))
        sq_two = blur_lanes(blur_rows([b * b for b in twos]))
        cross = blur_lanes(blur_rows([a * b for a, b in zip(ones, twos)]))
        num_one = 2.0 * mean_one * mean_two + SSIM_ONE
        num_two = 2.0 * (cross - mean_one * mean_two) + SSIM_TWO
        den_one = mean_one * mean_one + mean_two * mean_two + SSIM_ONE
        den_two = (sq_one - mean_one * mean_one) + (sq_two - mean_two * mean_two) + SSIM_TWO
        den_one_inv = 1.0 / den_one
        den_two_inv = 1.0 / den_two
        both_inv = den_one_inv * den_two_inv
        value = num_one * num_two * both_inv
        row = tile_row * 16 - 5 + y
        scale = jnp.where((row >= 0) & (row < 512), -SSIM_SHARE, 0.0)
        by_mean = 2.0 * mean_two * (num_two - num_one) * both_inv + 2.0 * mean_one * value * (
            den_two_inv - den_one_inv
        )
        map_m[y] = scale * by_mean
        map_q[y] = (-2.0 * scale) * value * den_two_inv
        map_x[y] = (2.0 * scale) * num_one * both_inv
        return carry

    lax.fori_loop(0, 26, similarity, 0)

    def image_grad(y, carry):
        by_mean = blur_lanes(blur_rows([map_m[y + k] for k in range(11)]))
        by_sq = blur_lanes(blur_rows([map_q[y + k] for k in range(11)]))
        by_cross = blur_lanes(blur_rows([map_x[y + k] for k in range(11)]))
        one = shown[y + 10]
        two = truth[y + 10]
        gap = one - two
        result = by_mean + one * by_sq + two * by_cross
        result = result + (1.0 - SSIM_SHARE) * gap / jnp.sqrt(gap * gap + SMOOTH_EPS)
        start = pl.multiple_of(y * 8, 8)
        for b in range(4):
            frame[pl.ds(b * 128 + start, 8), :] = result[:, b * 128 : b * 128 + 128]
        return carry

    lax.fori_loop(0, 16, image_grad, 0)
    left[...] = jnp.zeros((512, 128), F32)
    right[...] = jnp.zeros((512, 128), F32)
    for w in range(2):
        for c in range(3):
            for b in range(4):
                for half, target in enumerate((left, right)):
                    start = b * 128 + half * 64 + w * 3 + c
                    block = block_transpose(frame[pl.ds(start, 8, stride=8), :])
                    target[pl.ds((w * 32 + b * 8) * 8 + c, 8, stride=8), :] = block

    tri = triangle((iota((256, 128), 0) & 127) < iota((256, 128), 1))
    suf = triangle((iota((256, 128), 0) & 127) > iota((256, 128), 1))

    def composite(tile, carry):
        feat = feats[pl.ds(pl.multiple_of(tile * 16, 16), 16), :]
        weights, delta_x, delta_v = tile_weights(feat, tile & 31, tile_row, tri, alpha, pair)
        start = pl.multiple_of(tile * 8, 8)
        grad = jnp.concatenate([left[pl.ds(start, 8), :], right[pl.ds(start, 8), :]], axis=1)
        colours = stack_splits(feat[8:16], (0, 1, 0, 2, 0, 1))
        slopes = stack_splits(grad, (0, 0, 1, 0, 2, 1))
        gain = dot(slopes, colours, TN) * weights
        one, two = split2(gain)
        share[...] = gain
        pair[:, 0:128] = one
        pair[:, 128:256] = two
        behind = dot(pair[...], suf, NN)
        value = alpha[...]
        share[...] = share[...] - behind * (value / (1.0 - value))
        sum_0 = jnp.zeros((16, 128), F32)
        sum_1 = jnp.zeros((16, 128), F32)
        sum_2 = jnp.zeros((16, 128), F32)
        for j in range(16):
            delta_y = delta_v - float(j)
            part = share[j * 16 : j * 16 + 16, :]
            sum_0 = sum_0 + part
            part = part * delta_y
            sum_1 = sum_1 + part
            sum_2 = sum_2 + part * delta_y
        w_one, w_two = split2(weights)
        three = stack_splits(grad, (0, 1, 2))
        big = dot(three, w_one, NN)
        small = dot(three, w_two, NN)
        by_colour = (big[0:8] + big[8:16]) + (small[0:8] + small[8:16]) + big[16:24]

        def total(terms):
            return jnp.sum(terms, axis=0, keepdims=True)

        e_0 = total(sum_0)
        e_x = total(sum_0 * delta_x)
        e_y = total(sum_1)
        e_xx = total(sum_0 * delta_x * delta_x)
        e_xy = total(sum_1 * delta_x)
        e_yy = total(sum_2)
        conic_0, conic_1, conic_2 = feat[2:3], feat[3:4], feat[4:5]
        rows_out[pl.ds(pl.multiple_of(tile * 16, 16), 16), :] = jnp.concatenate(
            [
                -conic_0 * e_x - conic_1 * e_y,
                -conic_2 * e_y - conic_1 * e_x,
                -0.5 * e_xx,
                -e_xy,
                -0.5 * e_yy,
                e_0,
                by_colour[0:3],
                jnp.zeros((7, 128), F32),
            ],
            axis=0,
        )
        return carry

    lax.fori_loop(0, 64, composite, 0)
    acc[...] = jnp.zeros((576, 256), F32)
    for w in range(2):

        def scatter(pair_no, carry):
            tile = w * 32 + pair_no * 2
            idx = jnp.concatenate([lists[pl.ds(tile, 1), :], lists[pl.ds(tile + 1, 1), :]], axis=1)
            start = pl.multiple_of(tile * 16, 32)
            both = rows_out[pl.ds(start, 32), :]
            rows = jnp.concatenate([both[0:9], both[16:25]], axis=1)
            onehot = high_onehot(idx)
            parts = split3(spread_rows(rows, low_mask(idx)))
            total = dot(parts[0], onehot, NT) + dot(parts[1], onehot, NT) + dot(parts[2], onehot, NT)
            acc[w * 288 : w * 288 + 288, :] += total
            return carry

        lax.fori_loop(0, 16, scatter, 0)

    is_first = first_half()
    for high in range(2):
        lane_part = slice(high * 128, high * 128 + 128)

        def project_back(low, carry):
            row0 = pl.multiple_of(low * 8, 8)
            q = high * 4 + low
            values = unpack_slots(recv, q)
            gauss = values[0:3] + values[4:10]

            def grad_of(w, f):
                return acc[pl.ds((w * 9 + f) * 32 + row0, 8), lane_part]

            totals = None
            for w in range(2):
                cam = [own[w, n] for n in range(12)]
                _, pull = jax.vjp(lambda *g: image_values(list(g), cam), *gauss)
                parts = pull([grad_of(w, f) for f in range(5)])
                totals = parts if totals is None else [a + b for a, b in zip(totals, parts)]
            totals = list(totals)
            result = totals[0:3] + [grad_of(0, 5) + grad_of(1, 5)] + totals[3:9]
            result += [grad_of(w, 6 + c) for w in range(2) for c in range(3)]
            for f in range(8):
                even = jnp.where(is_first, result[f], half_roll(result[f + 8]))
                odd = jnp.where(is_first, half_roll(result[f]), result[f + 8])
                back[pl.ds(q * 128 + f, 8, stride=16), :] = even
                back[pl.ds(q * 128 + 8 + f, 8, stride=16), :] = odd
            return carry

        lax.fori_loop(0, 4, project_back, 0)


def param_kernel(cam, params, recv, chosen, group_in, out, blocks, outs, acc):
    load_params(params, blocks)
    acc[...] = jnp.zeros((512, 256), F32)
    is_first = first_half()

    def scatter(p, carry):
        idx = chosen[pl.ds(p, 1), :]
        onehot = high_onehot(idx)
        mask = low_mask(idx)
        lows, highs = [], []
        for b in range(2):
            start = pl.multiple_of(p * 32 + b * 16, 16)
            even = recv[pl.ds(start, 8), :]
            odd = recv[pl.ds(start + 8, 8), :]
            lows.append(jnp.where(is_first, even, half_roll(odd)))
            highs.append(jnp.where(is_first, half_roll(even), odd))
        for part, pieces in enumerate((lows, highs)):
            rows = jnp.concatenate(pieces, axis=1)
            splits = split3(spread_rows(rows, mask))
            total = dot(splits[0], onehot, NT) + dot(splits[1], onehot, NT) + dot(splits[2], onehot, NT)
            acc[part * 256 : part * 256 + 256, :] += total
        return carry

    lax.fori_loop(0, 32, scatter, 0)

    for high in range(2):
        lane_part = slice(high * 128, high * 128 + 128)

        def compute(low, carry):
            base = (high * 4 + low) * 512
            row0 = pl.multiple_of(low * 8, 8)

            def load(p):
                return blocks[pl.ds(base + p, 8, stride=64), :]

            def save(p, value):
                outs[pl.ds(base + p, 8, stride=64), :] = value

            def grad_of(f):
                return acc[pl.ds(f * 32 + row0, 8), lane_part]

            anchors = group_anchors(cam, group_in[pl.ds(row0, 8), lane_part])
            mean = [load(0), load(1), load(2)]
            totals = [grad_of(0), grad_of(1), grad_of(2)]
            _, pull = jax.vjp(lambda *g: shape_values(list(g)), *[load(3 + n) for n in range(7)])
            for n, value in enumerate(pull([grad_of(4 + n) for n in range(6)])):
                save(3 + n, value)
            save(10, grad_of(3) / (1.0 + jnp.exp(load(10))))
            colour = [[grad_of(10 + 3 * w + c) for c in range(3)] for w in range(2)]
            bases, pulls = [], []
            for w in range(2):
                anchor = anchors[w]
                basis, pull = jax.vjp(lambda *m: colour_basis(list(m), anchor)[1:], *mean)
                bases.append(basis)
                pulls.append(pull)
            slopes = [[None] * 15, [None] * 15]
            for c in range(3):
                save(11 + 16 * c, HARMONIC_ZERO * (colour[0][c] + colour[1][c]))
                for k in range(15):
                    coef = load(12 + 16 * c + k)
                    save(
                        12 + 16 * c + k,
                        bases[0][k] * colour[0][c] + bases[1][k] * colour[1][c],
                    )
                    for w in range(2):
                        term = coef * colour[w][c]
                        slopes[w][k] = term if c == 0 else slopes[w][k] + term
            for w in range(2):
                totals = [a + b for a, b in zip(totals, pulls[w](slopes[w]))]
            for n in range(3):
                save(n, totals[n])
            return carry

        lax.fori_loop(0, 4, compute, 0)
    for row in range(64):
        out[:, row * 128 : (row + 1) * 128] = outs[pl.ds(row * 64, 59), :]


def struct(shape, dtype=F32):
    return jax.ShapeDtypeStruct(shape, dtype)


VM = pl.BlockSpec(memory_space=pltpu.VMEM)
SM = pl.BlockSpec(memory_space=pltpu.SMEM)
PARAMS_C = pltpu.CompilerParams(vmem_limit_bytes=VMEM_BYTES)


def run_send(cam, params, slist, counts):
    return pl.pallas_call(
        send_kernel,
        out_shape=(struct((1024, 128)), struct((32, 256)), struct((32, 256), I32)),
        in_specs=[SM, VM, VM, VM],
        out_specs=(VM, VM, VM),
        scratch_shapes=[
            pltpu.VMEM((4096, 128), F32),
            pltpu.VMEM((512, 256), F32),
            pltpu.VMEM((512, 256), BF16),
            pltpu.VMEM((512, 256), BF16),
            pltpu.VMEM((512, 256), BF16),
            pltpu.VMEM((8192, 256), BF16),
            pltpu.VMEM((64, 256), F32),
            pltpu.VMEM((32, 256), I32),
            pltpu.VMEM((32, 256), F32),
        ],
        compiler_params=PARAMS_C,
        name="send_values",
    )(cam, params, slist, counts)


def run_render(own, place, lens, recv, lists):
    return pl.pallas_call(
        render_kernel,
        out_shape=(struct((128, 512)), struct((1024, 128))),
        in_specs=[SM, SM, SM, VM, VM],
        out_specs=(VM, VM),
        scratch_shapes=[
            pltpu.VMEM((576, 256), F32),
            pltpu.VMEM((576, 256), BF16),
            pltpu.VMEM((576, 256), BF16),
            pltpu.VMEM((576, 256), BF16),
            pltpu.VMEM((256, 128), F32),
            pltpu.VMEM((256, 256), BF16),
            pltpu.VMEM((512, 128), F32),
            pltpu.VMEM((512, 128), F32),
            pltpu.VMEM((512, 128), F32),
        ],
        compiler_params=PARAMS_C,
        name="render_band",
    )(own, place, lens, recv, lists)


def run_grad(own, place, shown, truth, feats, lists, recv):
    return pl.pallas_call(
        grad_kernel,
        out_shape=struct((1024, 128)),
        in_specs=[SM, SM, VM, VM, VM, VM, VM],
        out_specs=VM,
        scratch_shapes=[
            pltpu.VMEM((26, 8, 512), F32),
            pltpu.VMEM((26, 8, 512), F32),
            pltpu.VMEM((26, 8, 512), F32),
            pltpu.VMEM((8, 128), F32),
            pltpu.VMEM((512, 128), F32),
            pltpu.VMEM((512, 128), F32),
            pltpu.VMEM((512, 128), F32),
            pltpu.VMEM((576, 256), F32),
            pltpu.VMEM((256, 128), F32),
            pltpu.VMEM((256, 256), BF16),
            pltpu.VMEM((256, 128), F32),
            pltpu.VMEM((1024, 128), F32),
        ],
        compiler_params=PARAMS_C,
        name="loss_gradient",
    )(own, place, shown, truth, feats, lists, recv)


def run_params(cam, params, recv, chosen, group):
    return pl.pallas_call(
        param_kernel,
        out_shape=struct((59, 8192)),
        in_specs=[SM, VM, VM, VM, VM],
        out_specs=VM,
        scratch_shapes=[
            pltpu.VMEM((4096, 128), F32),
            pltpu.VMEM((4096, 128), F32),
            pltpu.VMEM((512, 256), F32),
        ],
        compiler_params=PARAMS_C,
        name="param_gradient",
    )(cam, params, recv, chosen, group)


def with_halo(rows):
    count = lax.axis_size("tile")
    down = [(i, i + 1) for i in range(count - 1)]
    up = [(i + 1, i) for i in range(count - 1)]
    above = lax.ppermute(rows[6:16], "tile", down)
    below = lax.ppermute(rows[0:10], "tile", up)
    return jnp.concatenate([above, rows, below], axis=0)


def exchange(blocks):
    moved = lax.all_to_all(
        blocks.reshape(128, 8, 128), ("view", "tile"), split_axis=0, concat_axis=0, tiled=True
    )
    return moved.reshape(1024, 128)


def shards(params, send_list, send_counts, camera, ground_truth, tile_lists, list_lengths):
    tile_row = lax.axis_index("tile")
    view_group = lax.axis_index("view")
    cams = camera_table(camera)
    own = lax.dynamic_slice_in_dim(cams, 2 * view_group, 2, 0)
    place = tile_row.astype(I32).reshape(1)
    truth = jnp.transpose(ground_truth.reshape(6, 16, 512), (1, 0, 2))
    truth = with_halo(jnp.pad(truth, ((0, 0), (0, 2), (0, 0))))
    sent, group, chosen = run_send(cams, params, send_list, send_counts)
    recv = exchange(sent)
    lists = tile_lists.reshape(64, 128)
    image, feats = run_render(own, place, list_lengths.reshape(64), recv, lists)
    shown = with_halo(image.reshape(16, 8, 512))
    back = run_grad(own, place, shown, truth, feats, lists, recv)
    returned = exchange(back)
    return run_params(cams, params, returned, chosen, group)


def solution(mesh):
    in_specs = (
        P(None, ("view", "tile")),
        P(("view", "tile"), None),
        P(("view", "tile"), None),
        P(),
        P("view", None, "tile", None),
        P("view", "tile", None, None),
        P("view", "tile", None),
    )
    out_specs = P(None, ("view", "tile"))
    return jax.shard_map(shards, mesh=mesh, in_specs=in_specs, out_specs=out_specs, check_vma=False)
```

```python
import jax
import jax.numpy as jnp
import numpy as np
from jax import lax
from jax.experimental import pallas as pl
from jax.experimental.pallas import tpu as pltpu
from jax.sharding import PartitionSpec as P

F32 = jnp.float32
BF16 = jnp.bfloat16
I32 = jnp.int32

TILE = 16
GROUP = 4
FOCAL = 1000.0
LOW_PASS = 0.3
SSIM_SHARE = 0.2
SMOOTH_EPS = 1e-06
SSIM_ONE = 0.0001
SSIM_TWO = 0.0009
LOG2E = 1.4426950408889634
HARMONIC_ZERO = 0.28209479177387814
HARMONIC_ONE = 0.4886025119029199
HARMONIC_TWO = (
    1.0925484305920792,
    -1.0925484305920792,
    0.31539156525252005,
    -1.0925484305920792,
    0.5462742152960396,
)
HARMONIC_THREE = (
    -0.5900435899266435,
    2.890611442640554,
    -0.4570457994644658,
    0.3731763325901154,
    -0.4570457994644658,
    1.445305721320277,
    -0.5900435899266435,
)
VMEM_BYTES = 56 * 1024 * 1024
CHOOSE = 8
GATHER = 4
LOOKUP = 4
SCAT = 4
BACK = 4
MESH = pl.DeviceIdType.MESH
NT = (((1,), (1,)), ((), ()))
NN = (((1,), (0,)), ((), ()))
TN = (((0,), (0,)), ((), ()))


def window_taps():
    offsets_np = np.arange(11) - 5.0
    weights = np.exp(-offsets_np * offsets_np / 4.5)
    weights = weights / weights.sum()
    return [float(weight) for weight in weights]


TAPS = window_taps()


def matrix_product(left_side, right_side):
    return [
        [
            left_side[row_idx][0] * right_side[0][col_idx]
            + left_side[row_idx][1] * right_side[1][col_idx]
            + left_side[row_idx][2] * right_side[2][col_idx]
            for col_idx in range(3)
        ]
        for row_idx in range(3)
    ]


def rotation(angles):
    cos_a, sin_a = (jnp.cos(angles[0]), jnp.sin(angles[0]))
    cos_b, sin_b = (jnp.cos(angles[1]), jnp.sin(angles[1]))
    cos_c, sin_c = (jnp.cos(angles[2]), jnp.sin(angles[2]))
    zero, one = jnp.zeros_like(cos_a), jnp.ones_like(cos_a)
    about_x = [[one, zero, zero], [zero, cos_a, -sin_a], [zero, sin_a, cos_a]]
    about_y = [[cos_b, zero, sin_b], [zero, one, zero], [-sin_b, zero, cos_b]]
    about_z = [[cos_c, -sin_c, zero], [sin_c, cos_c, zero], [zero, zero, one]]
    return matrix_product(about_z, matrix_product(about_y, about_x))


def camera_values(numbers):
    rot = rotation(numbers[0:3])
    move = list(numbers[3:6])
    anchor = [
        -(rot[0][c] * move[0] + rot[1][c] * move[1] + rot[2][c] * move[2]) for c in range(3)
    ]
    return rot[0] + rot[1] + rot[2] + move, anchor


def own_cameras(cam, group):
    return [
        camera_values([jnp.full((8, 128), cam[2 * group + w, n], F32) for n in range(6)])[0]
        for w in range(2)
    ]


def all_anchors(cam):
    numbers = [jnp.broadcast_to(cam[:, n : n + 1], (8, 128)) for n in range(6)]
    anchor = camera_values(numbers)[1]
    return [[jnp.broadcast_to(a[n : n + 1, :], (8, 128)) for a in anchor] for n in range(8)]


def own_number():
    return lax.axis_index("view") * 32 + lax.axis_index("tile")


def device_of(number):
    return (lax.div(number, 32), lax.rem(number, 32))


def greet_all(me):
    barrier = pltpu.get_barrier_semaphore()

    def greet(o, carry):
        pl.semaphore_signal(
            barrier, inc=1, device_id=device_of(lax.rem(me + o, 128)), device_id_type=MESH
        )
        return carry

    lax.fori_loop(1, 128, greet, 0)
    return barrier


def block_copy(pack, recv, me, number, sems):
    return pltpu.make_async_remote_copy(
        src_ref=pack.at[pl.ds(pl.multiple_of(number * 8, 8), 8)],
        dst_ref=recv.at[pl.ds(pl.multiple_of(me * 8, 8), 8)],
        send_sem=sems.at[0],
        recv_sem=sems.at[1],
        device_id=device_of(number),
        device_id_type=MESH,
    )


def push_blocks(pack, recv, me, first, count, sems):
    def push(n, carry):
        number = first + n

        @pl.when(number != me)
        def _():
            block_copy(pack, recv, me, number, sems).start()

        return carry

    lax.fori_loop(0, count, push, 0)


def finish_blocks(pack, recv, me, sems):
    start = pl.multiple_of(me * 8, 8)
    recv[pl.ds(start, 8), :] = pack[pl.ds(start, 8), :]
    whole = pltpu.make_async_remote_copy(
        src_ref=pack.at[pl.ds(0, 1016)],
        dst_ref=recv.at[pl.ds(0, 1016)],
        send_sem=sems.at[0],
        recv_sem=sems.at[1],
        device_id=device_of(lax.rem(me + 1, 128)),
        device_id_type=MESH,
    )
    whole.wait()


def harmonics(dir_x, dir_y, dir_z):
    sq_x, sq_y, sq_z = (dir_x * dir_x, dir_y * dir_y, dir_z * dir_z)
    prod_xy, prod_yz, prod_xz = (dir_x * dir_y, dir_y * dir_z, dir_x * dir_z)
    return [
        None,
        -HARMONIC_ONE * dir_y,
        HARMONIC_ONE * dir_z,
        -HARMONIC_ONE * dir_x,
        HARMONIC_TWO[0] * prod_xy,
        HARMONIC_TWO[1] * prod_yz,
        HARMONIC_TWO[2] * (2.0 * sq_z - sq_x - sq_y),
        HARMONIC_TWO[3] * prod_xz,
        HARMONIC_TWO[4] * (sq_x - sq_y),
        HARMONIC_THREE[0] * dir_y * (3.0 * sq_x - sq_y),
        HARMONIC_THREE[1] * prod_xy * dir_z,
        HARMONIC_THREE[2] * dir_y * (4.0 * sq_z - sq_x - sq_y),
        HARMONIC_THREE[3] * dir_z * (2.0 * sq_z - 3.0 * sq_x - 3.0 * sq_y),
        HARMONIC_THREE[4] * dir_x * (4.0 * sq_z - sq_x - sq_y),
        HARMONIC_THREE[5] * dir_z * (sq_x - sq_y),
        HARMONIC_THREE[6] * dir_x * (sq_x - 3.0 * sq_y),
    ]


def shape_values(gauss):
    scales = [jnp.exp(gauss[axis]) for axis in range(3)]
    norm_inv = 1.0 / jnp.sqrt(
        gauss[3] * gauss[3] + gauss[4] * gauss[4] + gauss[5] * gauss[5] + gauss[6] * gauss[6]
    )
    quat_w, quat_x, quat_y, quat_z = [gauss[3 + n] * norm_inv for n in range(4)]
    quat_rot = [
        [
            1.0 - 2.0 * (quat_y * quat_y + quat_z * quat_z),
            2.0 * (quat_x * quat_y - quat_w * quat_z),
            2.0 * (quat_x * quat_z + quat_w * quat_y),
        ],
        [
            2.0 * (quat_x * quat_y + quat_w * quat_z),
            1.0 - 2.0 * (quat_x * quat_x + quat_z * quat_z),
            2.0 * (quat_y * quat_z - quat_w * quat_x),
        ],
        [
            2.0 * (quat_x * quat_z - quat_w * quat_y),
            2.0 * (quat_y * quat_z + quat_w * quat_x),
            1.0 - 2.0 * (quat_x * quat_x + quat_y * quat_y),
        ],
    ]
    spread = [[quat_rot[r][c] * scales[c] for c in range(3)] for r in range(3)]

    def dot_rows(one, two):
        return (
            spread[one][0] * spread[two][0]
            + spread[one][1] * spread[two][1]
            + spread[one][2] * spread[two][2]
        )

    return [
        dot_rows(0, 0),
        dot_rows(0, 1),
        dot_rows(0, 2),
        dot_rows(1, 1),
        dot_rows(1, 2),
        dot_rows(2, 2),
    ]


def colour_basis(mean, anchor):
    ray_x, ray_y, ray_z = (mean[0] - anchor[0], mean[1] - anchor[1], mean[2] - anchor[2])
    len_inv = 1.0 / jnp.sqrt(ray_x * ray_x + ray_y * ray_y + ray_z * ray_z)
    return harmonics(ray_x * len_inv, ray_y * len_inv, ray_z * len_inv)


def image_values(gauss, cam):
    point = [
        cam[3 * r] * gauss[0] + cam[3 * r + 1] * gauss[1] + cam[3 * r + 2] * gauss[2] + cam[9 + r]
        for r in range(3)
    ]
    inv_depth = 1.0 / point[2]
    jac = FOCAL * inv_depth
    jac_xz = -FOCAL * point[0] * inv_depth * inv_depth
    jac_yz = -FOCAL * point[1] * inv_depth * inv_depth
    row_x = [jac * cam[c] + jac_xz * cam[6 + c] for c in range(3)]
    row_y = [jac * cam[3 + c] + jac_yz * cam[6 + c] for c in range(3)]
    s_xx, s_xy, s_xz, s_yy, s_yz, s_zz = gauss[3:9]
    by_x = [
        s_xx * row_x[0] + s_xy * row_x[1] + s_xz * row_x[2],
        s_xy * row_x[0] + s_yy * row_x[1] + s_yz * row_x[2],
        s_xz * row_x[0] + s_yz * row_x[1] + s_zz * row_x[2],
    ]
    by_y = [
        s_xx * row_y[0] + s_xy * row_y[1] + s_xz * row_y[2],
        s_xy * row_y[0] + s_yy * row_y[1] + s_yz * row_y[2],
        s_xz * row_y[0] + s_yz * row_y[1] + s_zz * row_y[2],
    ]
    cov_xx = row_x[0] * by_x[0] + row_x[1] * by_x[1] + row_x[2] * by_x[2] + LOW_PASS
    cov_xy = row_y[0] * by_x[0] + row_y[1] * by_x[1] + row_y[2] * by_x[2]
    cov_yy = row_y[0] * by_y[0] + row_y[1] * by_y[1] + row_y[2] * by_y[2] + LOW_PASS
    det_inv = 1.0 / (cov_xx * cov_yy - cov_xy * cov_xy)
    return [
        FOCAL * point[0] * inv_depth + 256.0,
        FOCAL * point[1] * inv_depth + 256.0,
        cov_yy * det_inv,
        -cov_xy * det_inv,
        cov_xx * det_inv,
    ]


def split3(value):
    one = value.astype(BF16)
    rest = value - one.astype(F32)
    two = rest.astype(BF16)
    three = (rest - two.astype(F32)).astype(BF16)
    return one, two, three


def split2(value):
    one = value.astype(BF16)
    return one, (value - one.astype(F32)).astype(BF16)


def dot(left, right, dims):
    return lax.dot_general(left, right, dims, preferred_element_type=F32)


def iota(shape, dim):
    return lax.broadcasted_iota(I32, shape, dim)


def high_onehot(idx):
    high = ((idx >> 12) << 7) | (idx & 127)
    return jnp.where(iota((256, idx.shape[1]), 0) == high, 1.0, 0.0).astype(BF16)


def low_mask(idx):
    return iota((32, idx.shape[1]), 0) == ((idx >> 7) & 31)


def pick(tables, onehot, mask, rows):
    total = dot(tables[0], onehot, NN)
    for table in tables[1:]:
        total = total + dot(table, onehot, NN)
    picked = jnp.where(mask[None], total.reshape(rows, 32, mask.shape[1]), 0.0)
    return jnp.sum(picked, axis=1)


def spread_rows(rows, mask):
    count = rows.shape[0]
    return jnp.where(mask[None], rows[:, None, :], 0.0).reshape(count * 32, rows.shape[1])


def add_up(left, onehot):
    total = None
    for part in split2(left):
        term = dot(part, onehot, NT)
        total = term if total is None else total + term
    return total


def half_roll(value):
    return pltpu.roll(value, 64, 1)


def first_half():
    return iota((8, 128), 1) < 64


def load_params(params, blocks):
    for row in range(64):
        blocks[pl.ds(row * 64, 59), :] = params[:, row * 128 : (row + 1) * 128]


def group_anchors(table, group):
    anchors = []
    for slot in range(2):
        triple = []
        for c in range(3):
            value = table[slot][c]
            for number in range(1, 4):
                value = jnp.where(group > number + 0.5, table[2 * number + slot][c], value)
            triple.append(value)
        anchors.append(triple)
    return anchors


def send_kernel(
    cam, params, slist, counts, recv, group_out, chosen,
    send, blocks, tab, t0, t1, t2, hot, stab, pos, val, sems,
):
    me = own_number()
    barrier = greet_all(me)
    table = all_anchors(cam)
    cnt = counts[...].astype(F32)
    lanes = iota((32, 128), 1)
    first = iota((32, 128), 0) * 4
    slot_lane = iota((32, 256), 1)
    off = jnp.zeros((32, 256), F32)
    own = jnp.zeros((32, 256), F32)
    for j in range(4):
        off_j = jnp.sum(jnp.where(lanes < first + j, cnt, 0.0), axis=1, keepdims=True)
        own_j = jnp.sum(jnp.where(lanes == first + j, cnt, 0.0), axis=1, keepdims=True)
        here = (slot_lane >> 6) == j
        off = jnp.where(here, off_j, off)
        own = jnp.where(here, own_j, own)
    place = (slot_lane & 63).astype(F32)
    pos[...] = jnp.minimum(off + place, 8191.0).astype(I32)
    group = (iota((32, 256), 0) >> 3).astype(F32) + 1.0
    val[...] = jnp.where(place < own, group, 0.0)
    for row in range(64):
        piece = slist[:, row * 128 : (row + 1) * 128]
        half = slice((row // 32) * 128, (row // 32) * 128 + 128)
        stab[row % 32 : row % 32 + 1, half] = (piece >> 6).astype(F32)
        stab[32 + row % 32 : 33 + row % 32, half] = (piece & 63).astype(F32)
    load_params(params, blocks)
    group_out[...] = jnp.zeros((32, 256), F32)
    stab_b = stab[...].astype(BF16)

    def choose(step, carry):
        rows = [step * CHOOSE + g for g in range(CHOOSE)]
        places = [pos[pl.ds(p, 1), :] for p in rows]
        found = [dot(stab_b, high_onehot(idx), NN) for idx in places]
        total = None
        for g, p in enumerate(rows):
            both = found[g][0:32] * 64.0 + found[g][32:64]
            ids = jnp.sum(jnp.where(low_mask(places[g]), both, 0.0), axis=0, keepdims=True).astype(I32)
            chosen[pl.ds(p, 1), :] = ids
            onehot = high_onehot(ids)
            hot[pl.ds(pl.multiple_of(p * 256, 256), 256), :] = onehot
            left = jnp.where(low_mask(ids), val[pl.ds(p, 1), :], 0.0).astype(BF16)
            part = dot(left, onehot, NT)
            total = part if g == 0 else total + part
        group_out[...] += total
        return carry

    lax.fori_loop(0, 32 // CHOOSE, choose, 0)

    for high in range(2):
        lane_part = slice(high * 128, high * 128 + 128)

        def compute(low, carry):
            base = (high * 4 + low) * 512
            row0 = pl.multiple_of(low * 8, 8)

            def load(p):
                return blocks[pl.ds(base + p, 8, stride=64), :]

            anchors = group_anchors(table, group_out[pl.ds(row0, 8), lane_part])
            mean = [load(0), load(1), load(2)]
            values = mean + [0.99 / (1.0 + jnp.exp(-load(10)))]
            values += shape_values([load(3 + n) for n in range(7)])
            bases = [colour_basis(mean, anchor) for anchor in anchors]
            sums = [[None] * 3, [None] * 3]
            for c in range(3):
                flat = 0.5 + HARMONIC_ZERO * load(11 + 16 * c)
                sums[0][c] = flat
                sums[1][c] = flat
                for k in range(1, 16):
                    coef = load(11 + 16 * c + k)
                    sums[0][c] = sums[0][c] + bases[0][k] * coef
                    sums[1][c] = sums[1][c] + bases[1][k] * coef
            values += sums[0] + sums[1]
            for f in range(16):
                tab[pl.ds(f * 32 + row0, 8), lane_part] = values[f]
            return carry

        lax.fori_loop(0, 4, compute, 0)

    t0[...], t1[...], t2[...] = split3(tab[...])
    is_first = first_half()
    shift = lax.div(me, 4) + 1
    pl.semaphore_wait(barrier, 127)

    def gather(step, carry):
        for g in range(GATHER):
            p = lax.rem(step * GATHER + g + shift, 32)
            onehot = hot[pl.ds(pl.multiple_of(p * 256, 256), 256), :]
            mask = low_mask(chosen[pl.ds(p, 1), :])
            rows = []
            for part in range(2):
                cut = pl.ds(part * 256, 256)
                rows.append(pick([t0[cut, :], t1[cut, :], t2[cut, :]], onehot, mask, 8))
            for b in range(2):
                one = rows[0][:, b * 128 : b * 128 + 128]
                two = rows[1][:, b * 128 : b * 128 + 128]
                start = pl.multiple_of(p * 32 + b * 16, 16)
                send[pl.ds(start, 8), :] = jnp.where(is_first, one, half_roll(two))
                send[pl.ds(start + 8, 8), :] = jnp.where(is_first, half_roll(one), two)
        for g in range(GATHER):
            p = lax.rem(step * GATHER + g + shift, 32)
            push_blocks(send, recv, me, p * 4, 4, sems)
        return carry

    lax.fori_loop(0, 32 // GATHER, gather, 0)
    finish_blocks(send, recv, me, sems)


def unpack_slots(recv, q):
    is_first = first_half()
    low, high = [], []
    for f in range(8):
        even = recv[pl.ds(q * 128 + f, 8, stride=16), :]
        odd = recv[pl.ds(q * 128 + 8 + f, 8, stride=16), :]
        low.append(jnp.where(is_first, even, half_roll(odd)))
        high.append(jnp.where(is_first, half_roll(even), odd))
    return low + high


def block_transpose(value):
    turn = (iota((8, 128), 0) - (iota((8, 128), 1) >> 4)) & 7
    result = value
    for d in range(1, 8):
        moved = pltpu.roll(pltpu.roll(value, d, 0), 128 - 16 * d, 1)
        result = jnp.where(turn == d, moved, result)
    return result


def triangle(keep):
    return jnp.where(keep, 1.0, 0.0).astype(BF16)


def pixel_rows(feat, column, tile_row):
    def row(f):
        return jnp.broadcast_to(feat[f : f + 1, :], (16, 128))

    shift = iota((16, 128), 0).astype(F32) + (column * 16).astype(F32)
    delta_x = row(0) - shift
    square = (-0.5 * LOG2E) * row(2) * delta_x * delta_x
    cross = -LOG2E * row(3) * delta_x
    quad = (-0.5 * LOG2E) * row(4)
    delta_v = row(1) - (tile_row * 16).astype(F32)
    return delta_x, delta_v, square, cross, quad, row(5)


def tile_weights(feats, columns, tile_row, tri, alpha, pair):
    shifts = []
    for g, feat in enumerate(feats):
        delta_x, delta_v, square, cross, quad, opacity = pixel_rows(feat, columns[g], tile_row)
        shifts.append((delta_x, delta_v))
        for j in range(16):
            delta_y = delta_v - float(j)
            value = opacity * jnp.exp2(square + delta_y * (cross + quad * delta_y))
            rows = slice(g * 256 + j * 16, g * 256 + j * 16 + 16)
            alpha[rows, :] = value
            one, two = split2(jnp.log(1.0 - value))
            pair[rows, 0:128] = one
            pair[rows, 128:256] = two
    weights = []
    for g in range(len(feats)):
        rows = slice(g * 256, g * 256 + 256)
        weights.append(jnp.exp(dot(pair[rows, :], tri, NN)) * alpha[rows, :])
    return weights, shifts


def stack_splits(value, order):
    one, two, three = split3(value)
    parts = [one.astype(F32), two.astype(F32), three.astype(F32)]
    return jnp.concatenate([parts[n] for n in order], axis=0).astype(BF16)


def greet_bands(tile_row):
    barrier = pltpu.get_barrier_semaphore()
    for step in (1, 31):
        other = lax.rem(tile_row + step, 32)
        pl.semaphore_signal(barrier, inc=1, device_id={"tile": other}, device_id_type=MESH)
    pl.semaphore_wait(barrier, 2)


def halo_copies(rows, tile_row, sems):
    def copy(source, target, step, n):
        return pltpu.make_async_remote_copy(
            src_ref=rows.at[pl.ds(source, 80)],
            dst_ref=rows.at[pl.ds(target, 80)],
            send_sem=sems.at[2 * n],
            recv_sem=sems.at[2 * n + 1],
            device_id={"tile": lax.rem(tile_row + step, 32)},
            device_id_type=MESH,
        )

    return copy(128, 0, 1, 0), copy(80, 208, 31, 1)


def send_halo(rows, tile_row, sems):
    down, up = halo_copies(rows, tile_row, sems)

    @pl.when(tile_row < 31)
    def _():
        down.start()

    @pl.when(tile_row > 0)
    def _():
        up.start()


def take_halo(rows, tile_row, sems):
    down, up = halo_copies(rows, tile_row, sems)

    @pl.when(tile_row < 31)
    def _():
        down.wait_send()
        up.wait_recv()

    @pl.when(tile_row > 0)
    def _():
        up.wait_send()
        down.wait_recv()

    @pl.when(tile_row == 0)
    def _():
        rows[0:80, :] = jnp.zeros((80, 512), F32)

    @pl.when(tile_row == 31)
    def _():
        rows[208:288, :] = jnp.zeros((80, 512), F32)


def render_kernel(
    cam, lens, recv, lists, true, shown, truth, feats,
    tab, t0, t1, t2, alpha, pair, left, right, frame, sems_one, sems_two,
):
    tile_row = lax.axis_index("tile")
    own = own_cameras(cam, lax.axis_index("view"))
    frame[...] = jnp.zeros((512, 128), F32)
    for n in range(6):
        for b in range(4):
            for half in range(2):
                rows = true[n * 16 + half * 8 : n * 16 + half * 8 + 8, b * 128 : b * 128 + 128]
                frame[pl.ds(b * 128 + half * 64 + n, 8, stride=8), :] = rows
    for b in range(4):
        truth[80:208, b * 128 : b * 128 + 128] = frame[b * 128 : b * 128 + 128, :]
    greet_bands(tile_row)
    send_halo(truth, tile_row, sems_two)
    for high in range(2):
        lane_part = slice(high * 128, high * 128 + 128)

        def compute(low, carry):
            row0 = pl.multiple_of(low * 8, 8)
            values = unpack_slots(recv, high * 4 + low)
            gauss = values[0:3] + values[4:10]
            for w in range(2):
                seen = image_values(gauss, own[w])
                seen = seen + [values[3]] + values[10 + 3 * w : 13 + 3 * w]
                for f in range(9):
                    tab[pl.ds((w * 9 + f) * 32 + row0, 8), lane_part] = seen[f]
            return carry

        lax.fori_loop(0, 4, compute, 0)
    t0[...], t1[...], t2[...] = split3(tab[...])
    lane = iota((1, 256), 1)

    for w in range(2):
        cut = slice(w * 288, w * 288 + 288)

        def look_up(step, carry):
            for g in range(LOOKUP):
                tile = w * 32 + (step * LOOKUP + g) * 2
                idx = jnp.concatenate([lists[pl.ds(tile, 1), :], lists[pl.ds(tile + 1, 1), :]], axis=1)
                rows = pick([t0[cut, :], t1[cut, :], t2[cut, :]], high_onehot(idx), low_mask(idx), 9)
                length = jnp.where(lane < 128, lens[w, 0, tile - w * 32], lens[w, 0, tile - w * 32 + 1])
                rows = jnp.where((lane & 127) < length, rows, 0.0)
                start = pl.multiple_of(tile * 16, 32)
                for b in range(2):
                    part = rows[:, b * 128 : b * 128 + 128]
                    feats[pl.ds(start + b * 16, 6), :] = part[0:6]
                    feats[pl.ds(start + b * 16 + 6, 2), :] = jnp.zeros((2, 128), F32)
                    feats[pl.ds(start + b * 16 + 8, 3), :] = part[6:9]
                    feats[pl.ds(start + b * 16 + 11, 5), :] = jnp.zeros((5, 128), F32)
            return carry

        lax.fori_loop(0, 16 // LOOKUP, look_up, 0)

    tri = triangle((iota((256, 128), 0) & 127) < iota((256, 128), 1))

    def composite(step, carry):
        tiles = [step * GROUP + g for g in range(GROUP)]
        given = [feats[pl.ds(pl.multiple_of(tile * 16, 16), 16), :] for tile in tiles]
        weights, _ = tile_weights(given, [tile & 31 for tile in tiles], tile_row, tri, alpha, pair)
        for g, tile in enumerate(tiles):
            one, two = split2(weights[g])
            colours = stack_splits(given[g][8:16], (0, 1, 2))
            big = dot(colours, one, NT)
            small = dot(colours, two, NT)
            result = (big[0:8] + big[8:16]) + (small[0:8] + small[8:16]) + big[16:24]
            start = pl.multiple_of(tile * 8, 8)
            left[pl.ds(start, 8), :] = result[:, 0:128]
            right[pl.ds(start, 8), :] = result[:, 128:256]
        return carry

    lax.fori_loop(0, 64 // GROUP, composite, 0)
    for w in range(2):
        for c in range(3):
            for b in range(4):
                for half, source in enumerate((left, right)):
                    block = source[pl.ds((w * 32 + b * 8) * 8 + c, 8, stride=8), :]
                    start = b * 128 + half * 64 + w * 3 + c
                    frame[pl.ds(start, 8, stride=8), :] = block_transpose(block)
    for b in range(4):
        shown[80:208, b * 128 : b * 128 + 128] = frame[b * 128 : b * 128 + 128, :]
    send_halo(shown, tile_row, sems_one)
    take_halo(shown, tile_row, sems_one)
    take_halo(truth, tile_row, sems_two)


def blur_lanes(value):
    padded = jnp.concatenate([value, jnp.zeros((8, 128), F32)], axis=1)
    total = TAPS[5] * padded
    for k in range(1, 6):
        total = total + TAPS[5 + k] * (pltpu.roll(padded, k, 1) + pltpu.roll(padded, 640 - k, 1))
    return total[:, 0:512]


def blur_rows(rows):
    total = TAPS[5] * rows[5]
    for k in range(1, 6):
        total = total + TAPS[5 + k] * (rows[5 - k] + rows[5 + k])
    return total


def grad_kernel(
    cam, shown, truth, feats, lists, recv, back,
    map_m, map_q, map_x, pack, left, right, frame, acc, alpha, pair, share, rows_out, sems,
):
    me = own_number()
    barrier = greet_all(me)
    tile_row = lax.axis_index("tile")
    own = own_cameras(cam, lax.axis_index("view"))

    def at(y):
        return pl.ds(pl.multiple_of(y * 8, 8), 8)


    def similarity(y, carry):
        ones = [shown[at(y + k), :] for k in range(11)]
        twos = [truth[at(y + k), :] for k in range(11)]
        mean_one = blur_lanes(blur_rows(ones))
        mean_two = blur_lanes(blur_rows(twos))
        sq_one = blur_lanes(blur_rows([a * a for a in ones]))
        sq_two = blur_lanes(blur_rows([b * b for b in twos]))
        cross = blur_lanes(blur_rows([a * b for a, b in zip(ones, twos)]))
        num_one = 2.0 * mean_one * mean_two + SSIM_ONE
        num_two = 2.0 * (cross - mean_one * mean_two) + SSIM_TWO
        den_one = mean_one * mean_one + mean_two * mean_two + SSIM_ONE
        den_two = (sq_one - mean_one * mean_one) + (sq_two - mean_two * mean_two) + SSIM_TWO
        den_one_inv = 1.0 / den_one
        den_two_inv = 1.0 / den_two
        both_inv = den_one_inv * den_two_inv
        value = num_one * num_two * both_inv
        row = tile_row * 16 - 5 + y
        scale = jnp.where((row >= 0) & (row < 512), -SSIM_SHARE, 0.0)
        by_mean = 2.0 * mean_two * (num_two - num_one) * both_inv + 2.0 * mean_one * value * (
            den_two_inv - den_one_inv
        )
        map_m[y] = scale * by_mean
        map_q[y] = (-2.0 * scale) * value * den_two_inv
        map_x[y] = (2.0 * scale) * num_one * both_inv
        return carry

    lax.fori_loop(0, 26, similarity, 0)

    def image_grad(y, carry):
        by_mean = blur_lanes(blur_rows([map_m[y + k] for k in range(11)]))
        by_sq = blur_lanes(blur_rows([map_q[y + k] for k in range(11)]))
        by_cross = blur_lanes(blur_rows([map_x[y + k] for k in range(11)]))
        one = shown[at(y + 10), :]
        two = truth[at(y + 10), :]
        gap = one - two
        result = by_mean + one * by_sq + two * by_cross
        result = result + (1.0 - SSIM_SHARE) * gap / jnp.sqrt(gap * gap + SMOOTH_EPS)
        start = pl.multiple_of(y * 8, 8)
        for b in range(4):
            frame[pl.ds(b * 128 + start, 8), :] = result[:, b * 128 : b * 128 + 128]
        return carry

    lax.fori_loop(0, 16, image_grad, 0)
    left[...] = jnp.zeros((512, 128), F32)
    right[...] = jnp.zeros((512, 128), F32)
    for w in range(2):
        for c in range(3):
            for b in range(4):
                for half, target in enumerate((left, right)):
                    start = b * 128 + half * 64 + w * 3 + c
                    block = block_transpose(frame[pl.ds(start, 8, stride=8), :])
                    target[pl.ds((w * 32 + b * 8) * 8 + c, 8, stride=8), :] = block

    tri = triangle((iota((256, 128), 0) & 127) < iota((256, 128), 1))
    suf = triangle((iota((256, 128), 0) & 127) > iota((256, 128), 1))

    def total(terms):
        return jnp.sum(terms, axis=0, keepdims=True)

    def composite(step, carry):
        tiles = [step * GROUP + g for g in range(GROUP)]
        given = [feats[pl.ds(pl.multiple_of(tile * 16, 16), 16), :] for tile in tiles]
        weights, shifts = tile_weights(given, [tile & 31 for tile in tiles], tile_row, tri, alpha, pair)
        slopes = []
        for g, tile in enumerate(tiles):
            rows = slice(g * 256, g * 256 + 256)
            start = pl.multiple_of(tile * 8, 8)
            grad = jnp.concatenate([left[pl.ds(start, 8), :], right[pl.ds(start, 8), :]], axis=1)
            slopes.append(grad)
            colours = stack_splits(given[g][8:16], (0, 1, 0, 2, 0, 1))
            gain = dot(stack_splits(grad, (0, 0, 1, 0, 2, 1)), colours, TN) * weights[g]
            one, two = split2(gain)
            share[rows, :] = gain
            pair[rows, 0:128] = one
            pair[rows, 128:256] = two
        for g, tile in enumerate(tiles):
            rows = slice(g * 256, g * 256 + 256)
            w_one, w_two = split2(weights[g])
            three = stack_splits(slopes[g], (0, 1, 2))
            big = dot(three, w_one, NN)
            small = dot(three, w_two, NN)
            by_colour = (big[0:8] + big[8:16]) + (small[0:8] + small[8:16]) + big[16:24]
            behind = dot(pair[rows, :], suf, NN)
            value = alpha[rows, :]
            delta_x, delta_v = shifts[g]
            cost = share[rows, :] - behind * (value / (1.0 - value))
            sum_0 = jnp.zeros((16, 128), F32)
            sum_1 = jnp.zeros((16, 128), F32)
            sum_2 = jnp.zeros((16, 128), F32)
            for j in range(16):
                delta_y = delta_v - float(j)
                part = cost[j * 16 : j * 16 + 16, :]
                sum_0 = sum_0 + part
                part = part * delta_y
                sum_1 = sum_1 + part
                sum_2 = sum_2 + part * delta_y
            e_0 = total(sum_0)
            e_x = total(sum_0 * delta_x)
            e_y = total(sum_1)
            e_xx = total(sum_0 * delta_x * delta_x)
            e_xy = total(sum_1 * delta_x)
            e_yy = total(sum_2)
            conic_0, conic_1, conic_2 = given[g][2:3], given[g][3:4], given[g][4:5]
            rows_out[pl.ds(pl.multiple_of(tile * 16, 16), 16), :] = jnp.concatenate(
                [
                    -conic_0 * e_x - conic_1 * e_y,
                    -conic_2 * e_y - conic_1 * e_x,
                    -0.5 * e_xx,
                    -e_xy,
                    -0.5 * e_yy,
                    e_0,
                    by_colour[0:3],
                    jnp.zeros((7, 128), F32),
                ],
                axis=0,
            )
        return carry

    lax.fori_loop(0, 64 // GROUP, composite, 0)
    acc[...] = jnp.zeros((1152, 128), F32)
    for w in range(2):

        def scatter(step, carry):
            total = None
            for g in range(SCAT):
                tile = w * 32 + (step * SCAT + g) * 2
                idx = jnp.concatenate([lists[pl.ds(tile, 1), :], lists[pl.ds(tile + 1, 1), :]], axis=1)
                both = rows_out[pl.ds(pl.multiple_of(tile * 16, 32), 32), :]
                rows = jnp.concatenate([both[0:9], both[16:25]], axis=1)
                part = add_up(spread_rows(rows, low_mask(idx)), high_onehot(idx))
                total = part if g == 0 else total + part
            acc[w * 288 : w * 288 + 288, :] += total[:, 0:128]
            acc[576 + w * 288 : 576 + w * 288 + 288, :] += total[:, 128:256]
            return carry

        lax.fori_loop(0, 16 // SCAT, scatter, 0)

    is_first = first_half()
    shift = lax.div(me, 16) + 1
    pl.semaphore_wait(barrier, 127)

    def project_back(step, carry):
        q = lax.rem(step + shift, 8)
        values = unpack_slots(recv, q)
        gauss = values[0:3] + values[4:10]
        row0 = lax.div(q, 4) * 576 + lax.rem(q, 4) * 8

        def grad_of(w, f):
            return acc[pl.ds(pl.multiple_of((w * 9 + f) * 32 + row0, 8), 8), :]

        totals = None
        for w in range(2):
            cam_w = own[w]
            _, pull = jax.vjp(lambda *g: image_values(list(g), cam_w), *gauss)
            parts = pull([grad_of(w, f) for f in range(5)])
            totals = parts if totals is None else [a + b for a, b in zip(totals, parts)]
        totals = list(totals)
        result = totals[0:3] + [grad_of(0, 5) + grad_of(1, 5)] + totals[3:9]
        result += [grad_of(w, 6 + c) for w in range(2) for c in range(3)]
        for f in range(8):
            even = jnp.where(is_first, result[f], half_roll(result[f + 8]))
            odd = jnp.where(is_first, half_roll(result[f]), result[f + 8])
            pack[pl.ds(q * 128 + f, 8, stride=16), :] = even
            pack[pl.ds(q * 128 + 8 + f, 8, stride=16), :] = odd
        push_blocks(pack, back, me, q * 16, 16, sems)
        return carry

    lax.fori_loop(0, 8, project_back, 0)
    finish_blocks(pack, back, me, sems)


def param_kernel(cam, params, recv, chosen, group_in, out, blocks, outs, acc):
    table = all_anchors(cam)
    load_params(params, blocks)
    acc[...] = jnp.zeros((512, 256), F32)
    is_first = first_half()

    def scatter(step, carry):
        totals = [None, None]
        for g in range(BACK):
            p = step * BACK + g
            idx = chosen[pl.ds(p, 1), :]
            onehot = high_onehot(idx)
            mask = low_mask(idx)
            lows, highs = [], []
            for b in range(2):
                start = pl.multiple_of(p * 32 + b * 16, 16)
                even = recv[pl.ds(start, 8), :]
                odd = recv[pl.ds(start + 8, 8), :]
                lows.append(jnp.where(is_first, even, half_roll(odd)))
                highs.append(jnp.where(is_first, half_roll(even), odd))
            for part, pieces in enumerate((lows, highs)):
                rows = jnp.concatenate(pieces, axis=1)
                term = add_up(spread_rows(rows, mask), onehot)
                totals[part] = term if g == 0 else totals[part] + term
        for part in range(2):
            acc[part * 256 : part * 256 + 256, :] += totals[part]
        return carry

    lax.fori_loop(0, 32 // BACK, scatter, 0)

    for high in range(2):
        lane_part = slice(high * 128, high * 128 + 128)

        def compute(low, carry):
            base = (high * 4 + low) * 512
            row0 = pl.multiple_of(low * 8, 8)

            def load(p):
                return blocks[pl.ds(base + p, 8, stride=64), :]

            def save(p, value):
                outs[pl.ds(base + p, 8, stride=64), :] = value

            def grad_of(f):
                return acc[pl.ds(f * 32 + row0, 8), lane_part]

            anchors = group_anchors(table, group_in[pl.ds(row0, 8), lane_part])
            mean = [load(0), load(1), load(2)]
            totals = [grad_of(0), grad_of(1), grad_of(2)]
            _, pull = jax.vjp(lambda *g: shape_values(list(g)), *[load(3 + n) for n in range(7)])
            for n, value in enumerate(pull([grad_of(4 + n) for n in range(6)])):
                save(3 + n, value)
            save(10, grad_of(3) / (1.0 + jnp.exp(load(10))))
            colour = [[grad_of(10 + 3 * w + c) for c in range(3)] for w in range(2)]
            bases, pulls = [], []
            for w in range(2):
                anchor = anchors[w]
                basis, pull = jax.vjp(lambda *m: colour_basis(list(m), anchor)[1:], *mean)
                bases.append(basis)
                pulls.append(pull)
            slopes = [[None] * 15, [None] * 15]
            for c in range(3):
                save(11 + 16 * c, HARMONIC_ZERO * (colour[0][c] + colour[1][c]))
                for k in range(15):
                    coef = load(12 + 16 * c + k)
                    save(
                        12 + 16 * c + k,
                        bases[0][k] * colour[0][c] + bases[1][k] * colour[1][c],
                    )
                    for w in range(2):
                        term = coef * colour[w][c]
                        slopes[w][k] = term if c == 0 else slopes[w][k] + term
            for w in range(2):
                totals = [a + b for a, b in zip(totals, pulls[w](slopes[w]))]
            for n in range(3):
                save(n, totals[n])
            return carry

        lax.fori_loop(0, 4, compute, 0)
    for row in range(64):
        out[:, row * 128 : (row + 1) * 128] = outs[pl.ds(row * 64, 59), :]


def struct(shape, dtype=F32):
    return jax.ShapeDtypeStruct(shape, dtype)


VM = pl.BlockSpec(memory_space=pltpu.VMEM)
SM = pl.BlockSpec(memory_space=pltpu.SMEM)
PARAMS_C = pltpu.CompilerParams(vmem_limit_bytes=VMEM_BYTES)


def comm(number):
    return pltpu.CompilerParams(
        vmem_limit_bytes=VMEM_BYTES, collective_id=number, has_side_effects=True
    )


def run_send(cam, params, slist, counts):
    return pl.pallas_call(
        send_kernel,
        out_shape=(struct((1024, 128)), struct((32, 256)), struct((32, 256), I32)),
        in_specs=[VM, VM, VM, VM],
        out_specs=(VM, VM, VM),
        scratch_shapes=[
            pltpu.VMEM((1024, 128), F32),
            pltpu.VMEM((4096, 128), F32),
            pltpu.VMEM((512, 256), F32),
            pltpu.VMEM((512, 256), BF16),
            pltpu.VMEM((512, 256), BF16),
            pltpu.VMEM((512, 256), BF16),
            pltpu.VMEM((8192, 256), BF16),
            pltpu.VMEM((64, 256), F32),
            pltpu.VMEM((32, 256), I32),
            pltpu.VMEM((32, 256), F32),
            pltpu.SemaphoreType.DMA((2,)),
        ],
        compiler_params=comm(0),
        name="send_values",
    )(cam, params, slist, counts)


def run_render(cam, lens, recv, lists, true):
    return pl.pallas_call(
        render_kernel,
        out_shape=(struct((288, 512)), struct((288, 512)), struct((1024, 128))),
        in_specs=[SM, SM, VM, VM, VM],
        out_specs=(VM, VM, VM),
        scratch_shapes=[
            pltpu.VMEM((576, 256), F32),
            pltpu.VMEM((576, 256), BF16),
            pltpu.VMEM((576, 256), BF16),
            pltpu.VMEM((576, 256), BF16),
            pltpu.VMEM((GROUP * 256, 128), F32),
            pltpu.VMEM((GROUP * 256, 256), BF16),
            pltpu.VMEM((512, 128), F32),
            pltpu.VMEM((512, 128), F32),
            pltpu.VMEM((512, 128), F32),
            pltpu.SemaphoreType.DMA((4,)),
            pltpu.SemaphoreType.DMA((4,)),
        ],
        compiler_params=comm(1),
        name="render_band",
    )(cam, lens, recv, lists, true)


def run_grad(cam, shown, truth, feats, lists, recv):
    return pl.pallas_call(
        grad_kernel,
        out_shape=struct((1024, 128)),
        in_specs=[SM, VM, VM, VM, VM, VM],
        out_specs=VM,
        scratch_shapes=[
            pltpu.VMEM((26, 8, 512), F32),
            pltpu.VMEM((26, 8, 512), F32),
            pltpu.VMEM((26, 8, 512), F32),
            pltpu.VMEM((1024, 128), F32),
            pltpu.VMEM((512, 128), F32),
            pltpu.VMEM((512, 128), F32),
            pltpu.VMEM((512, 128), F32),
            pltpu.VMEM((1152, 128), F32),
            pltpu.VMEM((GROUP * 256, 128), F32),
            pltpu.VMEM((GROUP * 256, 256), BF16),
            pltpu.VMEM((GROUP * 256, 128), F32),
            pltpu.VMEM((1024, 128), F32),
            pltpu.SemaphoreType.DMA((2,)),
        ],
        compiler_params=comm(2),
        name="loss_gradient",
    )(cam, shown, truth, feats, lists, recv)


def run_params(cam, params, recv, chosen, group):
    return pl.pallas_call(
        param_kernel,
        out_shape=struct((59, 8192)),
        in_specs=[VM, VM, VM, VM, VM],
        out_specs=VM,
        scratch_shapes=[
            pltpu.VMEM((4096, 128), F32),
            pltpu.VMEM((4096, 128), F32),
            pltpu.VMEM((512, 256), F32),
        ],
        compiler_params=PARAMS_C,
        name="param_gradient",
    )(cam, params, recv, chosen, group)


def shards(params, send_list, send_counts, camera, ground_truth, tile_lists, list_lengths):
    recv, group, chosen = run_send(camera, params, send_list, send_counts)
    lists = tile_lists.reshape(64, 128)
    true = ground_truth.reshape(96, 512)
    shown, truth, feats = run_render(camera, list_lengths, recv, lists, true)
    returned = run_grad(camera, shown, truth, feats, lists, recv)
    return run_params(camera, params, returned, chosen, group)


def solution(mesh):
    in_specs = (
        P(None, ("view", "tile")),
        P(("view", "tile"), None),
        P(("view", "tile"), None),
        P(),
        P("view", None, "tile", None),
        P("view", "tile", None, None),
        P("view", "tile", None),
    )
    out_specs = P(None, ("view", "tile"))
    return jax.shard_map(shards, mesh=mesh, in_specs=in_specs, out_specs=out_specs, check_vma=False)
```

```python
import jax
import jax.numpy as jnp
import numpy as np
from jax import lax
from jax.experimental import pallas as pl
from jax.experimental.pallas import tpu as pltpu
from jax.sharding import PartitionSpec as P

F32 = jnp.float32
BF16 = jnp.bfloat16
I32 = jnp.int32

TILE = 16
GROUP = 4
FOCAL = 1000.0
LOW_PASS = 0.3
SSIM_SHARE = 0.2
SMOOTH_EPS = 1e-06
SSIM_ONE = 0.0001
SSIM_TWO = 0.0009
LOG2E = 1.4426950408889634
HARMONIC_ZERO = 0.28209479177387814
HARMONIC_ONE = 0.4886025119029199
HARMONIC_TWO = (
    1.0925484305920792,
    -1.0925484305920792,
    0.31539156525252005,
    -1.0925484305920792,
    0.5462742152960396,
)
HARMONIC_THREE = (
    -0.5900435899266435,
    2.890611442640554,
    -0.4570457994644658,
    0.3731763325901154,
    -0.4570457994644658,
    1.445305721320277,
    -0.5900435899266435,
)
VMEM_BYTES = 56 * 1024 * 1024
CHOOSE = 8
GATHER = 4
LOOKUP = 8
SCAT = 8
BACK = 8
MESH = pl.DeviceIdType.MESH
NT = (((1,), (1,)), ((), ()))
NN = (((1,), (0,)), ((), ()))
TN = (((0,), (0,)), ((), ()))


def window_taps():
    offsets_np = np.arange(11) - 5.0
    weights = np.exp(-offsets_np * offsets_np / 4.5)
    weights = weights / weights.sum()
    return [float(weight) for weight in weights]


TAPS = window_taps()


def matrix_product(left_side, right_side):
    return [
        [
            left_side[row_idx][0] * right_side[0][col_idx]
            + left_side[row_idx][1] * right_side[1][col_idx]
            + left_side[row_idx][2] * right_side[2][col_idx]
            for col_idx in range(3)
        ]
        for row_idx in range(3)
    ]


def rotation(angles):
    cos_a, sin_a = (jnp.cos(angles[0]), jnp.sin(angles[0]))
    cos_b, sin_b = (jnp.cos(angles[1]), jnp.sin(angles[1]))
    cos_c, sin_c = (jnp.cos(angles[2]), jnp.sin(angles[2]))
    zero, one = jnp.zeros_like(cos_a), jnp.ones_like(cos_a)
    about_x = [[one, zero, zero], [zero, cos_a, -sin_a], [zero, sin_a, cos_a]]
    about_y = [[cos_b, zero, sin_b], [zero, one, zero], [-sin_b, zero, cos_b]]
    about_z = [[cos_c, -sin_c, zero], [sin_c, cos_c, zero], [zero, zero, one]]
    return matrix_product(about_z, matrix_product(about_y, about_x))


def camera_values(numbers):
    rot = rotation(numbers[0:3])
    move = list(numbers[3:6])
    anchor = [
        -(rot[0][c] * move[0] + rot[1][c] * move[1] + rot[2][c] * move[2]) for c in range(3)
    ]
    return rot[0] + rot[1] + rot[2] + move, anchor


def own_cameras(cam, group):
    return [
        camera_values([jnp.full((8, 128), cam[2 * group + w, n], F32) for n in range(6)])[0]
        for w in range(2)
    ]


def all_anchors(cam):
    numbers = [jnp.broadcast_to(cam[:, n : n + 1], (8, 128)) for n in range(6)]
    anchor = camera_values(numbers)[1]
    return [[jnp.broadcast_to(a[n : n + 1, :], (8, 128)) for a in anchor] for n in range(8)]


def own_number():
    return lax.axis_index("view") * 32 + lax.axis_index("tile")


def device_of(number):
    return (lax.div(number, 32), lax.rem(number, 32))


def greet_all(me):
    barrier = pltpu.get_barrier_semaphore()

    def greet(o, carry):
        pl.semaphore_signal(
            barrier, inc=1, device_id=device_of(lax.rem(me + o, 128)), device_id_type=MESH
        )
        return carry

    lax.fori_loop(1, 128, greet, 0)
    return barrier


def block_copy(pack, recv, me, number, sems):
    return pltpu.make_async_remote_copy(
        src_ref=pack.at[pl.ds(pl.multiple_of(number * 8, 8), 8)],
        dst_ref=recv.at[pl.ds(pl.multiple_of(me * 8, 8), 8)],
        send_sem=sems.at[0],
        recv_sem=sems.at[1],
        device_id=device_of(number),
        device_id_type=MESH,
    )


def push_blocks(pack, recv, me, first, count, sems):
    def push(n, carry):
        number = first + n

        @pl.when(number != me)
        def _():
            block_copy(pack, recv, me, number, sems).start()

        return carry

    lax.fori_loop(0, count, push, 0)


def finish_blocks(pack, recv, me, sems):
    start = pl.multiple_of(me * 8, 8)
    recv[pl.ds(start, 8), :] = pack[pl.ds(start, 8), :]
    whole = pltpu.make_async_remote_copy(
        src_ref=pack.at[pl.ds(0, 1016)],
        dst_ref=recv.at[pl.ds(0, 1016)],
        send_sem=sems.at[0],
        recv_sem=sems.at[1],
        device_id=device_of(lax.rem(me + 1, 128)),
        device_id_type=MESH,
    )
    whole.wait()


def harmonics(dir_x, dir_y, dir_z):
    sq_x, sq_y, sq_z = (dir_x * dir_x, dir_y * dir_y, dir_z * dir_z)
    prod_xy, prod_yz, prod_xz = (dir_x * dir_y, dir_y * dir_z, dir_x * dir_z)
    return [
        None,
        -HARMONIC_ONE * dir_y,
        HARMONIC_ONE * dir_z,
        -HARMONIC_ONE * dir_x,
        HARMONIC_TWO[0] * prod_xy,
        HARMONIC_TWO[1] * prod_yz,
        HARMONIC_TWO[2] * (2.0 * sq_z - sq_x - sq_y),
        HARMONIC_TWO[3] * prod_xz,
        HARMONIC_TWO[4] * (sq_x - sq_y),
        HARMONIC_THREE[0] * dir_y * (3.0 * sq_x - sq_y),
        HARMONIC_THREE[1] * prod_xy * dir_z,
        HARMONIC_THREE[2] * dir_y * (4.0 * sq_z - sq_x - sq_y),
        HARMONIC_THREE[3] * dir_z * (2.0 * sq_z - 3.0 * sq_x - 3.0 * sq_y),
        HARMONIC_THREE[4] * dir_x * (4.0 * sq_z - sq_x - sq_y),
        HARMONIC_THREE[5] * dir_z * (sq_x - sq_y),
        HARMONIC_THREE[6] * dir_x * (sq_x - 3.0 * sq_y),
    ]


def shape_values(gauss):
    scales = [jnp.exp(gauss[axis]) for axis in range(3)]
    norm_inv = 1.0 / jnp.sqrt(
        gauss[3] * gauss[3] + gauss[4] * gauss[4] + gauss[5] * gauss[5] + gauss[6] * gauss[6]
    )
    quat_w, quat_x, quat_y, quat_z = [gauss[3 + n] * norm_inv for n in range(4)]
    quat_rot = [
        [
            1.0 - 2.0 * (quat_y * quat_y + quat_z * quat_z),
            2.0 * (quat_x * quat_y - quat_w * quat_z),
            2.0 * (quat_x * quat_z + quat_w * quat_y),
        ],
        [
            2.0 * (quat_x * quat_y + quat_w * quat_z),
            1.0 - 2.0 * (quat_x * quat_x + quat_z * quat_z),
            2.0 * (quat_y * quat_z - quat_w * quat_x),
        ],
        [
            2.0 * (quat_x * quat_z - quat_w * quat_y),
            2.0 * (quat_y * quat_z + quat_w * quat_x),
            1.0 - 2.0 * (quat_x * quat_x + quat_y * quat_y),
        ],
    ]
    spread = [[quat_rot[r][c] * scales[c] for c in range(3)] for r in range(3)]

    def dot_rows(one, two):
        return (
            spread[one][0] * spread[two][0]
            + spread[one][1] * spread[two][1]
            + spread[one][2] * spread[two][2]
        )

    return [
        dot_rows(0, 0),
        dot_rows(0, 1),
        dot_rows(0, 2),
        dot_rows(1, 1),
        dot_rows(1, 2),
        dot_rows(2, 2),
    ]


def colour_basis(mean, anchor):
    ray_x, ray_y, ray_z = (mean[0] - anchor[0], mean[1] - anchor[1], mean[2] - anchor[2])
    len_inv = 1.0 / jnp.sqrt(ray_x * ray_x + ray_y * ray_y + ray_z * ray_z)
    return harmonics(ray_x * len_inv, ray_y * len_inv, ray_z * len_inv)


def image_values(gauss, cam):
    point = [
        cam[3 * r] * gauss[0] + cam[3 * r + 1] * gauss[1] + cam[3 * r + 2] * gauss[2] + cam[9 + r]
        for r in range(3)
    ]
    inv_depth = 1.0 / point[2]
    jac = FOCAL * inv_depth
    jac_xz = -FOCAL * point[0] * inv_depth * inv_depth
    jac_yz = -FOCAL * point[1] * inv_depth * inv_depth
    row_x = [jac * cam[c] + jac_xz * cam[6 + c] for c in range(3)]
    row_y = [jac * cam[3 + c] + jac_yz * cam[6 + c] for c in range(3)]
    s_xx, s_xy, s_xz, s_yy, s_yz, s_zz = gauss[3:9]
    by_x = [
        s_xx * row_x[0] + s_xy * row_x[1] + s_xz * row_x[2],
        s_xy * row_x[0] + s_yy * row_x[1] + s_yz * row_x[2],
        s_xz * row_x[0] + s_yz * row_x[1] + s_zz * row_x[2],
    ]
    by_y = [
        s_xx * row_y[0] + s_xy * row_y[1] + s_xz * row_y[2],
        s_xy * row_y[0] + s_yy * row_y[1] + s_yz * row_y[2],
        s_xz * row_y[0] + s_yz * row_y[1] + s_zz * row_y[2],
    ]
    cov_xx = row_x[0] * by_x[0] + row_x[1] * by_x[1] + row_x[2] * by_x[2] + LOW_PASS
    cov_xy = row_y[0] * by_x[0] + row_y[1] * by_x[1] + row_y[2] * by_x[2]
    cov_yy = row_y[0] * by_y[0] + row_y[1] * by_y[1] + row_y[2] * by_y[2] + LOW_PASS
    det_inv = 1.0 / (cov_xx * cov_yy - cov_xy * cov_xy)
    return [
        FOCAL * point[0] * inv_depth + 256.0,
        FOCAL * point[1] * inv_depth + 256.0,
        cov_yy * det_inv,
        -cov_xy * det_inv,
        cov_xx * det_inv,
    ]


def split3(value):
    one = value.astype(BF16)
    rest = value - one.astype(F32)
    two = rest.astype(BF16)
    three = (rest - two.astype(F32)).astype(BF16)
    return one, two, three


def split2(value):
    one = value.astype(BF16)
    return one, (value - one.astype(F32)).astype(BF16)


def dot(left, right, dims):
    return lax.dot_general(left, right, dims, preferred_element_type=F32)


def iota(shape, dim):
    return lax.broadcasted_iota(I32, shape, dim)


def high_onehot(idx):
    high = ((idx >> 12) << 7) | (idx & 127)
    return jnp.where(iota((256, idx.shape[1]), 0) == high, 1.0, 0.0).astype(BF16)


def low_mask(idx):
    return iota((32, idx.shape[1]), 0) == ((idx >> 7) & 31)


def pick(tables, start, rows, exact, onehot, mask):
    cut = pl.ds(start * 32, rows * 32)
    total = dot(tables[0][cut, :], onehot, NN) + dot(tables[1][cut, :], onehot, NN)
    fine = dot(tables[2][pl.ds(start * 32, exact * 32), :], onehot, NN)
    if exact < rows:
        fine = jnp.concatenate([total[0 : exact * 32] + fine, total[exact * 32 :]], axis=0)
    else:
        fine = total + fine
    picked = jnp.where(mask[None], fine.reshape(rows, 32, mask.shape[1]), 0.0)
    return jnp.sum(picked, axis=1)


def spread_rows(rows, mask):
    count = rows.shape[0]
    return jnp.where(mask[None], rows[:, None, :], 0.0).reshape(count * 32, rows.shape[1])


def add_up(left, onehot):
    total = None
    for part in split2(left):
        term = dot(part, onehot, NT)
        total = term if total is None else total + term
    return total


def half_roll(value):
    return pltpu.roll(value, 64, 1)


def first_half():
    return iota((8, 128), 1) < 64


def param_copies(params, blocks, sems):
    return [
        pltpu.make_async_copy(
            params.at[:, pl.ds(row * 128, 128)], blocks.at[pl.ds(row * 64, 59)], sems.at[row]
        )
        for row in range(64)
    ]


def result_copy(outs, out, row, sems):
    return pltpu.make_async_copy(
        outs.at[pl.ds(pl.multiple_of(row * 64, 64), 59)],
        out.at[:, pl.ds(pl.multiple_of(row * 128, 128), 128)],
        sems.at[row],
    )


def group_anchors(table, group):
    anchors = []
    for slot in range(2):
        triple = []
        for c in range(3):
            value = table[slot][c]
            for number in range(1, 4):
                value = jnp.where(group > number + 0.5, table[2 * number + slot][c], value)
            triple.append(value)
        anchors.append(triple)
    return anchors


def choose_slots(slist, counts, group_out, chosen, hot, stab, pos, val):
    cnt = counts[...].astype(F32)
    lanes = iota((32, 128), 1)
    first = iota((32, 128), 0) * 4
    slot_lane = iota((32, 256), 1)
    off = jnp.zeros((32, 256), F32)
    own = jnp.zeros((32, 256), F32)
    for j in range(4):
        off_j = jnp.sum(jnp.where(lanes < first + j, cnt, 0.0), axis=1, keepdims=True)
        own_j = jnp.sum(jnp.where(lanes == first + j, cnt, 0.0), axis=1, keepdims=True)
        here = (slot_lane >> 6) == j
        off = jnp.where(here, off_j, off)
        own = jnp.where(here, own_j, own)
    place = (slot_lane & 63).astype(F32)
    pos[...] = jnp.minimum(off + place, 8191.0).astype(I32)
    group = (iota((32, 256), 0) >> 3).astype(F32) + 1.0
    val[...] = jnp.where(place < own, group, 0.0)
    for row in range(64):
        piece = slist[:, row * 128 : (row + 1) * 128]
        half = slice((row // 32) * 128, (row // 32) * 128 + 128)
        stab[row % 32 : row % 32 + 1, half] = (piece >> 6).astype(F32)
        stab[32 + row % 32 : 33 + row % 32, half] = (piece & 63).astype(F32)
    group_out[...] = jnp.zeros((32, 256), F32)
    stab_b = stab[...].astype(BF16)

    def choose(step, carry):
        rows = [step * CHOOSE + g for g in range(CHOOSE)]
        places = [pos[pl.ds(p, 1), :] for p in rows]
        found = [dot(stab_b, high_onehot(idx), NN) for idx in places]
        total = None
        for g, p in enumerate(rows):
            both = found[g][0:32] * 64.0 + found[g][32:64]
            ids = jnp.sum(jnp.where(low_mask(places[g]), both, 0.0), axis=0, keepdims=True).astype(I32)
            chosen[pl.ds(p, 1), :] = ids
            onehot = high_onehot(ids)
            hot[pl.ds(pl.multiple_of(p * 256, 256), 256), :] = onehot
            left = jnp.where(low_mask(ids), val[pl.ds(p, 1), :], 0.0).astype(BF16)
            part = dot(left, onehot, NT)
            total = part if g == 0 else total + part
        group_out[...] += total
        return carry

    lax.fori_loop(0, 32 // CHOOSE, choose, 0)


def source_tables(table, group_out, blocks, tab, t0, t1, t2):
    for high in range(2):
        lane_part = slice(high * 128, high * 128 + 128)

        def compute(low, carry):
            base = (high * 4 + low) * 512
            row0 = pl.multiple_of(low * 8, 8)

            def load(p):
                return blocks[pl.ds(base + p, 8, stride=64), :]

            anchors = group_anchors(table, group_out[pl.ds(row0, 8), lane_part])
            mean = [load(0), load(1), load(2)]
            values = mean + shape_values([load(3 + n) for n in range(7)])
            values += [0.99 / (1.0 + jnp.exp(-load(10)))]
            bases = [colour_basis(mean, anchor) for anchor in anchors]
            sums = [[None] * 3, [None] * 3]
            for c in range(3):
                flat = 0.5 + HARMONIC_ZERO * load(11 + 16 * c)
                sums[0][c] = flat
                sums[1][c] = flat
                for k in range(1, 16):
                    coef = load(11 + 16 * c + k)
                    sums[0][c] = sums[0][c] + bases[0][k] * coef
                    sums[1][c] = sums[1][c] + bases[1][k] * coef
            values += sums[0] + sums[1]
            for f in range(16):
                tab[pl.ds(f * 32 + row0, 8), lane_part] = values[f]
            return carry

        lax.fori_loop(0, 4, compute, 0)
    t0[...], t1[...], t2[...] = split3(tab[...])


def send_slots(me, chosen, hot, tables, send, recv, sems):
    is_first = first_half()
    shift = lax.div(me, 4) + 1

    def gather(step, carry):
        for g in range(GATHER):
            p = lax.rem(step * GATHER + g + shift, 32)
            onehot = hot[pl.ds(pl.multiple_of(p * 256, 256), 256), :]
            mask = low_mask(chosen[pl.ds(p, 1), :])
            low = pick(tables, 0, 8, 8, onehot, mask)
            high = pick(tables, 8, 8, 1, onehot, mask)
            for b in range(2):
                one = low[:, b * 128 : b * 128 + 128]
                two = high[:, b * 128 : b * 128 + 128]
                start = pl.multiple_of(p * 32 + b * 16, 16)
                send[pl.ds(start, 8), :] = jnp.where(is_first, one, half_roll(two))
                send[pl.ds(start + 8, 8), :] = jnp.where(is_first, half_roll(one), two)
        for g in range(GATHER):
            p = lax.rem(step * GATHER + g + shift, 32)
            push_blocks(send, recv, me, p * 4, 4, sems)
        return carry

    lax.fori_loop(0, 32 // GATHER, gather, 0)


def unpack_slots(recv, q):
    is_first = first_half()
    low, high = [], []
    for f in range(8):
        even = recv[pl.ds(q * 128 + f, 8, stride=16), :]
        odd = recv[pl.ds(q * 128 + 8 + f, 8, stride=16), :]
        low.append(jnp.where(is_first, even, half_roll(odd)))
        high.append(jnp.where(is_first, half_roll(even), odd))
    return low + high


def block_transpose(value):
    turn = (iota((8, 128), 0) - (iota((8, 128), 1) >> 4)) & 7
    result = value
    for d in range(1, 8):
        moved = pltpu.roll(pltpu.roll(value, d, 0), 128 - 16 * d, 1)
        result = jnp.where(turn == d, moved, result)
    return result


def triangle(keep):
    return jnp.where(keep, 1.0, 0.0).astype(BF16)


def pixel_rows(feat, column, tile_row):
    def row(f):
        return jnp.broadcast_to(feat[f : f + 1, :], (16, 128))

    shift = iota((16, 128), 0).astype(F32) + (column * 16).astype(F32)
    delta_x = row(0) - shift
    square = (-0.5 * LOG2E) * row(2) * delta_x * delta_x
    cross = -LOG2E * row(3) * delta_x
    quad = (-0.5 * LOG2E) * row(4)
    delta_v = row(1) - (tile_row * 16).astype(F32)
    return delta_x, delta_v, square, cross, quad, row(5)


def tile_weights(feats, columns, bases, tile_row, tri, alpha, pair):
    for g, feat in enumerate(feats):
        delta_x, delta_v, square, cross, quad, opacity = pixel_rows(feat, columns[g], tile_row)
        for j in range(16):
            delta_y = delta_v - float(j)
            value = opacity * jnp.exp2(square + delta_y * (cross + quad * delta_y))
            rows = slice(g * 256 + j * 16, g * 256 + j * 16 + 16)
            alpha[pl.ds(pl.multiple_of(bases[g] + j * 16, 16), 16), :] = value
            one, two = split2(jnp.log(1.0 - value))
            pair[rows, 0:128] = one
            pair[rows, 128:256] = two
    weights = []
    for g in range(len(feats)):
        rows = slice(g * 256, g * 256 + 256)
        weights.append(jnp.exp(dot(pair[rows, :], tri, NN)) * alpha[pl.ds(bases[g], 256), :])
    return weights


def stack_splits(value, order):
    one, two, three = split3(value)
    parts = [one.astype(F32), two.astype(F32), three.astype(F32)]
    return jnp.concatenate([parts[n] for n in order], axis=0).astype(BF16)


def greet_bands(tile_row):
    barrier = pltpu.get_barrier_semaphore()
    for step in (1, 31):
        other = lax.rem(tile_row + step, 32)
        pl.semaphore_signal(barrier, inc=1, device_id={"tile": other}, device_id_type=MESH)
    pl.semaphore_wait(barrier, 2)


def halo_copies(rows, tile_row, sems):
    def copy(source, target, step, n):
        return pltpu.make_async_remote_copy(
            src_ref=rows.at[pl.ds(source, 80)],
            dst_ref=rows.at[pl.ds(target, 80)],
            send_sem=sems.at[2 * n],
            recv_sem=sems.at[2 * n + 1],
            device_id={"tile": lax.rem(tile_row + step, 32)},
            device_id_type=MESH,
        )

    return copy(128, 0, 1, 0), copy(80, 208, 31, 1)


def send_halo(rows, tile_row, sems):
    down, up = halo_copies(rows, tile_row, sems)

    @pl.when(tile_row < 31)
    def _():
        down.start()

    @pl.when(tile_row > 0)
    def _():
        up.start()


def take_halo(rows, tile_row, sems):
    down, up = halo_copies(rows, tile_row, sems)

    @pl.when(tile_row < 31)
    def _():
        down.wait_send()
        up.wait_recv()

    @pl.when(tile_row > 0)
    def _():
        up.wait_send()
        down.wait_recv()

    @pl.when(tile_row == 0)
    def _():
        rows[0:80, :] = jnp.zeros((80, 512), F32)

    @pl.when(tile_row == 31)
    def _():
        rows[208:288, :] = jnp.zeros((80, 512), F32)


def true_rows(true, truth, frame):
    frame[...] = jnp.zeros((512, 128), F32)
    for n in range(6):
        for b in range(4):
            for half in range(2):
                rows = true[n * 16 + half * 8 : n * 16 + half * 8 + 8, b * 128 : b * 128 + 128]
                frame[pl.ds(b * 128 + half * 64 + n, 8, stride=8), :] = rows
    for b in range(4):
        truth[80:208, b * 128 : b * 128 + 128] = frame[b * 128 : b * 128 + 128, :]


def band_tables(own, recv, tab, t0, t1, t2):
    for high in range(2):
        lane_part = slice(high * 128, high * 128 + 128)

        def compute(low, carry):
            row0 = pl.multiple_of(low * 8, 8)
            values = unpack_slots(recv, high * 4 + low)
            for w in range(2):
                seen = image_values(values[0:9], own[w])
                seen = seen + [values[9]] + values[10 + 3 * w : 13 + 3 * w]
                for f in range(9):
                    tab[pl.ds((w * 9 + f) * 32 + row0, 8), lane_part] = seen[f]
            return carry

        lax.fori_loop(0, 4, compute, 0)
    t0[...], t1[...], t2[...] = split3(tab[...])


def list_features(lists, lens, tables, feats):
    lane = iota((1, 256), 1)
    for w in range(2):

        def look_up(step, carry):
            for g in range(LOOKUP):
                tile = w * 32 + (step * LOOKUP + g) * 2
                idx = jnp.concatenate([lists[pl.ds(tile, 1), :], lists[pl.ds(tile + 1, 1), :]], axis=1)
                rows = pick(tables, w * 9, 9, 5, high_onehot(idx), low_mask(idx))
                length = jnp.where(lane < 128, lens[w, 0, tile - w * 32], lens[w, 0, tile - w * 32 + 1])
                rows = jnp.where((lane & 127) < length, rows, 0.0)
                start = pl.multiple_of(tile * 16, 32)
                for b in range(2):
                    part = rows[:, b * 128 : b * 128 + 128]
                    feats[pl.ds(start + b * 16, 6), :] = part[0:6]
                    feats[pl.ds(start + b * 16 + 6, 2), :] = jnp.zeros((2, 128), F32)
                    feats[pl.ds(start + b * 16 + 8, 3), :] = part[6:9]
                    feats[pl.ds(start + b * 16 + 11, 5), :] = jnp.zeros((5, 128), F32)
            return carry

        lax.fori_loop(0, 16 // LOOKUP, look_up, 0)


def render_tiles(tile_row, feats, alpha, keep, pair, left, right):
    tri = triangle((iota((256, 128), 0) & 127) < iota((256, 128), 1))

    def composite(step, carry):
        tiles = [step * GROUP + g for g in range(GROUP)]
        given = [feats[pl.ds(pl.multiple_of(tile * 16, 16), 16), :] for tile in tiles]
        bases = [pl.multiple_of(tile * 256, 256) for tile in tiles]
        weights = tile_weights(
            given, [tile & 31 for tile in tiles], bases, tile_row, tri, alpha, pair
        )
        for g, tile in enumerate(tiles):
            keep[pl.ds(bases[g], 256), :] = weights[g]
            one, two = split2(weights[g])
            colours = stack_splits(given[g][8:16], (0, 1, 2))
            big = dot(colours, one, NT)
            small = dot(colours, two, NT)
            result = (big[0:8] + big[8:16]) + (small[0:8] + small[8:16]) + big[16:24]
            start = pl.multiple_of(tile * 8, 8)
            left[pl.ds(start, 8), :] = result[:, 0:128]
            right[pl.ds(start, 8), :] = result[:, 128:256]
        return carry

    lax.fori_loop(0, 64 // GROUP, composite, 0)


def shown_rows(left, right, frame, shown):
    for w in range(2):
        for c in range(3):
            for b in range(4):
                for half, source in enumerate((left, right)):
                    block = source[pl.ds((w * 32 + b * 8) * 8 + c, 8, stride=8), :]
                    start = b * 128 + half * 64 + w * 3 + c
                    frame[pl.ds(start, 8, stride=8), :] = block_transpose(block)
    for b in range(4):
        shown[80:208, b * 128 : b * 128 + 128] = frame[b * 128 : b * 128 + 128, :]


def blur_lanes(value):
    padded = jnp.concatenate([value, jnp.zeros((8, 128), F32)], axis=1)
    moved = [pltpu.roll(padded, 639, 1), padded, pltpu.roll(padded, 1, 1), pltpu.roll(padded, 2, 1)]

    def part(far):
        total = None
        for near in range(-1, 3):
            tap = 4 * far + near
            if -5 <= tap <= 5:
                term = TAPS[5 + tap] * moved[near + 1]
                total = term if total is None else total + term
        return total

    total = part(0) + pltpu.roll(part(1), 4, 1) + pltpu.roll(part(-1), 636, 1)
    return total[:, 0:512]


def blur_rows(rows):
    total = TAPS[5] * rows[5]
    for k in range(1, 6):
        total = total + TAPS[5 + k] * (rows[5 - k] + rows[5 + k])
    return total


def at(y):
    return pl.ds(pl.multiple_of(y * 8, 8), 8)


def true_means(truth, mean):
    def one_row(y, carry):
        mean[y] = blur_lanes(blur_rows([truth[at(y + k), :] for k in range(11)]))
        return carry

    lax.fori_loop(0, 26, one_row, 0)


def loss_slopes(tile_row, shown, truth, mean, map_m, map_q, map_x, frame):
    def similarity(y, carry):
        ones = [shown[at(y + k), :] for k in range(11)]
        twos = [truth[at(y + k), :] for k in range(11)]
        mean_one = blur_lanes(blur_rows(ones))
        mean_two = mean[y]
        squares = blur_lanes(blur_rows([a * a + b * b for a, b in zip(ones, twos)]))
        cross = blur_lanes(blur_rows([a * b for a, b in zip(ones, twos)]))
        num_one = 2.0 * mean_one * mean_two + SSIM_ONE
        num_two = 2.0 * (cross - mean_one * mean_two) + SSIM_TWO
        power = mean_one * mean_one + mean_two * mean_two
        den_one_inv = 1.0 / (power + SSIM_ONE)
        den_two_inv = 1.0 / (squares - power + SSIM_TWO)
        both_inv = den_one_inv * den_two_inv
        value = num_one * num_two * both_inv
        row = tile_row * 16 - 5 + y
        scale = jnp.where((row >= 0) & (row < 512), -SSIM_SHARE, 0.0)
        by_mean = 2.0 * mean_two * (num_two - num_one) * both_inv + 2.0 * mean_one * value * (
            den_two_inv - den_one_inv
        )
        map_m[y] = scale * by_mean
        map_q[y] = (-2.0 * scale) * value * den_two_inv
        map_x[y] = (2.0 * scale) * num_one * both_inv
        return carry

    lax.fori_loop(0, 26, similarity, 0, unroll=2)

    def image_grad(y, carry):
        by_mean = blur_lanes(blur_rows([map_m[y + k] for k in range(11)]))
        by_sq = blur_lanes(blur_rows([map_q[y + k] for k in range(11)]))
        by_cross = blur_lanes(blur_rows([map_x[y + k] for k in range(11)]))
        one = shown[at(y + 10), :]
        two = truth[at(y + 10), :]
        gap = one - two
        result = by_mean + one * by_sq + two * by_cross
        result = result + (1.0 - SSIM_SHARE) * gap / jnp.sqrt(gap * gap + SMOOTH_EPS)
        start = pl.multiple_of(y * 8, 8)
        for b in range(4):
            frame[pl.ds(b * 128 + start, 8), :] = result[:, b * 128 : b * 128 + 128]
        return carry

    lax.fori_loop(0, 16, image_grad, 0, unroll=2)


def tile_slopes(frame, left, right):
    left[...] = jnp.zeros((512, 128), F32)
    right[...] = jnp.zeros((512, 128), F32)
    for w in range(2):
        for c in range(3):
            for b in range(4):
                for half, target in enumerate((left, right)):
                    start = b * 128 + half * 64 + w * 3 + c
                    block = block_transpose(frame[pl.ds(start, 8, stride=8), :])
                    target[pl.ds((w * 32 + b * 8) * 8 + c, 8, stride=8), :] = block


def feature_slopes(tile_row, feats, alpha, keep, pair, left, right, rows_out):
    suf = triangle((iota((256, 128), 0) & 127) > iota((256, 128), 1))

    def total(terms):
        return jnp.sum(terms, axis=0, keepdims=True)

    def composite(step, carry):
        tiles = [step * GROUP + g for g in range(GROUP)]
        given = [feats[pl.ds(pl.multiple_of(tile * 16, 16), 16), :] for tile in tiles]
        bases = [pl.ds(pl.multiple_of(tile * 256, 256), 256) for tile in tiles]
        slopes, gains = [], []
        for g, tile in enumerate(tiles):
            rows = slice(g * 256, g * 256 + 256)
            start = pl.multiple_of(tile * 8, 8)
            grad = jnp.concatenate([left[pl.ds(start, 8), :], right[pl.ds(start, 8), :]], axis=1)
            slopes.append(grad)
            colours = stack_splits(given[g][8:16], (0, 1, 0, 2, 0, 1))
            gain = dot(stack_splits(grad, (0, 0, 1, 0, 2, 1)), colours, TN) * keep[bases[g], :]
            one, two = split2(gain)
            gains.append(gain)
            pair[rows, 0:128] = one
            pair[rows, 128:256] = two
        for g, tile in enumerate(tiles):
            rows = slice(g * 256, g * 256 + 256)
            w_one, w_two = split2(keep[bases[g], :])
            three = stack_splits(slopes[g], (0, 1, 2))
            big = dot(three, w_one, NN)
            small = dot(three, w_two, NN)
            by_colour = (big[0:8] + big[8:16]) + (small[0:8] + small[8:16]) + big[16:24]
            behind = dot(pair[rows, :], suf, NN)
            value = alpha[bases[g], :]
            feat = given[g]
            delta_x = jnp.broadcast_to(feat[0:1, :], (16, 128)) - (
                iota((16, 128), 0).astype(F32) + ((tile & 31) * 16).astype(F32)
            )
            delta_v = jnp.broadcast_to(feat[1:2, :], (16, 128)) - (tile_row * 16).astype(F32)
            cost = gains[g] - behind * (value / (1.0 - value))
            sum_0 = jnp.zeros((16, 128), F32)
            sum_1 = jnp.zeros((16, 128), F32)
            sum_2 = jnp.zeros((16, 128), F32)
            for j in range(16):
                delta_y = delta_v - float(j)
                part = cost[j * 16 : j * 16 + 16, :]
                sum_0 = sum_0 + part
                part = part * delta_y
                sum_1 = sum_1 + part
                sum_2 = sum_2 + part * delta_y
            e_0 = total(sum_0)
            e_x = total(sum_0 * delta_x)
            e_y = total(sum_1)
            e_xx = total(sum_0 * delta_x * delta_x)
            e_xy = total(sum_1 * delta_x)
            e_yy = total(sum_2)
            conic_0, conic_1, conic_2 = feat[2:3], feat[3:4], feat[4:5]
            rows_out[pl.ds(pl.multiple_of(tile * 16, 16), 16), :] = jnp.concatenate(
                [
                    -conic_0 * e_x - conic_1 * e_y,
                    -conic_2 * e_y - conic_1 * e_x,
                    -0.5 * e_xx,
                    -e_xy,
                    -0.5 * e_yy,
                    e_0,
                    by_colour[0:3],
                    jnp.zeros((7, 128), F32),
                ],
                axis=0,
            )
        return carry

    lax.fori_loop(0, 64 // GROUP, composite, 0)


def scatter_features(lists, rows_out, acc):
    acc[...] = jnp.zeros((1152, 128), F32)
    for w in range(2):

        def scatter(step, carry):
            total = None
            for g in range(SCAT):
                tile = w * 32 + (step * SCAT + g) * 2
                idx = jnp.concatenate([lists[pl.ds(tile, 1), :], lists[pl.ds(tile + 1, 1), :]], axis=1)
                both = rows_out[pl.ds(pl.multiple_of(tile * 16, 32), 32), :]
                rows = jnp.concatenate([both[0:9], both[16:25]], axis=1)
                part = add_up(spread_rows(rows, low_mask(idx)), high_onehot(idx))
                total = part if g == 0 else total + part
            acc[w * 288 : w * 288 + 288, :] += total[:, 0:128]
            acc[576 + w * 288 : 576 + w * 288 + 288, :] += total[:, 128:256]
            return carry

        lax.fori_loop(0, 16 // SCAT, scatter, 0)


def return_slots(me, own, recv, acc, pack, back, sems):
    is_first = first_half()
    shift = lax.div(me, 16) + 1

    def project_back(step, carry):
        q = lax.rem(step + shift, 8)
        values = unpack_slots(recv, q)
        row0 = lax.div(q, 4) * 576 + lax.rem(q, 4) * 8

        def grad_of(w, f):
            return acc[pl.ds(pl.multiple_of((w * 9 + f) * 32 + row0, 8), 8), :]

        totals = None
        for w in range(2):
            cam_w = own[w]
            _, pull = jax.vjp(lambda *g: image_values(list(g), cam_w), *values[0:9])
            parts = pull([grad_of(w, f) for f in range(5)])
            totals = parts if totals is None else [a + b for a, b in zip(totals, parts)]
        result = list(totals) + [grad_of(0, 5) + grad_of(1, 5)]
        result += [grad_of(w, 6 + c) for w in range(2) for c in range(3)]
        for f in range(8):
            even = jnp.where(is_first, result[f], half_roll(result[f + 8]))
            odd = jnp.where(is_first, half_roll(result[f]), result[f + 8])
            pack[pl.ds(q * 128 + f, 8, stride=16), :] = even
            pack[pl.ds(q * 128 + 8 + f, 8, stride=16), :] = odd
        push_blocks(pack, back, me, q * 16, 16, sems)
        return carry

    lax.fori_loop(0, 8, project_back, 0)


def scatter_slots(chosen, hot, recv, acc):
    is_first = first_half()
    acc[...] = jnp.zeros((1024, 128), F32)

    def scatter(step, carry):
        totals = [None, None]
        for g in range(BACK):
            p = step * BACK + g
            onehot = hot[pl.ds(pl.multiple_of(p * 256, 256), 256), :]
            mask = low_mask(chosen[pl.ds(p, 1), :])
            lows, highs = [], []
            for b in range(2):
                start = pl.multiple_of(p * 32 + b * 16, 16)
                even = recv[pl.ds(start, 8), :]
                odd = recv[pl.ds(start + 8, 8), :]
                lows.append(jnp.where(is_first, even, half_roll(odd)))
                highs.append(jnp.where(is_first, half_roll(even), odd))
            for part, pieces in enumerate((lows, highs)):
                rows = jnp.concatenate(pieces, axis=1)
                term = add_up(spread_rows(rows, mask), onehot)
                totals[part] = term if g == 0 else totals[part] + term
        for part in range(2):
            for high in range(2):
                start = high * 512 + part * 256
                acc[start : start + 256, :] += totals[part][:, high * 128 : high * 128 + 128]
        return carry

    lax.fori_loop(0, 32 // BACK, scatter, 0)


def param_slopes(table, group_in, blocks, acc, outs, out, sems):
    def compute(q, carry):
        base = q * 512
        row0 = lax.rem(q, 4) * 8
        high = lax.div(q, 4)

        def load(p):
            return blocks[pl.ds(base + p, 8, stride=64), :]

        def save(p, value):
            outs[pl.ds(base + p, 8, stride=64), :] = value

        def grad_of(f):
            return acc[pl.ds(pl.multiple_of(high * 512 + f * 32 + row0, 8), 8), :]

        group = group_in[pl.ds(pl.multiple_of(row0, 8), 8), pl.ds(pl.multiple_of(high * 128, 128), 128)]
        anchors = group_anchors(table, group)
        mean = [load(0), load(1), load(2)]
        totals = [grad_of(0), grad_of(1), grad_of(2)]
        _, pull = jax.vjp(lambda *g: shape_values(list(g)), *[load(3 + n) for n in range(7)])
        for n, value in enumerate(pull([grad_of(3 + n) for n in range(6)])):
            save(3 + n, value)
        save(10, grad_of(9) / (1.0 + jnp.exp(load(10))))
        colour = [[grad_of(10 + 3 * w + c) for c in range(3)] for w in range(2)]
        bases, pulls = [], []
        for w in range(2):
            anchor = anchors[w]
            basis, pull = jax.vjp(lambda *m: colour_basis(list(m), anchor)[1:], *mean)
            bases.append(basis)
            pulls.append(pull)
        slopes = [[None] * 15, [None] * 15]
        for c in range(3):
            save(11 + 16 * c, HARMONIC_ZERO * (colour[0][c] + colour[1][c]))
            for k in range(15):
                coef = load(12 + 16 * c + k)
                save(12 + 16 * c + k, bases[0][k] * colour[0][c] + bases[1][k] * colour[1][c])
                for w in range(2):
                    term = coef * colour[w][c]
                    slopes[w][k] = term if c == 0 else slopes[w][k] + term
        for w in range(2):
            totals = [a + b for a, b in zip(totals, pulls[w](slopes[w]))]
        for n in range(3):
            save(n, totals[n])
        for n in range(8):
            result_copy(outs, out, q * 8 + n, sems).start()
        return carry

    lax.fori_loop(0, 8, compute, 0)

    def finish(row, carry):
        result_copy(outs, out, row, sems).wait()
        return carry

    lax.fori_loop(0, 64, finish, 0)


def splat_kernel(
    cam_v, cam_s, params, slist, counts, lens, lists, true, out,
    blocks, outs, group, chosen, hot, stab, pos, val, tab_s, s0, s1, s2,
    send, recv, tab_d, d0, d1, d2, feats, alpha, keep, pair, left, right, frame,
    shown, truth, mean, map_m, map_q, map_x, rows_out, acc_d, pack, back, acc_s,
    in_sems, out_sems, send_sems, back_sems, shown_sems, truth_sems,
):
    me = own_number()
    tile_row = lax.axis_index("tile")
    loads = param_copies(params, blocks, in_sems)
    for load in loads:
        load.start()
    barrier = greet_all(me)
    own = own_cameras(cam_s, lax.axis_index("view"))
    table = all_anchors(cam_v)
    true_rows(true, truth, frame)
    choose_slots(slist, counts, group, chosen, hot, stab, pos, val)
    for load in loads:
        load.wait()
    source_tables(table, group, blocks, tab_s, s0, s1, s2)
    pl.semaphore_wait(barrier, 127)
    send_halo(truth, tile_row, truth_sems)
    send_slots(me, chosen, hot, [s0, s1, s2], send, recv, send_sems)
    take_halo(truth, tile_row, truth_sems)
    true_means(truth, mean)
    finish_blocks(send, recv, me, send_sems)
    band_tables(own, recv, tab_d, d0, d1, d2)
    list_features(lists, lens, [d0, d1, d2], feats)
    render_tiles(tile_row, feats, alpha, keep, pair, left, right)
    shown_rows(left, right, frame, shown)
    send_halo(shown, tile_row, shown_sems)
    take_halo(shown, tile_row, shown_sems)
    loss_slopes(tile_row, shown, truth, mean, map_m, map_q, map_x, frame)
    tile_slopes(frame, left, right)
    feature_slopes(tile_row, feats, alpha, keep, pair, left, right, rows_out)
    scatter_features(lists, rows_out, acc_d)
    return_slots(me, own, recv, acc_d, pack, back, back_sems)
    finish_blocks(pack, back, me, back_sems)
    scatter_slots(chosen, hot, back, acc_s)
    param_slopes(table, group, blocks, acc_s, outs, out, out_sems)


def struct(shape, dtype=F32):
    return jax.ShapeDtypeStruct(shape, dtype)


VM = pl.BlockSpec(memory_space=pltpu.VMEM)
SM = pl.BlockSpec(memory_space=pltpu.SMEM)
ANY = pl.BlockSpec(memory_space=pl.ANY)


def vm(*shape, dtype=F32):
    return pltpu.VMEM(shape, dtype)


def shards(params, send_list, send_counts, camera, ground_truth, tile_lists, list_lengths):
    lists = tile_lists.reshape(64, 128)
    true = ground_truth.reshape(96, 512)
    dma = pltpu.SemaphoreType.DMA
    return pl.pallas_call(
        splat_kernel,
        out_shape=struct((59, 8192)),
        in_specs=[VM, SM, ANY, VM, VM, SM, VM, VM],
        out_specs=ANY,
        scratch_shapes=[
            vm(4096, 128),
            vm(4096, 128),
            vm(32, 256),
            vm(32, 256, dtype=I32),
            vm(8192, 256, dtype=BF16),
            vm(64, 256),
            vm(32, 256, dtype=I32),
            vm(32, 256),
            vm(512, 256),
            vm(512, 256, dtype=BF16),
            vm(512, 256, dtype=BF16),
            vm(512, 256, dtype=BF16),
            vm(1024, 128),
            vm(1024, 128),
            vm(576, 256),
            vm(576, 256, dtype=BF16),
            vm(576, 256, dtype=BF16),
            vm(576, 256, dtype=BF16),
            vm(1024, 128),
            vm(16384, 128),
            vm(16384, 128),
            vm(GROUP * 256, 256, dtype=BF16),
            vm(512, 128),
            vm(512, 128),
            vm(512, 128),
            vm(288, 512),
            vm(288, 512),
            vm(26, 8, 512),
            vm(26, 8, 512),
            vm(26, 8, 512),
            vm(26, 8, 512),
            vm(1024, 128),
            vm(1152, 128),
            vm(1024, 128),
            vm(1024, 128),
            vm(1024, 128),
            dma((64,)),
            dma((64,)),
            dma((2,)),
            dma((2,)),
            dma((4,)),
            dma((4,)),
        ],
        compiler_params=pltpu.CompilerParams(
            vmem_limit_bytes=VMEM_BYTES, collective_id=0, has_side_effects=True
        ),
        name="splat_gradient",
    )(camera, camera, params, send_list, send_counts, list_lengths, lists, true)


def solution(mesh):
    in_specs = (
        P(None, ("view", "tile")),
        P(("view", "tile"), None),
        P(("view", "tile"), None),
        P(),
        P("view", None, "tile", None),
        P("view", "tile", None, None),
        P("view", "tile", None),
    )
    out_specs = P(None, ("view", "tile"))
    return jax.shard_map(shards, mesh=mesh, in_specs=in_specs, out_specs=out_specs, check_vma=False)
```

```python
import jax
import jax.numpy as jnp
import numpy as np
from jax import lax
from jax.experimental import pallas as pl
from jax.experimental.pallas import tpu as pltpu
from jax.sharding import PartitionSpec as P

F32 = jnp.float32
BF16 = jnp.bfloat16
I32 = jnp.int32

TILE = 16
GROUP = 4
FOCAL = 1000.0
LOW_PASS = 0.3
SSIM_SHARE = 0.2
SMOOTH_EPS = 1e-06
SSIM_ONE = 0.0001
SSIM_TWO = 0.0009
LOG2E = 1.4426950408889634
HARMONIC_ZERO = 0.28209479177387814
HARMONIC_ONE = 0.4886025119029199
HARMONIC_TWO = (
    1.0925484305920792,
    -1.0925484305920792,
    0.31539156525252005,
    -1.0925484305920792,
    0.5462742152960396,
)
HARMONIC_THREE = (
    -0.5900435899266435,
    2.890611442640554,
    -0.4570457994644658,
    0.3731763325901154,
    -0.4570457994644658,
    1.445305721320277,
    -0.5900435899266435,
)
VMEM_BYTES = 56 * 1024 * 1024
CHOOSE = 8
GATHER = 4
LOOKUP = 8
SCAT = 8
BACK = 8
MESH = pl.DeviceIdType.MESH
FIRST_MEANS = 10
NT = (((1,), (1,)), ((), ()))
NN = (((1,), (0,)), ((), ()))
TN = (((0,), (0,)), ((), ()))


def window_taps():
    offsets_np = np.arange(11) - 5.0
    weights = np.exp(-offsets_np * offsets_np / 4.5)
    weights = weights / weights.sum()
    return [float(weight) for weight in weights]


TAPS = window_taps()


def matrix_product(left_side, right_side):
    return [
        [
            left_side[row_idx][0] * right_side[0][col_idx]
            + left_side[row_idx][1] * right_side[1][col_idx]
            + left_side[row_idx][2] * right_side[2][col_idx]
            for col_idx in range(3)
        ]
        for row_idx in range(3)
    ]


def rotation(angles):
    cos_a, sin_a = (jnp.cos(angles[0]), jnp.sin(angles[0]))
    cos_b, sin_b = (jnp.cos(angles[1]), jnp.sin(angles[1]))
    cos_c, sin_c = (jnp.cos(angles[2]), jnp.sin(angles[2]))
    zero, one = jnp.zeros_like(cos_a), jnp.ones_like(cos_a)
    about_x = [[one, zero, zero], [zero, cos_a, -sin_a], [zero, sin_a, cos_a]]
    about_y = [[cos_b, zero, sin_b], [zero, one, zero], [-sin_b, zero, cos_b]]
    about_z = [[cos_c, -sin_c, zero], [sin_c, cos_c, zero], [zero, zero, one]]
    return matrix_product(about_z, matrix_product(about_y, about_x))


def camera_values(numbers):
    rot = rotation(numbers[0:3])
    move = list(numbers[3:6])
    anchor = [
        -(rot[0][c] * move[0] + rot[1][c] * move[1] + rot[2][c] * move[2]) for c in range(3)
    ]
    return rot[0] + rot[1] + rot[2] + move, anchor


def own_cameras(cam, group):
    return [
        camera_values([jnp.full((8, 128), cam[2 * group + w, n], F32) for n in range(6)])[0]
        for w in range(2)
    ]


def all_anchors(cam):
    numbers = [jnp.broadcast_to(cam[:, n : n + 1], (8, 128)) for n in range(6)]
    anchor = camera_values(numbers)[1]
    return [[jnp.broadcast_to(a[n : n + 1, :], (8, 128)) for a in anchor] for n in range(8)]


def own_number():
    return lax.axis_index("view") * 32 + lax.axis_index("tile")


def device_of(number):
    return (lax.div(number, 32), lax.rem(number, 32))


def greet(barrier, me, o):
    pl.semaphore_signal(
        barrier, inc=1, device_id=device_of(lax.rem(me + o, 128)), device_id_type=MESH
    )


def block_copy(pack, recv, me, number, sems):
    return pltpu.make_async_remote_copy(
        src_ref=pack.at[pl.ds(pl.multiple_of(number * 8, 8), 8)],
        dst_ref=recv.at[pl.ds(pl.multiple_of(me * 8, 8), 8)],
        send_sem=sems.at[0],
        recv_sem=sems.at[1],
        device_id=device_of(number),
        device_id_type=MESH,
    )


def push_blocks(pack, recv, me, first, count, sems):
    for n in range(1, count):
        block_copy(pack, recv, me, first + lax.rem(me + n, count), sems).start()

    @pl.when(lax.div(me, count) * count != first)
    def _():
        block_copy(pack, recv, me, first + lax.rem(me, count), sems).start()


def finish_blocks(pack, recv, me, sems):
    start = pl.multiple_of(me * 8, 8)
    recv[pl.ds(start, 8), :] = pack[pl.ds(start, 8), :]
    whole = pltpu.make_async_remote_copy(
        src_ref=pack.at[pl.ds(0, 1016)],
        dst_ref=recv.at[pl.ds(0, 1016)],
        send_sem=sems.at[0],
        recv_sem=sems.at[1],
        device_id=device_of(lax.rem(me + 1, 128)),
        device_id_type=MESH,
    )
    whole.wait()


def harmonics(dir_x, dir_y, dir_z):
    sq_x, sq_y, sq_z = (dir_x * dir_x, dir_y * dir_y, dir_z * dir_z)
    prod_xy, prod_yz, prod_xz = (dir_x * dir_y, dir_y * dir_z, dir_x * dir_z)
    return [
        None,
        -HARMONIC_ONE * dir_y,
        HARMONIC_ONE * dir_z,
        -HARMONIC_ONE * dir_x,
        HARMONIC_TWO[0] * prod_xy,
        HARMONIC_TWO[1] * prod_yz,
        HARMONIC_TWO[2] * (2.0 * sq_z - sq_x - sq_y),
        HARMONIC_TWO[3] * prod_xz,
        HARMONIC_TWO[4] * (sq_x - sq_y),
        HARMONIC_THREE[0] * dir_y * (3.0 * sq_x - sq_y),
        HARMONIC_THREE[1] * prod_xy * dir_z,
        HARMONIC_THREE[2] * dir_y * (4.0 * sq_z - sq_x - sq_y),
        HARMONIC_THREE[3] * dir_z * (2.0 * sq_z - 3.0 * sq_x - 3.0 * sq_y),
        HARMONIC_THREE[4] * dir_x * (4.0 * sq_z - sq_x - sq_y),
        HARMONIC_THREE[5] * dir_z * (sq_x - sq_y),
        HARMONIC_THREE[6] * dir_x * (sq_x - 3.0 * sq_y),
    ]


def shape_values(gauss):
    scales = [jnp.exp(gauss[axis]) for axis in range(3)]
    norm_inv = 1.0 / jnp.sqrt(
        gauss[3] * gauss[3] + gauss[4] * gauss[4] + gauss[5] * gauss[5] + gauss[6] * gauss[6]
    )
    quat_w, quat_x, quat_y, quat_z = [gauss[3 + n] * norm_inv for n in range(4)]
    quat_rot = [
        [
            1.0 - 2.0 * (quat_y * quat_y + quat_z * quat_z),
            2.0 * (quat_x * quat_y - quat_w * quat_z),
            2.0 * (quat_x * quat_z + quat_w * quat_y),
        ],
        [
            2.0 * (quat_x * quat_y + quat_w * quat_z),
            1.0 - 2.0 * (quat_x * quat_x + quat_z * quat_z),
            2.0 * (quat_y * quat_z - quat_w * quat_x),
        ],
        [
            2.0 * (quat_x * quat_z - quat_w * quat_y),
            2.0 * (quat_y * quat_z + quat_w * quat_x),
            1.0 - 2.0 * (quat_x * quat_x + quat_y * quat_y),
        ],
    ]
    spread = [[quat_rot[r][c] * scales[c] for c in range(3)] for r in range(3)]

    def dot_rows(one, two):
        return (
            spread[one][0] * spread[two][0]
            + spread[one][1] * spread[two][1]
            + spread[one][2] * spread[two][2]
        )

    return [
        dot_rows(0, 0),
        dot_rows(0, 1),
        dot_rows(0, 2),
        dot_rows(1, 1),
        dot_rows(1, 2),
        dot_rows(2, 2),
    ]


def colour_basis(mean, anchor):
    ray_x, ray_y, ray_z = (mean[0] - anchor[0], mean[1] - anchor[1], mean[2] - anchor[2])
    len_inv = 1.0 / jnp.sqrt(ray_x * ray_x + ray_y * ray_y + ray_z * ray_z)
    return harmonics(ray_x * len_inv, ray_y * len_inv, ray_z * len_inv)


def image_values(gauss, cam):
    point = [
        cam[3 * r] * gauss[0] + cam[3 * r + 1] * gauss[1] + cam[3 * r + 2] * gauss[2] + cam[9 + r]
        for r in range(3)
    ]
    inv_depth = 1.0 / point[2]
    jac = FOCAL * inv_depth
    jac_xz = -FOCAL * point[0] * inv_depth * inv_depth
    jac_yz = -FOCAL * point[1] * inv_depth * inv_depth
    row_x = [jac * cam[c] + jac_xz * cam[6 + c] for c in range(3)]
    row_y = [jac * cam[3 + c] + jac_yz * cam[6 + c] for c in range(3)]
    s_xx, s_xy, s_xz, s_yy, s_yz, s_zz = gauss[3:9]
    by_x = [
        s_xx * row_x[0] + s_xy * row_x[1] + s_xz * row_x[2],
        s_xy * row_x[0] + s_yy * row_x[1] + s_yz * row_x[2],
        s_xz * row_x[0] + s_yz * row_x[1] + s_zz * row_x[2],
    ]
    by_y = [
        s_xx * row_y[0] + s_xy * row_y[1] + s_xz * row_y[2],
        s_xy * row_y[0] + s_yy * row_y[1] + s_yz * row_y[2],
        s_xz * row_y[0] + s_yz * row_y[1] + s_zz * row_y[2],
    ]
    cov_xx = row_x[0] * by_x[0] + row_x[1] * by_x[1] + row_x[2] * by_x[2] + LOW_PASS
    cov_xy = row_y[0] * by_x[0] + row_y[1] * by_x[1] + row_y[2] * by_x[2]
    cov_yy = row_y[0] * by_y[0] + row_y[1] * by_y[1] + row_y[2] * by_y[2] + LOW_PASS
    det_inv = 1.0 / (cov_xx * cov_yy - cov_xy * cov_xy)
    return [
        FOCAL * point[0] * inv_depth + 256.0,
        FOCAL * point[1] * inv_depth + 256.0,
        cov_yy * det_inv,
        -cov_xy * det_inv,
        cov_xx * det_inv,
    ]


def split3(value):
    one = value.astype(BF16)
    rest = value - one.astype(F32)
    two = rest.astype(BF16)
    three = (rest - two.astype(F32)).astype(BF16)
    return one, two, three


def split2(value):
    one = value.astype(BF16)
    return one, (value - one.astype(F32)).astype(BF16)


def dot(left, right, dims):
    return lax.dot_general(left, right, dims, preferred_element_type=F32)


def iota(shape, dim):
    return lax.broadcasted_iota(I32, shape, dim)


def high_onehot(idx):
    high = ((idx >> 12) << 7) | (idx & 127)
    return jnp.where(iota((256, idx.shape[1]), 0) == high, 1.0, 0.0).astype(BF16)


def low_mask(idx):
    return iota((32, idx.shape[1]), 0) == ((idx >> 7) & 31)


def stack_tables(tab, stack, rows, exact):
    one, two, three = split3(tab)
    stack[0 : rows * 32, :] = one
    stack[rows * 32 : rows * 64, :] = two
    stack[rows * 64 : rows * 64 + exact * 32, :] = three[0 : exact * 32]


def pick(stack, rows, exact, onehot, mask):
    found = dot(stack, onehot, NN)
    total = found[0 : rows * 32] + found[rows * 32 : rows * 64]
    fine = total[0 : exact * 32] + found[rows * 64 : rows * 64 + exact * 32]

    def low_sum(part, count):
        picked = jnp.where(mask[None], part.reshape(count, 32, mask.shape[1]), 0.0)
        return jnp.sum(picked, axis=1)

    return jnp.concatenate(
        [low_sum(fine, exact), low_sum(total[exact * 32 :], rows - exact)], axis=0
    )


def spread_rows(rows, mask):
    count = rows.shape[0]
    return jnp.where(mask[None], rows[:, None, :], 0.0).reshape(count * mask.shape[0], rows.shape[1])


def add_up(left, onehot):
    size = left.shape[0]
    found = dot(jnp.concatenate(split2(left), axis=0), onehot, NT)
    return found[0:size] + found[size:]


def half_roll(value):
    return pltpu.roll(value, 64, 1)


def first_half():
    return iota((8, 128), 1) < 64


def param_copies(params, blocks, sems):
    return [
        pltpu.make_async_copy(
            params.at[:, pl.ds(row * 128, 128)], blocks.at[pl.ds(row * 64, 59)], sems.at[row]
        )
        for row in range(64)
    ]


def result_copy(outs, out, row, sems):
    return pltpu.make_async_copy(
        outs.at[pl.ds(pl.multiple_of(row * 64, 64), 59)],
        out.at[:, pl.ds(pl.multiple_of(row * 128, 128), 128)],
        sems.at[row],
    )


def group_anchors(table, group):
    anchors = []
    for slot in range(2):
        triple = []
        for c in range(3):
            value = table[slot][c]
            for number in range(1, 4):
                value = jnp.where(group > number + 0.5, table[2 * number + slot][c], value)
            triple.append(value)
        anchors.append(triple)
    return anchors


def choose_slots(barrier, me, slist, counts, group_out, chosen, hot, stab, pos, val):
    cnt = counts[...].astype(F32)
    lanes = iota((32, 128), 1)
    first = iota((32, 128), 0) * 4
    slot_lane = iota((32, 256), 1)
    off = jnp.zeros((32, 256), F32)
    own = jnp.zeros((32, 256), F32)
    for j in range(4):
        off_j = jnp.sum(jnp.where(lanes < first + j, cnt, 0.0), axis=1, keepdims=True)
        own_j = jnp.sum(jnp.where(lanes == first + j, cnt, 0.0), axis=1, keepdims=True)
        here = (slot_lane >> 6) == j
        off = jnp.where(here, off_j, off)
        own = jnp.where(here, own_j, own)
    place = (slot_lane & 63).astype(F32)
    pos[...] = jnp.minimum(off + place, 8191.0).astype(I32)
    group = (iota((32, 256), 0) >> 3).astype(F32) + 1.0
    val[...] = jnp.where(place < own, group, 0.0)
    for row in range(64):
        piece = slist[:, row * 128 : (row + 1) * 128]
        half = slice((row // 32) * 128, (row // 32) * 128 + 128)
        stab[row % 32 : row % 32 + 1, half] = (piece >> 6).astype(F32)
        stab[32 + row % 32 : 33 + row % 32, half] = (piece & 63).astype(F32)
    group_out[...] = jnp.zeros((32, 256), F32)
    stab_b = stab[...].astype(BF16)

    def choose(step, carry):
        rows = [step * CHOOSE + g for g in range(CHOOSE)]
        places = [pos[pl.ds(p, 1), :] for p in rows]
        found = [dot(stab_b, high_onehot(idx), NN) for idx in places]
        total = None
        for g, p in enumerate(rows):
            both = found[g][0:32] * 64.0 + found[g][32:64]
            ids = jnp.sum(jnp.where(low_mask(places[g]), both, 0.0), axis=0, keepdims=True).astype(I32)
            chosen[pl.ds(p, 1), :] = ids
            onehot = high_onehot(ids)
            hot[pl.ds(pl.multiple_of(p * 256, 256), 256), :] = onehot
            left = jnp.where(low_mask(ids), val[pl.ds(p, 1), :], 0.0).astype(BF16)
            part = dot(left, onehot, NT)
            total = part if g == 0 else total + part
            for n in range(4):
                if g * 4 + n < CHOOSE * 4 - 1:
                    greet(barrier, me, step * (CHOOSE * 4) + g * 4 + n + 1)
        group_out[...] += total

        @pl.when(step < 32 // CHOOSE - 1)
        def _():
            greet(barrier, me, (step + 1) * (CHOOSE * 4))

        return carry

    lax.fori_loop(0, 32 // CHOOSE, choose, 0)


def source_tables(table, group_out, blocks, tab, stack):
    for high in range(2):
        lane_part = slice(high * 128, high * 128 + 128)

        def compute(low, carry):
            base = (high * 4 + low) * 512
            row0 = pl.multiple_of(low * 8, 8)

            def load(p):
                return blocks[pl.ds(base + p, 8, stride=64), :]

            anchors = group_anchors(table, group_out[pl.ds(row0, 8), lane_part])
            mean = [load(0), load(1), load(2)]
            values = mean + shape_values([load(3 + n) for n in range(7)])
            values += [0.99 / (1.0 + jnp.exp(-load(10)))]
            bases = [colour_basis(mean, anchor) for anchor in anchors]
            sums = [[None] * 3, [None] * 3]
            for c in range(3):
                flat = 0.5 + HARMONIC_ZERO * load(11 + 16 * c)
                sums[0][c] = flat
                sums[1][c] = flat
                for k in range(1, 16):
                    coef = load(11 + 16 * c + k)
                    sums[0][c] = sums[0][c] + bases[0][k] * coef
                    sums[1][c] = sums[1][c] + bases[1][k] * coef
            values += sums[0] + sums[1]
            for f in range(16):
                tab[pl.ds(f * 32 + row0, 8), lane_part] = values[f]
            return carry

        lax.fori_loop(0, 4, compute, 0)
    stack_tables(tab[...], stack, 16, 9)


def send_slots(me, chosen, hot, stack, send, recv, sems):
    is_first = first_half()
    shift = lax.div(me, 4) + 1

    def group_at(step, g):
        return lax.rem(step * GATHER + g + shift, 32)

    def gather(step, carry):
        for g in range(GATHER):
            p = group_at(step, g)
            onehot = hot[pl.ds(pl.multiple_of(p * 256, 256), 256), :]
            rows = pick(stack[...], 16, 9, onehot, low_mask(chosen[pl.ds(p, 1), :]))
            for b in range(2):
                one = rows[0:8, b * 128 : b * 128 + 128]
                two = rows[8:16, b * 128 : b * 128 + 128]
                start = pl.multiple_of(p * 32 + b * 16, 16)
                send[pl.ds(start, 8), :] = jnp.where(is_first, one, half_roll(two))
                send[pl.ds(start + 8, 8), :] = jnp.where(is_first, half_roll(one), two)
            if g < GATHER - 1:
                for n in range(4):
                    block_copy(send, recv, me, p * 4 + n, sems).start()

        @pl.when(step < 32 // GATHER - 1)
        def _():
            for n in range(4):
                block_copy(send, recv, me, group_at(step, GATHER - 1) * 4 + n, sems).start()

        return carry

    lax.fori_loop(0, 32 // GATHER, gather, 0)
    for n in range(1, 4):
        number = lax.div(me, 4) * 4 + lax.rem(me + n, 4)
        block_copy(send, recv, me, number, sems).start()


def unpack_slots(recv, q):
    is_first = first_half()
    low, high = [], []
    for f in range(8):
        even = recv[pl.ds(q * 128 + f, 8, stride=16), :]
        odd = recv[pl.ds(q * 128 + 8 + f, 8, stride=16), :]
        low.append(jnp.where(is_first, even, half_roll(odd)))
        high.append(jnp.where(is_first, half_roll(even), odd))
    return low + high


def block_transpose(value):
    turn = (iota((8, 128), 0) - (iota((8, 128), 1) >> 4)) & 7
    result = value
    for d in range(1, 8):
        moved = pltpu.roll(pltpu.roll(value, d, 0), 128 - 16 * d, 1)
        result = jnp.where(turn == d, moved, result)
    return result


def triangle(keep):
    return jnp.where(keep, 1.0, 0.0).astype(BF16)


def pixel_rows(feat, column, tile_row):
    def row(f):
        return jnp.broadcast_to(feat[f : f + 1, :], (16, 128))

    shift = iota((16, 128), 0).astype(F32) + (column * 16).astype(F32)
    delta_x = row(0) - shift
    square = (-0.5 * LOG2E) * row(2) * delta_x * delta_x
    cross = -LOG2E * row(3) * delta_x
    quad = (-0.5 * LOG2E) * row(4)
    delta_v = row(1) - (tile_row * 16).astype(F32)
    return delta_x, delta_v, square, cross, quad, row(5)


def tile_weights(feats, columns, bases, tile_row, tri, alpha, pair):
    for g, feat in enumerate(feats):
        delta_x, delta_v, square, cross, quad, opacity = pixel_rows(feat, columns[g], tile_row)
        for j in range(16):
            delta_y = delta_v - float(j)
            value = opacity * jnp.exp2(square + delta_y * (cross + quad * delta_y))
            rows = slice(g * 256 + j * 16, g * 256 + j * 16 + 16)
            alpha[pl.ds(pl.multiple_of(bases[g] + j * 16, 16), 16), :] = value
            one, two = split2(jnp.log(1.0 - value))
            pair[rows, 0:128] = one
            pair[rows, 128:256] = two
    weights = []
    for g in range(len(feats)):
        rows = slice(g * 256, g * 256 + 256)
        weights.append(jnp.exp(dot(pair[rows, :], tri, NN)) * alpha[pl.ds(bases[g], 256), :])
    return weights


def stack_splits(value, order):
    one, two, three = split3(value)
    parts = [one.astype(F32), two.astype(F32), three.astype(F32)]
    return jnp.concatenate([parts[n] for n in order], axis=0).astype(BF16)


def greet_bands(tile_row):
    barrier = pltpu.get_barrier_semaphore()
    for step in (1, 31):
        other = lax.rem(tile_row + step, 32)
        pl.semaphore_signal(barrier, inc=1, device_id={"tile": other}, device_id_type=MESH)
    pl.semaphore_wait(barrier, 2)


def halo_copies(rows, tile_row, sems):
    def copy(source, target, step, n):
        return pltpu.make_async_remote_copy(
            src_ref=rows.at[pl.ds(source, 80)],
            dst_ref=rows.at[pl.ds(target, 80)],
            send_sem=sems.at[2 * n],
            recv_sem=sems.at[2 * n + 1],
            device_id={"tile": lax.rem(tile_row + step, 32)},
            device_id_type=MESH,
        )

    return copy(128, 0, 1, 0), copy(80, 208, 31, 1)


def send_halo(rows, tile_row, sems):
    down, up = halo_copies(rows, tile_row, sems)

    @pl.when(tile_row < 31)
    def _():
        down.start()

    @pl.when(tile_row > 0)
    def _():
        up.start()


def take_halo(rows, tile_row, sems):
    down, up = halo_copies(rows, tile_row, sems)

    @pl.when(tile_row < 31)
    def _():
        down.wait_send()
        up.wait_recv()

    @pl.when(tile_row > 0)
    def _():
        up.wait_send()
        down.wait_recv()

    @pl.when(tile_row == 0)
    def _():
        rows[0:80, :] = jnp.zeros((80, 512), F32)

    @pl.when(tile_row == 31)
    def _():
        rows[208:288, :] = jnp.zeros((80, 512), F32)


def true_rows(true, truth, frame):
    frame[...] = jnp.zeros((512, 128), F32)
    for n in range(6):
        for b in range(4):
            for half in range(2):
                rows = true[n * 16 + half * 8 : n * 16 + half * 8 + 8, b * 128 : b * 128 + 128]
                frame[pl.ds(b * 128 + half * 64 + n, 8, stride=8), :] = rows
    for b in range(4):
        truth[80:208, b * 128 : b * 128 + 128] = frame[b * 128 : b * 128 + 128, :]


def band_tables(own, recv, tab, stacks):
    for high in range(2):
        lane_part = slice(high * 128, high * 128 + 128)

        def compute(low, carry):
            row0 = pl.multiple_of(low * 8, 8)
            values = unpack_slots(recv, high * 4 + low)
            for w in range(2):
                seen = image_values(values[0:9], own[w])
                seen = seen + [values[9]] + values[10 + 3 * w : 13 + 3 * w]
                for f in range(9):
                    tab[pl.ds((w * 9 + f) * 32 + row0, 8), lane_part] = seen[f]
            return carry

        lax.fori_loop(0, 4, compute, 0)
    for w in range(2):
        stack_tables(tab[w * 288 : w * 288 + 288, :], stacks[w], 9, 5)


def list_features(lists, lens, tables, feats):
    lane = iota((1, 256), 1)
    for w in range(2):

        def look_up(step, carry):
            for g in range(LOOKUP):
                tile = w * 32 + (step * LOOKUP + g) * 2
                idx = jnp.concatenate([lists[pl.ds(tile, 1), :], lists[pl.ds(tile + 1, 1), :]], axis=1)
                rows = pick(tables[w][...], 9, 5, high_onehot(idx), low_mask(idx))
                length = jnp.where(lane < 128, lens[w, 0, tile - w * 32], lens[w, 0, tile - w * 32 + 1])
                rows = jnp.where((lane & 127) < length, rows, 0.0)
                start = pl.multiple_of(tile * 16, 32)
                for b in range(2):
                    part = rows[:, b * 128 : b * 128 + 128]
                    feats[pl.ds(start + b * 16, 6), :] = part[0:6]
                    feats[pl.ds(start + b * 16 + 6, 2), :] = jnp.zeros((2, 128), F32)
                    feats[pl.ds(start + b * 16 + 8, 3), :] = part[6:9]
                    feats[pl.ds(start + b * 16 + 11, 5), :] = jnp.zeros((5, 128), F32)
            return carry

        lax.fori_loop(0, 16 // LOOKUP, look_up, 0)


def render_tiles(tile_row, feats, alpha, keep, pair, left, right):
    tri = triangle((iota((256, 128), 0) & 127) < iota((256, 128), 1))

    def composite(step, carry):
        tiles = [step * GROUP + g for g in range(GROUP)]
        given = [feats[pl.ds(pl.multiple_of(tile * 16, 16), 16), :] for tile in tiles]
        bases = [pl.multiple_of(tile * 256, 256) for tile in tiles]
        weights = tile_weights(
            given, [tile & 31 for tile in tiles], bases, tile_row, tri, alpha, pair
        )
        for g, tile in enumerate(tiles):
            keep[pl.ds(bases[g], 256), :] = weights[g]
            one, two = split2(weights[g])
            colours = stack_splits(given[g][8:16], (0, 1, 2))
            big = dot(colours, one, NT)
            small = dot(colours, two, NT)
            result = (big[0:8] + big[8:16]) + (small[0:8] + small[8:16]) + big[16:24]
            start = pl.multiple_of(tile * 8, 8)
            left[pl.ds(start, 8), :] = result[:, 0:128]
            right[pl.ds(start, 8), :] = result[:, 128:256]
        return carry

    lax.fori_loop(0, 64 // GROUP, composite, 0)


def shown_rows(left, right, frame, shown):
    for w in range(2):
        for c in range(3):
            for b in range(4):
                for half, source in enumerate((left, right)):
                    block = source[pl.ds((w * 32 + b * 8) * 8 + c, 8, stride=8), :]
                    start = b * 128 + half * 64 + w * 3 + c
                    frame[pl.ds(start, 8, stride=8), :] = block_transpose(block)
    for b in range(4):
        shown[80:208, b * 128 : b * 128 + 128] = frame[b * 128 : b * 128 + 128, :]


def blur_lanes(value):
    padded = jnp.concatenate([value, jnp.zeros((8, 128), F32)], axis=1)
    moved = [pltpu.roll(padded, 639, 1), padded, pltpu.roll(padded, 1, 1), pltpu.roll(padded, 2, 1)]

    def part(far):
        total = None
        for near in range(-1, 3):
            tap = 4 * far + near
            if -5 <= tap <= 5:
                term = TAPS[5 + tap] * moved[near + 1]
                total = term if total is None else total + term
        return total

    total = part(0) + pltpu.roll(part(1), 4, 1) + pltpu.roll(part(-1), 636, 1)
    return total[:, 0:512]


def blur_rows(rows):
    total = TAPS[5] * rows[5]
    for k in range(1, 6):
        total = total + TAPS[5 + k] * (rows[5 - k] + rows[5 + k])
    return total


def at(y):
    return pl.ds(pl.multiple_of(y * 8, 8), 8)


def true_means(truth, mean, first, count):
    def one_row(n, carry):
        y = first + n
        mean[y] = blur_lanes(blur_rows([truth[at(y + k), :] for k in range(11)]))
        return carry

    lax.fori_loop(0, count, one_row, 0, unroll=count // 2)


def loss_slopes(tile_row, shown, truth, mean, map_m, map_q, map_x, frame):
    def similarity(y, carry):
        ones = [shown[at(y + k), :] for k in range(11)]
        twos = [truth[at(y + k), :] for k in range(11)]
        mean_one = blur_lanes(blur_rows(ones))
        mean_two = mean[y]
        squares = blur_lanes(blur_rows([a * a + b * b for a, b in zip(ones, twos)]))
        cross = blur_lanes(blur_rows([a * b for a, b in zip(ones, twos)]))
        num_one = 2.0 * mean_one * mean_two + SSIM_ONE
        num_two = 2.0 * (cross - mean_one * mean_two) + SSIM_TWO
        power = mean_one * mean_one + mean_two * mean_two
        den_one_inv = 1.0 / (power + SSIM_ONE)
        den_two_inv = 1.0 / (squares - power + SSIM_TWO)
        both_inv = den_one_inv * den_two_inv
        value = num_one * num_two * both_inv
        row = tile_row * 16 - 5 + y
        scale = jnp.where((row >= 0) & (row < 512), -SSIM_SHARE, 0.0)
        by_mean = 2.0 * mean_two * (num_two - num_one) * both_inv + 2.0 * mean_one * value * (
            den_two_inv - den_one_inv
        )
        map_m[y] = scale * by_mean
        map_q[y] = (-2.0 * scale) * value * den_two_inv
        map_x[y] = (2.0 * scale) * num_one * both_inv
        return carry

    lax.fori_loop(0, 26, similarity, 0, unroll=2)

    def image_grad(y, carry):
        by_mean = blur_lanes(blur_rows([map_m[y + k] for k in range(11)]))
        by_sq = blur_lanes(blur_rows([map_q[y + k] for k in range(11)]))
        by_cross = blur_lanes(blur_rows([map_x[y + k] for k in range(11)]))
        one = shown[at(y + 10), :]
        two = truth[at(y + 10), :]
        gap = one - two
        result = by_mean + one * by_sq + two * by_cross
        result = result + (1.0 - SSIM_SHARE) * gap / jnp.sqrt(gap * gap + SMOOTH_EPS)
        start = pl.multiple_of(y * 8, 8)
        for b in range(4):
            frame[pl.ds(b * 128 + start, 8), :] = result[:, b * 128 : b * 128 + 128]
        return carry

    lax.fori_loop(0, 16, image_grad, 0, unroll=2)


def tile_slopes(frame, left, right):
    left[...] = jnp.zeros((512, 128), F32)
    right[...] = jnp.zeros((512, 128), F32)
    for w in range(2):
        for c in range(3):
            for b in range(4):
                for half, target in enumerate((left, right)):
                    start = b * 128 + half * 64 + w * 3 + c
                    block = block_transpose(frame[pl.ds(start, 8, stride=8), :])
                    target[pl.ds((w * 32 + b * 8) * 8 + c, 8, stride=8), :] = block


def feature_slopes(tile_row, feats, alpha, keep, pair, left, right, rows_out):
    suf = triangle((iota((256, 128), 0) & 127) > iota((256, 128), 1))

    def total(terms):
        return jnp.sum(terms, axis=0, keepdims=True)

    def composite(step, carry):
        tiles = [step * GROUP + g for g in range(GROUP)]
        given = [feats[pl.ds(pl.multiple_of(tile * 16, 16), 16), :] for tile in tiles]
        bases = [pl.ds(pl.multiple_of(tile * 256, 256), 256) for tile in tiles]
        slopes, gains = [], []
        for g, tile in enumerate(tiles):
            rows = slice(g * 256, g * 256 + 256)
            start = pl.multiple_of(tile * 8, 8)
            grad = jnp.concatenate([left[pl.ds(start, 8), :], right[pl.ds(start, 8), :]], axis=1)
            slopes.append(grad)
            colours = stack_splits(given[g][8:16], (0, 1, 0, 2, 0, 1))
            gain = dot(stack_splits(grad, (0, 0, 1, 0, 2, 1)), colours, TN) * keep[bases[g], :]
            one, two = split2(gain)
            gains.append(gain)
            pair[rows, 0:128] = one
            pair[rows, 128:256] = two
        for g, tile in enumerate(tiles):
            rows = slice(g * 256, g * 256 + 256)
            w_one, w_two = split2(keep[bases[g], :])
            three = stack_splits(slopes[g], (0, 1, 2))
            big = dot(three, w_one, NN)
            small = dot(three, w_two, NN)
            by_colour = (big[0:8] + big[8:16]) + (small[0:8] + small[8:16]) + big[16:24]
            behind = dot(pair[rows, :], suf, NN)
            value = alpha[bases[g], :]
            feat = given[g]
            delta_x = jnp.broadcast_to(feat[0:1, :], (16, 128)) - (
                iota((16, 128), 0).astype(F32) + ((tile & 31) * 16).astype(F32)
            )
            delta_v = jnp.broadcast_to(feat[1:2, :], (16, 128)) - (tile_row * 16).astype(F32)
            cost = gains[g] - behind * (value / (1.0 - value))
            sum_0 = jnp.zeros((16, 128), F32)
            sum_1 = jnp.zeros((16, 128), F32)
            sum_2 = jnp.zeros((16, 128), F32)
            for j in range(16):
                delta_y = delta_v - float(j)
                part = cost[j * 16 : j * 16 + 16, :]
                sum_0 = sum_0 + part
                part = part * delta_y
                sum_1 = sum_1 + part
                sum_2 = sum_2 + part * delta_y
            e_0 = total(sum_0)
            e_x = total(sum_0 * delta_x)
            e_y = total(sum_1)
            e_xx = total(sum_0 * delta_x * delta_x)
            e_xy = total(sum_1 * delta_x)
            e_yy = total(sum_2)
            conic_0, conic_1, conic_2 = feat[2:3], feat[3:4], feat[4:5]
            rows_out[pl.ds(pl.multiple_of(tile * 16, 16), 16), :] = jnp.concatenate(
                [
                    -conic_0 * e_x - conic_1 * e_y,
                    -conic_2 * e_y - conic_1 * e_x,
                    -0.5 * e_xx,
                    -e_xy,
                    -0.5 * e_yy,
                    e_0,
                    by_colour[0:3],
                    jnp.zeros((7, 128), F32),
                ],
                axis=0,
            )
        return carry

    lax.fori_loop(0, 64 // GROUP, composite, 0)


def scatter_features(lists, rows_out, acc, half):
    acc[...] = jnp.zeros((576, 128), F32)
    for w in range(2):

        def scatter(step, carry):
            total = None
            for g in range(SCAT):
                tile = w * 32 + (step * SCAT + g) * 2
                idx = jnp.concatenate([lists[pl.ds(tile, 1), :], lists[pl.ds(tile + 1, 1), :]], axis=1)
                both = rows_out[pl.ds(pl.multiple_of(tile * 16, 32), 32), :]
                rows = jnp.concatenate([both[0:9], both[16:25]], axis=1)
                mask = iota((16, 256), 0) + half * 16 == ((idx >> 7) & 31)
                part = add_up(spread_rows(rows, mask), high_onehot(idx))
                total = part if g == 0 else total + part
            acc[w * 144 : w * 144 + 144, :] += total[:, 0:128]
            acc[288 + w * 144 : 288 + w * 144 + 144, :] += total[:, 128:256]
            return carry

        lax.fori_loop(0, 16 // SCAT, scatter, 0)


def return_slots(me, own, recv, acc, pack, back, sems, half):
    is_first = first_half()

    def project_back(step, carry):
        high = lax.div(step, 2)
        low = lax.rem(step, 2)
        q = high * 4 + half * 2 + low
        values = unpack_slots(recv, q)
        row0 = high * 288 + low * 8

        def grad_of(w, f):
            return acc[pl.ds(pl.multiple_of((w * 9 + f) * 16 + row0, 8), 8), :]

        totals = None
        for w in range(2):
            cam_w = own[w]
            _, pull = jax.vjp(lambda *g: image_values(list(g), cam_w), *values[0:9])
            parts = pull([grad_of(w, f) for f in range(5)])
            totals = parts if totals is None else [a + b for a, b in zip(totals, parts)]
        result = list(totals) + [grad_of(0, 5) + grad_of(1, 5)]
        result += [grad_of(w, 6 + c) for w in range(2) for c in range(3)]
        for f in range(8):
            even = jnp.where(is_first, result[f], half_roll(result[f + 8]))
            odd = jnp.where(is_first, half_roll(result[f]), result[f + 8])
            pack[pl.ds(q * 128 + f, 8, stride=16), :] = even
            pack[pl.ds(q * 128 + 8 + f, 8, stride=16), :] = odd
        push_blocks(pack, back, me, q * 16, 16, sems)
        return carry

    lax.fori_loop(0, 4, project_back, 0)


def first_part(number):
    return lax.rem(lax.div(number, 4), 2)


def own_part(number):
    return lax.rem(lax.div(number, 32), 2)


def finish_part(pack, back, me, sems, early):
    def wait(rows):
        pltpu.make_async_remote_copy(
            src_ref=pack.at[pl.ds(0, rows)],
            dst_ref=back.at[pl.ds(0, rows)],
            send_sem=sems.at[0],
            recv_sem=sems.at[1],
            device_id=device_of(lax.rem(me + 1, 128)),
            device_id_type=MESH,
        ).wait()

    with_own = (first_part(me) == own_part(me)) if early else (first_part(me) != own_part(me))

    @pl.when(with_own)
    def _():
        wait(504)

    @pl.when(jnp.logical_not(with_own))
    def _():
        wait(512)


def scatter_slots(chosen, hot, recv, acc, part_no):
    is_first = first_half()

    def scatter(step, carry):
        totals = [None, None]
        for g in range(BACK):
            p = (step * BACK + g) * 2 + part_no
            onehot = hot[pl.ds(pl.multiple_of(p * 256, 256), 256), :]
            mask = low_mask(chosen[pl.ds(p, 1), :])
            lows, highs = [], []
            for b in range(2):
                start = pl.multiple_of(p * 32 + b * 16, 16)
                even = recv[pl.ds(start, 8), :]
                odd = recv[pl.ds(start + 8, 8), :]
                lows.append(jnp.where(is_first, even, half_roll(odd)))
                highs.append(jnp.where(is_first, half_roll(even), odd))
            for part, pieces in enumerate((lows, highs)):
                rows = jnp.concatenate(pieces, axis=1)
                term = add_up(spread_rows(rows, mask), onehot)
                totals[part] = term if g == 0 else totals[part] + term
        for part in range(2):
            for high in range(2):
                start = high * 512 + part * 256
                acc[start : start + 256, :] += totals[part][:, high * 128 : high * 128 + 128]
        return carry

    lax.fori_loop(0, 16 // BACK, scatter, 0)


def param_slopes(table, group_in, blocks, acc, outs, out, sems):
    def compute(q, carry):
        base = q * 512
        row0 = lax.rem(q, 4) * 8
        high = lax.div(q, 4)

        def load(p):
            return blocks[pl.ds(base + p, 8, stride=64), :]

        def save(p, value):
            outs[pl.ds(base + p, 8, stride=64), :] = value

        def grad_of(f):
            return acc[pl.ds(pl.multiple_of(high * 512 + f * 32 + row0, 8), 8), :]

        group = group_in[pl.ds(pl.multiple_of(row0, 8), 8), pl.ds(pl.multiple_of(high * 128, 128), 128)]
        anchors = group_anchors(table, group)
        mean = [load(0), load(1), load(2)]
        totals = [grad_of(0), grad_of(1), grad_of(2)]
        _, pull = jax.vjp(lambda *g: shape_values(list(g)), *[load(3 + n) for n in range(7)])
        for n, value in enumerate(pull([grad_of(3 + n) for n in range(6)])):
            save(3 + n, value)
        save(10, grad_of(9) / (1.0 + jnp.exp(load(10))))
        colour = [[grad_of(10 + 3 * w + c) for c in range(3)] for w in range(2)]
        bases, pulls = [], []
        for w in range(2):
            anchor = anchors[w]
            basis, pull = jax.vjp(lambda *m: colour_basis(list(m), anchor)[1:], *mean)
            bases.append(basis)
            pulls.append(pull)
        slopes = [[None] * 15, [None] * 15]
        for c in range(3):
            save(11 + 16 * c, HARMONIC_ZERO * (colour[0][c] + colour[1][c]))
            for k in range(15):
                coef = load(12 + 16 * c + k)
                save(12 + 16 * c + k, bases[0][k] * colour[0][c] + bases[1][k] * colour[1][c])
                for w in range(2):
                    term = coef * colour[w][c]
                    slopes[w][k] = term if c == 0 else slopes[w][k] + term
        for w in range(2):
            totals = [a + b for a, b in zip(totals, pulls[w](slopes[w]))]
        for n in range(3):
            save(n, totals[n])
        for n in range(8):
            result_copy(outs, out, q * 8 + n, sems).start()
        return carry

    lax.fori_loop(0, 8, compute, 0)

    def finish(row, carry):
        result_copy(outs, out, row, sems).wait()
        return carry

    lax.fori_loop(0, 64, finish, 0)


def splat_kernel(
    cam_v, cam_s, params, slist, counts, lens, lists, true, out,
    blocks, outs, group, chosen, hot, stab, pos, val, tab_s, stack_s,
    send, recv, tab_d, stack_0, stack_1, feats, alpha, keep, pair, left, right, frame,
    shown, truth, mean, map_m, map_q, map_x, rows_out, acc_d, pack, back, acc_s,
    in_sems, out_sems, send_sems, early_sems, late_sems, shown_sems, truth_sems,
):
    me = own_number()
    tile_row = lax.axis_index("tile")
    barrier = pltpu.get_barrier_semaphore()
    loads = param_copies(params, blocks, in_sems)
    for load in loads:
        load.start()
    own = own_cameras(cam_s, lax.axis_index("view"))
    table = all_anchors(cam_v)
    choose_slots(barrier, me, slist, counts, group, chosen, hot, stab, pos, val)
    true_rows(true, truth, frame)
    for load in loads:
        load.wait()
    source_tables(table, group, blocks, tab_s, stack_s)
    pl.semaphore_wait(barrier, 127)
    send_halo(truth, tile_row, truth_sems)
    send_slots(me, chosen, hot, stack_s, send, recv, send_sems)
    take_halo(truth, tile_row, truth_sems)
    true_means(truth, mean, 0, FIRST_MEANS)
    finish_blocks(send, recv, me, send_sems)
    stacks = [stack_0, stack_1]
    band_tables(own, recv, tab_d, stacks)
    list_features(lists, lens, stacks, feats)
    render_tiles(tile_row, feats, alpha, keep, pair, left, right)
    shown_rows(left, right, frame, shown)
    send_halo(shown, tile_row, shown_sems)
    true_means(truth, mean, FIRST_MEANS, 26 - FIRST_MEANS)
    take_halo(shown, tile_row, shown_sems)
    loss_slopes(tile_row, shown, truth, mean, map_m, map_q, map_x, frame)
    tile_slopes(frame, left, right)
    feature_slopes(tile_row, feats, alpha, keep, pair, left, right, rows_out)
    acc_s[...] = jnp.zeros((1024, 128), F32)
    early = first_part(me)
    scatter_features(lists, rows_out, acc_d, early)
    return_slots(me, own, recv, acc_d, pack, back, early_sems, early)
    scatter_features(lists, rows_out, acc_d, 1 - early)
    return_slots(me, own, recv, acc_d, pack, back, late_sems, 1 - early)
    start = pl.multiple_of(me * 8, 8)
    back[pl.ds(start, 8), :] = pack[pl.ds(start, 8), :]
    finish_part(pack, back, me, early_sems, True)
    scatter_slots(chosen, hot, back, acc_s, own_part(me))
    finish_part(pack, back, me, late_sems, False)
    scatter_slots(chosen, hot, back, acc_s, 1 - own_part(me))
    param_slopes(table, group, blocks, acc_s, outs, out, out_sems)


def struct(shape, dtype=F32):
    return jax.ShapeDtypeStruct(shape, dtype)


VM = pl.BlockSpec(memory_space=pltpu.VMEM)
SM = pl.BlockSpec(memory_space=pltpu.SMEM)
ANY = pl.BlockSpec(memory_space=pl.ANY)


def vm(*shape, dtype=F32):
    return pltpu.VMEM(shape, dtype)


def shards(params, send_list, send_counts, camera, ground_truth, tile_lists, list_lengths):
    lists = tile_lists.reshape(64, 128)
    true = ground_truth.reshape(96, 512)
    dma = pltpu.SemaphoreType.DMA
    return pl.pallas_call(
        splat_kernel,
        out_shape=struct((59, 8192)),
        in_specs=[VM, SM, ANY, VM, VM, SM, VM, VM],
        out_specs=ANY,
        scratch_shapes=[
            vm(4096, 128),
            vm(4096, 128),
            vm(32, 256),
            vm(32, 256, dtype=I32),
            vm(8192, 256, dtype=BF16),
            vm(64, 256),
            vm(32, 256, dtype=I32),
            vm(32, 256),
            vm(512, 256),
            vm(1312, 256, dtype=BF16),
            vm(1024, 128),
            vm(1024, 128),
            vm(576, 256),
            vm(736, 256, dtype=BF16),
            vm(736, 256, dtype=BF16),
            vm(1024, 128),
            vm(16384, 128),
            vm(16384, 128),
            vm(GROUP * 256, 256, dtype=BF16),
            vm(512, 128),
            vm(512, 128),
            vm(512, 128),
            vm(288, 512),
            vm(288, 512),
            vm(26, 8, 512),
            vm(26, 8, 512),
            vm(26, 8, 512),
            vm(26, 8, 512),
            vm(1024, 128),
            vm(576, 128),
            vm(1024, 128),
            vm(1024, 128),
            vm(1024, 128),
            dma((64,)),
            dma((64,)),
            dma((2,)),
            dma((2,)),
            dma((2,)),
            dma((4,)),
            dma((4,)),
        ],
        compiler_params=pltpu.CompilerParams(
            vmem_limit_bytes=VMEM_BYTES, collective_id=0, has_side_effects=True
        ),
        name="splat_gradient",
    )(camera, camera, params, send_list, send_counts, list_lengths, lists, true)


def solution(mesh):
    in_specs = (
        P(None, ("view", "tile")),
        P(("view", "tile"), None),
        P(("view", "tile"), None),
        P(),
        P("view", None, "tile", None),
        P("view", "tile", None, None),
        P("view", "tile", None),
    )
    out_specs = P(None, ("view", "tile"))
    return jax.shard_map(shards, mesh=mesh, in_specs=in_specs, out_specs=out_specs, check_vma=False)
```

```python
import jax
import jax.numpy as jnp
import numpy as np
from jax import lax
from jax.experimental import pallas as pl
from jax.experimental.pallas import tpu as pltpu
from jax.sharding import PartitionSpec as P

F32 = jnp.float32
BF16 = jnp.bfloat16
I32 = jnp.int32

TILE = 16
GROUP = 8
FOCAL = 1000.0
LOW_PASS = 0.3
SSIM_SHARE = 0.2
SMOOTH_EPS = 1e-06
SSIM_ONE = 0.0001
SSIM_TWO = 0.0009
LOG2E = 1.4426950408889634
HARMONIC_ZERO = 0.28209479177387814
HARMONIC_ONE = 0.4886025119029199
HARMONIC_TWO = (
    1.0925484305920792,
    -1.0925484305920792,
    0.31539156525252005,
    -1.0925484305920792,
    0.5462742152960396,
)
HARMONIC_THREE = (
    -0.5900435899266435,
    2.890611442640554,
    -0.4570457994644658,
    0.3731763325901154,
    -0.4570457994644658,
    1.445305721320277,
    -0.5900435899266435,
)
VMEM_BYTES = 56 * 1024 * 1024
CHOOSE = 16
GATHER = 8
LOOKUP = 8
SCAT = 16
BACK = 16
MESH = pl.DeviceIdType.MESH
FIRST_MEANS = 10
NT = (((1,), (1,)), ((), ()))
NN = (((1,), (0,)), ((), ()))
TN = (((0,), (0,)), ((), ()))


def window_taps():
    offsets_np = np.arange(11) - 5.0
    weights = np.exp(-offsets_np * offsets_np / 4.5)
    weights = weights / weights.sum()
    return [float(weight) for weight in weights]


TAPS = window_taps()


def matrix_product(left_side, right_side):
    return [
        [
            left_side[row_idx][0] * right_side[0][col_idx]
            + left_side[row_idx][1] * right_side[1][col_idx]
            + left_side[row_idx][2] * right_side[2][col_idx]
            for col_idx in range(3)
        ]
        for row_idx in range(3)
    ]


def rotation(angles):
    cos_a, sin_a = (jnp.cos(angles[0]), jnp.sin(angles[0]))
    cos_b, sin_b = (jnp.cos(angles[1]), jnp.sin(angles[1]))
    cos_c, sin_c = (jnp.cos(angles[2]), jnp.sin(angles[2]))
    zero, one = jnp.zeros_like(cos_a), jnp.ones_like(cos_a)
    about_x = [[one, zero, zero], [zero, cos_a, -sin_a], [zero, sin_a, cos_a]]
    about_y = [[cos_b, zero, sin_b], [zero, one, zero], [-sin_b, zero, cos_b]]
    about_z = [[cos_c, -sin_c, zero], [sin_c, cos_c, zero], [zero, zero, one]]
    return matrix_product(about_z, matrix_product(about_y, about_x))


def camera_values(numbers):
    rot = rotation(numbers[0:3])
    move = list(numbers[3:6])
    anchor = [
        -(rot[0][c] * move[0] + rot[1][c] * move[1] + rot[2][c] * move[2]) for c in range(3)
    ]
    return rot[0] + rot[1] + rot[2] + move, anchor


def own_cameras(cam, group):
    return [
        camera_values([jnp.full((8, 128), cam[2 * group + w, n], F32) for n in range(6)])[0]
        for w in range(2)
    ]


def all_anchors(cam):
    numbers = [jnp.broadcast_to(cam[:, n : n + 1], (8, 128)) for n in range(6)]
    anchor = camera_values(numbers)[1]
    return [[jnp.broadcast_to(a[n : n + 1, :], (8, 128)) for a in anchor] for n in range(8)]


def own_number():
    return lax.axis_index("view") * 32 + lax.axis_index("tile")


def device_of(number):
    return (lax.div(number, 32), lax.rem(number, 32))


def greet(barrier, me, o):
    pl.semaphore_signal(
        barrier, inc=1, device_id=device_of(lax.rem(me + o, 128)), device_id_type=MESH
    )


def block_copy(pack, recv, me, number, sems):
    return pltpu.make_async_remote_copy(
        src_ref=pack.at[pl.ds(pl.multiple_of(number * 8, 8), 8)],
        dst_ref=recv.at[pl.ds(pl.multiple_of(me * 8, 8), 8)],
        send_sem=sems.at[0],
        recv_sem=sems.at[1],
        device_id=device_of(number),
        device_id_type=MESH,
    )


def push_blocks(pack, recv, me, first, count, sems):
    def push(n, carry):
        number = first + n

        @pl.when(number != me)
        def _():
            block_copy(pack, recv, me, number, sems).start()

        return carry

    lax.fori_loop(0, count, push, 0)


def finish_blocks(pack, recv, me, sems):
    start = pl.multiple_of(me * 8, 8)
    recv[pl.ds(start, 8), :] = pack[pl.ds(start, 8), :]
    whole = pltpu.make_async_remote_copy(
        src_ref=pack.at[pl.ds(0, 1016)],
        dst_ref=recv.at[pl.ds(0, 1016)],
        send_sem=sems.at[0],
        recv_sem=sems.at[1],
        device_id=device_of(lax.rem(me + 1, 128)),
        device_id_type=MESH,
    )
    whole.wait()


def harmonics(dir_x, dir_y, dir_z):
    sq_x, sq_y, sq_z = (dir_x * dir_x, dir_y * dir_y, dir_z * dir_z)
    prod_xy, prod_yz, prod_xz = (dir_x * dir_y, dir_y * dir_z, dir_x * dir_z)
    return [
        None,
        -HARMONIC_ONE * dir_y,
        HARMONIC_ONE * dir_z,
        -HARMONIC_ONE * dir_x,
        HARMONIC_TWO[0] * prod_xy,
        HARMONIC_TWO[1] * prod_yz,
        HARMONIC_TWO[2] * (2.0 * sq_z - sq_x - sq_y),
        HARMONIC_TWO[3] * prod_xz,
        HARMONIC_TWO[4] * (sq_x - sq_y),
        HARMONIC_THREE[0] * dir_y * (3.0 * sq_x - sq_y),
        HARMONIC_THREE[1] * prod_xy * dir_z,
        HARMONIC_THREE[2] * dir_y * (4.0 * sq_z - sq_x - sq_y),
        HARMONIC_THREE[3] * dir_z * (2.0 * sq_z - 3.0 * sq_x - 3.0 * sq_y),
        HARMONIC_THREE[4] * dir_x * (4.0 * sq_z - sq_x - sq_y),
        HARMONIC_THREE[5] * dir_z * (sq_x - sq_y),
        HARMONIC_THREE[6] * dir_x * (sq_x - 3.0 * sq_y),
    ]


def shape_values(gauss):
    scales = [jnp.exp(gauss[axis]) for axis in range(3)]
    norm_inv = 1.0 / jnp.sqrt(
        gauss[3] * gauss[3] + gauss[4] * gauss[4] + gauss[5] * gauss[5] + gauss[6] * gauss[6]
    )
    quat_w, quat_x, quat_y, quat_z = [gauss[3 + n] * norm_inv for n in range(4)]
    quat_rot = [
        [
            1.0 - 2.0 * (quat_y * quat_y + quat_z * quat_z),
            2.0 * (quat_x * quat_y - quat_w * quat_z),
            2.0 * (quat_x * quat_z + quat_w * quat_y),
        ],
        [
            2.0 * (quat_x * quat_y + quat_w * quat_z),
            1.0 - 2.0 * (quat_x * quat_x + quat_z * quat_z),
            2.0 * (quat_y * quat_z - quat_w * quat_x),
        ],
        [
            2.0 * (quat_x * quat_z - quat_w * quat_y),
            2.0 * (quat_y * quat_z + quat_w * quat_x),
            1.0 - 2.0 * (quat_x * quat_x + quat_y * quat_y),
        ],
    ]
    spread = [[quat_rot[r][c] * scales[c] for c in range(3)] for r in range(3)]

    def dot_rows(one, two):
        return (
            spread[one][0] * spread[two][0]
            + spread[one][1] * spread[two][1]
            + spread[one][2] * spread[two][2]
        )

    return [
        dot_rows(0, 0),
        dot_rows(0, 1),
        dot_rows(0, 2),
        dot_rows(1, 1),
        dot_rows(1, 2),
        dot_rows(2, 2),
    ]


def colour_basis(mean, anchor):
    ray_x, ray_y, ray_z = (mean[0] - anchor[0], mean[1] - anchor[1], mean[2] - anchor[2])
    len_inv = 1.0 / jnp.sqrt(ray_x * ray_x + ray_y * ray_y + ray_z * ray_z)
    return harmonics(ray_x * len_inv, ray_y * len_inv, ray_z * len_inv)


def image_values(gauss, cam):
    point = [
        cam[3 * r] * gauss[0] + cam[3 * r + 1] * gauss[1] + cam[3 * r + 2] * gauss[2] + cam[9 + r]
        for r in range(3)
    ]
    inv_depth = 1.0 / point[2]
    jac = FOCAL * inv_depth
    jac_xz = -FOCAL * point[0] * inv_depth * inv_depth
    jac_yz = -FOCAL * point[1] * inv_depth * inv_depth
    row_x = [jac * cam[c] + jac_xz * cam[6 + c] for c in range(3)]
    row_y = [jac * cam[3 + c] + jac_yz * cam[6 + c] for c in range(3)]
    s_xx, s_xy, s_xz, s_yy, s_yz, s_zz = gauss[3:9]
    by_x = [
        s_xx * row_x[0] + s_xy * row_x[1] + s_xz * row_x[2],
        s_xy * row_x[0] + s_yy * row_x[1] + s_yz * row_x[2],
        s_xz * row_x[0] + s_yz * row_x[1] + s_zz * row_x[2],
    ]
    by_y = [
        s_xx * row_y[0] + s_xy * row_y[1] + s_xz * row_y[2],
        s_xy * row_y[0] + s_yy * row_y[1] + s_yz * row_y[2],
        s_xz * row_y[0] + s_yz * row_y[1] + s_zz * row_y[2],
    ]
    cov_xx = row_x[0] * by_x[0] + row_x[1] * by_x[1] + row_x[2] * by_x[2] + LOW_PASS
    cov_xy = row_y[0] * by_x[0] + row_y[1] * by_x[1] + row_y[2] * by_x[2]
    cov_yy = row_y[0] * by_y[0] + row_y[1] * by_y[1] + row_y[2] * by_y[2] + LOW_PASS
    det_inv = 1.0 / (cov_xx * cov_yy - cov_xy * cov_xy)
    return [
        FOCAL * point[0] * inv_depth + 256.0,
        FOCAL * point[1] * inv_depth + 256.0,
        cov_yy * det_inv,
        -cov_xy * det_inv,
        cov_xx * det_inv,
    ]


def split3(value):
    one = value.astype(BF16)
    rest = value - one.astype(F32)
    two = rest.astype(BF16)
    three = (rest - two.astype(F32)).astype(BF16)
    return one, two, three


def split2(value):
    one = value.astype(BF16)
    return one, (value - one.astype(F32)).astype(BF16)


def dot(left, right, dims):
    return lax.dot_general(left, right, dims, preferred_element_type=F32)


def iota(shape, dim):
    return lax.broadcasted_iota(I32, shape, dim)


def high_onehot(idx):
    high = ((idx >> 12) << 7) | (idx & 127)
    return jnp.where(iota((256, idx.shape[1]), 0) == high, 1.0, 0.0).astype(BF16)


def low_mask(idx):
    return iota((32, idx.shape[1]), 0) == ((idx >> 7) & 31)


def stack_tables(tab, stack, rows, exact):
    one, two, three = split3(tab)
    stack[0 : rows * 32, :] = one
    stack[rows * 32 : rows * 64, :] = two
    stack[rows * 64 : rows * 64 + exact * 32, :] = three[0 : exact * 32]


def pick(stack, rows, exact, onehot, mask):
    found = dot(stack, onehot, NN)
    total = found[0 : rows * 32] + found[rows * 32 : rows * 64]
    fine = total[0 : exact * 32] + found[rows * 64 : rows * 64 + exact * 32]

    def low_sum(part, count):
        picked = jnp.where(mask[None], part.reshape(count, 32, mask.shape[1]), 0.0)
        return jnp.sum(picked, axis=1)

    return jnp.concatenate(
        [low_sum(fine, exact), low_sum(total[exact * 32 :], rows - exact)], axis=0
    )


def spread_rows(rows, mask):
    count = rows.shape[0]
    return jnp.where(mask[None], rows[:, None, :], 0.0).reshape(count * mask.shape[0], rows.shape[1])


def add_up(left, onehot):
    size = left.shape[0]
    found = dot(jnp.concatenate(split2(left), axis=0), onehot, NT)
    return found[0:size] + found[size:]


def half_roll(value):
    return pltpu.roll(value, 64, 1)


def first_half():
    return iota((8, 128), 1) < 64


def param_copies(params, blocks, sems):
    return [
        pltpu.make_async_copy(
            params.at[:, pl.ds(row * 128, 128)], blocks.at[pl.ds(row * 64, 59)], sems.at[row]
        )
        for row in range(64)
    ]


def result_copy(outs, out, row, sems):
    return pltpu.make_async_copy(
        outs.at[pl.ds(pl.multiple_of(row * 64, 64), 59)],
        out.at[:, pl.ds(pl.multiple_of(row * 128, 128), 128)],
        sems.at[row],
    )


def group_anchors(table, group):
    anchors = []
    for slot in range(2):
        triple = []
        for c in range(3):
            value = table[slot][c]
            for number in range(1, 4):
                value = jnp.where(group > number + 0.5, table[2 * number + slot][c], value)
            triple.append(value)
        anchors.append(triple)
    return anchors


def choose_slots(barrier, me, slist, counts, group_out, chosen, hot, stab, pos, val):
    def greet_next(o, carry):
        greet(barrier, me, o)
        return carry

    lax.fori_loop(1, 128, greet_next, 0)
    cnt = counts[...].astype(F32)
    lanes = iota((32, 128), 1)
    first = iota((32, 128), 0) * 4
    slot_lane = iota((32, 256), 1)
    off = jnp.zeros((32, 256), F32)
    own = jnp.zeros((32, 256), F32)
    for j in range(4):
        off_j = jnp.sum(jnp.where(lanes < first + j, cnt, 0.0), axis=1, keepdims=True)
        own_j = jnp.sum(jnp.where(lanes == first + j, cnt, 0.0), axis=1, keepdims=True)
        here = (slot_lane >> 6) == j
        off = jnp.where(here, off_j, off)
        own = jnp.where(here, own_j, own)
    place = (slot_lane & 63).astype(F32)
    pos[...] = jnp.minimum(off + place, 8191.0).astype(I32)
    group = (iota((32, 256), 0) >> 3).astype(F32) + 1.0
    val[...] = jnp.where(place < own, group, 0.0)
    for row in range(64):
        piece = slist[:, row * 128 : (row + 1) * 128]
        half = slice((row // 32) * 128, (row // 32) * 128 + 128)
        stab[row % 32 : row % 32 + 1, half] = (piece >> 6).astype(F32)
        stab[32 + row % 32 : 33 + row % 32, half] = (piece & 63).astype(F32)
    group_out[...] = jnp.zeros((32, 256), F32)
    stab_b = stab[...].astype(BF16)

    def choose(step, carry):
        rows = [step * CHOOSE + g for g in range(CHOOSE)]
        places = [pos[pl.ds(p, 1), :] for p in rows]
        found = [dot(stab_b, high_onehot(idx), NN) for idx in places]
        total = None
        for g, p in enumerate(rows):
            both = found[g][0:32] * 64.0 + found[g][32:64]
            ids = jnp.sum(jnp.where(low_mask(places[g]), both, 0.0), axis=0, keepdims=True).astype(I32)
            chosen[pl.ds(p, 1), :] = ids
            onehot = high_onehot(ids)
            hot[pl.ds(pl.multiple_of(p * 256, 256), 256), :] = onehot
            left = jnp.where(low_mask(ids), val[pl.ds(p, 1), :], 0.0).astype(BF16)
            part = dot(left, onehot, NT)
            total = part if g == 0 else total + part
        group_out[...] += total
        return carry

    lax.fori_loop(0, 32 // CHOOSE, choose, 0)


def source_tables(table, group_out, blocks, tab, stack):
    for high in range(2):
        lane_part = slice(high * 128, high * 128 + 128)

        def compute(low, carry):
            base = (high * 4 + low) * 512
            row0 = pl.multiple_of(low * 8, 8)

            def load(p):
                return blocks[pl.ds(base + p, 8, stride=64), :]

            anchors = group_anchors(table, group_out[pl.ds(row0, 8), lane_part])
            mean = [load(0), load(1), load(2)]
            values = mean + shape_values([load(3 + n) for n in range(7)])
            values += [0.99 / (1.0 + jnp.exp(-load(10)))]
            bases = [colour_basis(mean, anchor) for anchor in anchors]
            sums = [[None] * 3, [None] * 3]
            for c in range(3):
                flat = 0.5 + HARMONIC_ZERO * load(11 + 16 * c)
                sums[0][c] = flat
                sums[1][c] = flat
                for k in range(1, 16):
                    coef = load(11 + 16 * c + k)
                    sums[0][c] = sums[0][c] + bases[0][k] * coef
                    sums[1][c] = sums[1][c] + bases[1][k] * coef
            values += sums[0] + sums[1]
            for f in range(16):
                tab[pl.ds(f * 32 + row0, 8), lane_part] = values[f]
            return carry

        lax.fori_loop(0, 4, compute, 0)
    stack_tables(tab[...], stack, 16, 9)


def send_slots(me, chosen, hot, stack, send, recv, sems):
    is_first = first_half()
    shift = lax.div(me, 4) + 1

    def group_at(step, g):
        return lax.rem(step * GATHER + g + shift, 32)

    def gather(step, carry):
        for g in range(GATHER):
            p = group_at(step, g)
            onehot = hot[pl.ds(pl.multiple_of(p * 256, 256), 256), :]
            rows = pick(stack[...], 16, 9, onehot, low_mask(chosen[pl.ds(p, 1), :]))
            for b in range(2):
                one = rows[0:8, b * 128 : b * 128 + 128]
                two = rows[8:16, b * 128 : b * 128 + 128]
                start = pl.multiple_of(p * 32 + b * 16, 16)
                send[pl.ds(start, 8), :] = jnp.where(is_first, one, half_roll(two))
                send[pl.ds(start + 8, 8), :] = jnp.where(is_first, half_roll(one), two)
        for g in range(GATHER):
            push_blocks(send, recv, me, group_at(step, g) * 4, 4, sems)
        return carry

    lax.fori_loop(0, 32 // GATHER, gather, 0)


def unpack_slots(recv, q):
    is_first = first_half()
    low, high = [], []
    for f in range(8):
        even = recv[pl.ds(q * 128 + f, 8, stride=16), :]
        odd = recv[pl.ds(q * 128 + 8 + f, 8, stride=16), :]
        low.append(jnp.where(is_first, even, half_roll(odd)))
        high.append(jnp.where(is_first, half_roll(even), odd))
    return low + high


def block_transpose(value):
    turn = (iota((8, 128), 0) - (iota((8, 128), 1) >> 4)) & 7
    result = value
    for d in range(1, 8):
        moved = pltpu.roll(pltpu.roll(value, d, 0), 128 - 16 * d, 1)
        result = jnp.where(turn == d, moved, result)
    return result


def triangle(keep):
    return jnp.where(keep, 1.0, 0.0).astype(BF16)


def pixel_rows(feat, column, tile_row):
    def row(f):
        return jnp.broadcast_to(feat[f : f + 1, :], (16, 128))

    shift = iota((16, 128), 0).astype(F32) + (column * 16).astype(F32)
    delta_x = row(0) - shift
    square = (-0.5 * LOG2E) * row(2) * delta_x * delta_x
    cross = -LOG2E * row(3) * delta_x
    quad = (-0.5 * LOG2E) * row(4)
    delta_v = row(1) - (tile_row * 16).astype(F32)
    return delta_x, delta_v, square, cross, quad, row(5)


def tile_weights(feats, columns, bases, tile_row, tri, alpha, pair):
    for g, feat in enumerate(feats):
        delta_x, delta_v, square, cross, quad, opacity = pixel_rows(feat, columns[g], tile_row)
        for j in range(16):
            delta_y = delta_v - float(j)
            value = opacity * jnp.exp2(square + delta_y * (cross + quad * delta_y))
            rows = slice(g * 256 + j * 16, g * 256 + j * 16 + 16)
            alpha[pl.ds(pl.multiple_of(bases[g] + j * 16, 16), 16), :] = value
            one, two = split2(jnp.log(1.0 - value))
            pair[rows, 0:128] = one
            pair[rows, 128:256] = two
    weights = []
    for g in range(len(feats)):
        rows = slice(g * 256, g * 256 + 256)
        weights.append(jnp.exp(dot(pair[rows, :], tri, NN)) * alpha[pl.ds(bases[g], 256), :])
    return weights


def stack_splits(value, order):
    one, two, three = split3(value)
    parts = [one.astype(F32), two.astype(F32), three.astype(F32)]
    return jnp.concatenate([parts[n] for n in order], axis=0).astype(BF16)


def greet_bands(tile_row):
    barrier = pltpu.get_barrier_semaphore()
    for step in (1, 31):
        other = lax.rem(tile_row + step, 32)
        pl.semaphore_signal(barrier, inc=1, device_id={"tile": other}, device_id_type=MESH)
    pl.semaphore_wait(barrier, 2)


def halo_copies(rows, tile_row, sems):
    def copy(source, target, step, n):
        return pltpu.make_async_remote_copy(
            src_ref=rows.at[pl.ds(source, 80)],
            dst_ref=rows.at[pl.ds(target, 80)],
            send_sem=sems.at[2 * n],
            recv_sem=sems.at[2 * n + 1],
            device_id={"tile": lax.rem(tile_row + step, 32)},
            device_id_type=MESH,
        )

    return copy(128, 0, 1, 0), copy(80, 208, 31, 1)


def send_halo(rows, tile_row, sems):
    down, up = halo_copies(rows, tile_row, sems)

    @pl.when(tile_row < 31)
    def _():
        down.start()

    @pl.when(tile_row > 0)
    def _():
        up.start()


def take_halo(rows, tile_row, sems):
    down, up = halo_copies(rows, tile_row, sems)

    @pl.when(tile_row < 31)
    def _():
        down.wait_send()
        up.wait_recv()

    @pl.when(tile_row > 0)
    def _():
        up.wait_send()
        down.wait_recv()

    @pl.when(tile_row == 0)
    def _():
        rows[0:80, :] = jnp.zeros((80, 512), F32)

    @pl.when(tile_row == 31)
    def _():
        rows[208:288, :] = jnp.zeros((80, 512), F32)


def true_rows(true, truth, frame):
    frame[...] = jnp.zeros((512, 128), F32)
    for n in range(6):
        for b in range(4):
            for half in range(2):
                rows = true[n * 16 + half * 8 : n * 16 + half * 8 + 8, b * 128 : b * 128 + 128]
                frame[pl.ds(b * 128 + half * 64 + n, 8, stride=8), :] = rows
    for b in range(4):
        truth[80:208, b * 128 : b * 128 + 128] = frame[b * 128 : b * 128 + 128, :]


def band_tables(own, recv, tab, stacks):
    for high in range(2):
        lane_part = slice(high * 128, high * 128 + 128)

        def compute(low, carry):
            row0 = pl.multiple_of(low * 8, 8)
            values = unpack_slots(recv, high * 4 + low)
            for w in range(2):
                seen = image_values(values[0:9], own[w])
                seen = seen + [values[9]] + values[10 + 3 * w : 13 + 3 * w]
                for f in range(9):
                    tab[pl.ds((w * 9 + f) * 32 + row0, 8), lane_part] = seen[f]
            return carry

        lax.fori_loop(0, 4, compute, 0)
    for w in range(2):
        stack_tables(tab[w * 288 : w * 288 + 288, :], stacks[w], 9, 5)


def list_features(lists, lens, tables, feats):
    lane = iota((1, 256), 1)
    for w in range(2):

        def look_up(step, carry):
            for g in range(LOOKUP):
                tile = w * 32 + (step * LOOKUP + g) * 2
                idx = jnp.concatenate([lists[pl.ds(tile, 1), :], lists[pl.ds(tile + 1, 1), :]], axis=1)
                rows = pick(tables[w][...], 9, 5, high_onehot(idx), low_mask(idx))
                length = jnp.where(lane < 128, lens[w, 0, tile - w * 32], lens[w, 0, tile - w * 32 + 1])
                rows = jnp.where((lane & 127) < length, rows, 0.0)
                start = pl.multiple_of(tile * 16, 32)
                for b in range(2):
                    part = rows[:, b * 128 : b * 128 + 128]
                    feats[pl.ds(start + b * 16, 6), :] = part[0:6]
                    feats[pl.ds(start + b * 16 + 6, 2), :] = jnp.zeros((2, 128), F32)
                    feats[pl.ds(start + b * 16 + 8, 3), :] = part[6:9]
                    feats[pl.ds(start + b * 16 + 11, 5), :] = jnp.zeros((5, 128), F32)
            return carry

        lax.fori_loop(0, 16 // LOOKUP, look_up, 0)


def render_tiles(tile_row, feats, alpha, keep, pair, left, right):
    tri = triangle((iota((256, 128), 0) & 127) < iota((256, 128), 1))

    def composite(step, carry):
        tiles = [step * GROUP + g for g in range(GROUP)]
        given = [feats[pl.ds(pl.multiple_of(tile * 16, 16), 16), :] for tile in tiles]
        bases = [pl.multiple_of(tile * 256, 256) for tile in tiles]
        weights = tile_weights(
            given, [tile & 31 for tile in tiles], bases, tile_row, tri, alpha, pair
        )
        for g, tile in enumerate(tiles):
            keep[pl.ds(bases[g], 256), :] = weights[g]
            one, two = split2(weights[g])
            colours = stack_splits(given[g][8:16], (0, 1, 2))
            big = dot(colours, one, NT)
            small = dot(colours, two, NT)
            result = (big[0:8] + big[8:16]) + (small[0:8] + small[8:16]) + big[16:24]
            start = pl.multiple_of(tile * 8, 8)
            left[pl.ds(start, 8), :] = result[:, 0:128]
            right[pl.ds(start, 8), :] = result[:, 128:256]
        return carry

    lax.fori_loop(0, 64 // GROUP, composite, 0)


def shown_rows(left, right, frame, shown):
    for w in range(2):
        for c in range(3):
            for b in range(4):
                for half, source in enumerate((left, right)):
                    block = source[pl.ds((w * 32 + b * 8) * 8 + c, 8, stride=8), :]
                    start = b * 128 + half * 64 + w * 3 + c
                    frame[pl.ds(start, 8, stride=8), :] = block_transpose(block)
    for b in range(4):
        shown[80:208, b * 128 : b * 128 + 128] = frame[b * 128 : b * 128 + 128, :]


def blur_lanes(value):
    padded = jnp.concatenate([value, jnp.zeros((8, 128), F32)], axis=1)
    moved = [pltpu.roll(padded, 639, 1), padded, pltpu.roll(padded, 1, 1), pltpu.roll(padded, 2, 1)]

    def part(far):
        total = None
        for near in range(-1, 3):
            tap = 4 * far + near
            if -5 <= tap <= 5:
                term = TAPS[5 + tap] * moved[near + 1]
                total = term if total is None else total + term
        return total

    total = part(0) + pltpu.roll(part(1), 4, 1) + pltpu.roll(part(-1), 636, 1)
    return total[:, 0:512]


def blur_rows(rows):
    total = TAPS[5] * rows[5]
    for k in range(1, 6):
        total = total + TAPS[5 + k] * (rows[5 - k] + rows[5 + k])
    return total


def at(y):
    return pl.ds(pl.multiple_of(y * 8, 8), 8)


def true_means(truth, mean, first, count):
    def one_row(n, carry):
        y = first + n
        mean[y] = blur_lanes(blur_rows([truth[at(y + k), :] for k in range(11)]))
        return carry

    lax.fori_loop(0, count, one_row, 0, unroll=count // 2)


def loss_slopes(tile_row, shown, truth, mean, map_m, map_q, map_x, frame):
    def similarity(y, carry):
        ones = [shown[at(y + k), :] for k in range(11)]
        twos = [truth[at(y + k), :] for k in range(11)]
        mean_one = blur_lanes(blur_rows(ones))
        mean_two = mean[y]
        squares = blur_lanes(blur_rows([a * a + b * b for a, b in zip(ones, twos)]))
        cross = blur_lanes(blur_rows([a * b for a, b in zip(ones, twos)]))
        num_one = 2.0 * mean_one * mean_two + SSIM_ONE
        num_two = 2.0 * (cross - mean_one * mean_two) + SSIM_TWO
        power = mean_one * mean_one + mean_two * mean_two
        den_one_inv = 1.0 / (power + SSIM_ONE)
        den_two_inv = 1.0 / (squares - power + SSIM_TWO)
        both_inv = den_one_inv * den_two_inv
        value = num_one * num_two * both_inv
        row = tile_row * 16 - 5 + y
        scale = jnp.where((row >= 0) & (row < 512), -SSIM_SHARE, 0.0)
        by_mean = 2.0 * mean_two * (num_two - num_one) * both_inv + 2.0 * mean_one * value * (
            den_two_inv - den_one_inv
        )
        map_m[y] = scale * by_mean
        map_q[y] = (-2.0 * scale) * value * den_two_inv
        map_x[y] = (2.0 * scale) * num_one * both_inv
        return carry

    lax.fori_loop(0, 26, similarity, 0, unroll=2)

    def image_grad(y, carry):
        by_mean = blur_lanes(blur_rows([map_m[y + k] for k in range(11)]))
        by_sq = blur_lanes(blur_rows([map_q[y + k] for k in range(11)]))
        by_cross = blur_lanes(blur_rows([map_x[y + k] for k in range(11)]))
        one = shown[at(y + 10), :]
        two = truth[at(y + 10), :]
        gap = one - two
        result = by_mean + one * by_sq + two * by_cross
        result = result + (1.0 - SSIM_SHARE) * gap / jnp.sqrt(gap * gap + SMOOTH_EPS)
        start = pl.multiple_of(y * 8, 8)
        for b in range(4):
            frame[pl.ds(b * 128 + start, 8), :] = result[:, b * 128 : b * 128 + 128]
        return carry

    lax.fori_loop(0, 16, image_grad, 0, unroll=2)


def tile_slopes(frame, left, right):
    left[...] = jnp.zeros((512, 128), F32)
    right[...] = jnp.zeros((512, 128), F32)
    for w in range(2):
        for c in range(3):
            for b in range(4):
                for half, target in enumerate((left, right)):
                    start = b * 128 + half * 64 + w * 3 + c
                    block = block_transpose(frame[pl.ds(start, 8, stride=8), :])
                    target[pl.ds((w * 32 + b * 8) * 8 + c, 8, stride=8), :] = block


def feature_slopes(tile_row, feats, alpha, keep, pair, left, right, rows_out):
    suf = triangle((iota((256, 128), 0) & 127) > iota((256, 128), 1))

    def total(terms):
        return jnp.sum(terms, axis=0, keepdims=True)

    def composite(step, carry):
        tiles = [step * GROUP + g for g in range(GROUP)]
        given = [feats[pl.ds(pl.multiple_of(tile * 16, 16), 16), :] for tile in tiles]
        bases = [pl.ds(pl.multiple_of(tile * 256, 256), 256) for tile in tiles]
        slopes, gains = [], []
        for g, tile in enumerate(tiles):
            rows = slice(g * 256, g * 256 + 256)
            start = pl.multiple_of(tile * 8, 8)
            grad = jnp.concatenate([left[pl.ds(start, 8), :], right[pl.ds(start, 8), :]], axis=1)
            slopes.append(grad)
            colours = stack_splits(given[g][8:16], (0, 1, 0, 2, 0, 1))
            gain = dot(stack_splits(grad, (0, 0, 1, 0, 2, 1)), colours, TN) * keep[bases[g], :]
            one, two = split2(gain)
            gains.append(gain)
            pair[rows, 0:128] = one
            pair[rows, 128:256] = two
        for g, tile in enumerate(tiles):
            rows = slice(g * 256, g * 256 + 256)
            w_one, w_two = split2(keep[bases[g], :])
            three = stack_splits(slopes[g], (0, 1, 2))
            big = dot(three, w_one, NN)
            small = dot(three, w_two, NN)
            by_colour = (big[0:8] + big[8:16]) + (small[0:8] + small[8:16]) + big[16:24]
            behind = dot(pair[rows, :], suf, NN)
            value = alpha[bases[g], :]
            feat = given[g]
            delta_x = jnp.broadcast_to(feat[0:1, :], (16, 128)) - (
                iota((16, 128), 0).astype(F32) + ((tile & 31) * 16).astype(F32)
            )
            delta_v = jnp.broadcast_to(feat[1:2, :], (16, 128)) - (tile_row * 16).astype(F32)
            cost = gains[g] - behind * (value / (1.0 - value))
            sum_0 = jnp.zeros((16, 128), F32)
            sum_1 = jnp.zeros((16, 128), F32)
            sum_2 = jnp.zeros((16, 128), F32)
            for j in range(16):
                delta_y = delta_v - float(j)
                part = cost[j * 16 : j * 16 + 16, :]
                sum_0 = sum_0 + part
                part = part * delta_y
                sum_1 = sum_1 + part
                sum_2 = sum_2 + part * delta_y
            e_0 = total(sum_0)
            e_x = total(sum_0 * delta_x)
            e_y = total(sum_1)
            e_xx = total(sum_0 * delta_x * delta_x)
            e_xy = total(sum_1 * delta_x)
            e_yy = total(sum_2)
            conic_0, conic_1, conic_2 = feat[2:3], feat[3:4], feat[4:5]
            rows_out[pl.ds(pl.multiple_of(tile * 16, 16), 16), :] = jnp.concatenate(
                [
                    -conic_0 * e_x - conic_1 * e_y,
                    -conic_2 * e_y - conic_1 * e_x,
                    -0.5 * e_xx,
                    -e_xy,
                    -0.5 * e_yy,
                    e_0,
                    by_colour[0:3],
                    jnp.zeros((7, 128), F32),
                ],
                axis=0,
            )
        return carry

    lax.fori_loop(0, 64 // GROUP, composite, 0)


def scatter_features(lists, rows_out, acc, half):
    acc[...] = jnp.zeros((576, 128), F32)
    for w in range(2):

        def scatter(step, carry):
            total = None
            for g in range(SCAT):
                tile = w * 32 + (step * SCAT + g) * 2
                idx = jnp.concatenate([lists[pl.ds(tile, 1), :], lists[pl.ds(tile + 1, 1), :]], axis=1)
                both = rows_out[pl.ds(pl.multiple_of(tile * 16, 32), 32), :]
                rows = jnp.concatenate([both[0:9], both[16:25]], axis=1)
                mask = iota((16, 256), 0) + half * 16 == ((idx >> 7) & 31)
                part = add_up(spread_rows(rows, mask), high_onehot(idx))
                total = part if g == 0 else total + part
            acc[w * 144 : w * 144 + 144, :] += total[:, 0:128]
            acc[288 + w * 144 : 288 + w * 144 + 144, :] += total[:, 128:256]
            return carry

        lax.fori_loop(0, 16 // SCAT, scatter, 0)


def return_slots(me, own, recv, acc, pack, back, sems, half):
    is_first = first_half()

    def project_back(step, carry):
        turn = lax.rem(step + lax.div(me, 8), 4)
        high = lax.div(turn, 2)
        low = lax.rem(turn, 2)
        q = high * 4 + half * 2 + low
        values = unpack_slots(recv, q)
        row0 = high * 288 + low * 8

        def grad_of(w, f):
            return acc[pl.ds(pl.multiple_of((w * 9 + f) * 16 + row0, 8), 8), :]

        totals = None
        for w in range(2):
            cam_w = own[w]
            _, pull = jax.vjp(lambda *g: image_values(list(g), cam_w), *values[0:9])
            parts = pull([grad_of(w, f) for f in range(5)])
            totals = parts if totals is None else [a + b for a, b in zip(totals, parts)]
        result = list(totals) + [grad_of(0, 5) + grad_of(1, 5)]
        result += [grad_of(w, 6 + c) for w in range(2) for c in range(3)]
        for f in range(8):
            even = jnp.where(is_first, result[f], half_roll(result[f + 8]))
            odd = jnp.where(is_first, half_roll(result[f]), result[f + 8])
            pack[pl.ds(q * 128 + f, 8, stride=16), :] = even
            pack[pl.ds(q * 128 + 8 + f, 8, stride=16), :] = odd
        push_blocks(pack, back, me, q * 16, 16, sems)
        return carry

    lax.fori_loop(0, 4, project_back, 0)


def first_part(number):
    return lax.rem(lax.div(number, 4), 2)


def own_part(number):
    return lax.rem(lax.div(number, 32), 2)


def finish_part(pack, back, me, sems, early):
    def wait(rows):
        pltpu.make_async_remote_copy(
            src_ref=pack.at[pl.ds(0, rows)],
            dst_ref=back.at[pl.ds(0, rows)],
            send_sem=sems.at[0],
            recv_sem=sems.at[1],
            device_id=device_of(lax.rem(me + 1, 128)),
            device_id_type=MESH,
        ).wait()

    with_own = (first_part(me) == own_part(me)) if early else (first_part(me) != own_part(me))

    @pl.when(with_own)
    def _():
        wait(504)

    @pl.when(jnp.logical_not(with_own))
    def _():
        wait(512)


def scatter_slots(chosen, hot, recv, acc, part_no):
    is_first = first_half()

    def scatter(step, carry):
        totals = [None, None]
        for g in range(BACK):
            p = (step * BACK + g) * 2 + part_no
            onehot = hot[pl.ds(pl.multiple_of(p * 256, 256), 256), :]
            mask = low_mask(chosen[pl.ds(p, 1), :])
            lows, highs = [], []
            for b in range(2):
                start = pl.multiple_of(p * 32 + b * 16, 16)
                even = recv[pl.ds(start, 8), :]
                odd = recv[pl.ds(start + 8, 8), :]
                lows.append(jnp.where(is_first, even, half_roll(odd)))
                highs.append(jnp.where(is_first, half_roll(even), odd))
            for part, pieces in enumerate((lows, highs)):
                rows = jnp.concatenate(pieces, axis=1)
                term = add_up(spread_rows(rows, mask), onehot)
                totals[part] = term if g == 0 else totals[part] + term
        for part in range(2):
            for high in range(2):
                start = high * 512 + part * 256
                acc[start : start + 256, :] += totals[part][:, high * 128 : high * 128 + 128]
        return carry

    lax.fori_loop(0, 16 // BACK, scatter, 0)


def param_slopes(table, group_in, blocks, acc, outs, out, sems):
    def compute(q, carry):
        base = q * 512
        row0 = lax.rem(q, 4) * 8
        high = lax.div(q, 4)

        def load(p):
            return blocks[pl.ds(base + p, 8, stride=64), :]

        def save(p, value):
            outs[pl.ds(base + p, 8, stride=64), :] = value

        def grad_of(f):
            return acc[pl.ds(pl.multiple_of(high * 512 + f * 32 + row0, 8), 8), :]

        group = group_in[pl.ds(pl.multiple_of(row0, 8), 8), pl.ds(pl.multiple_of(high * 128, 128), 128)]
        anchors = group_anchors(table, group)
        mean = [load(0), load(1), load(2)]
        totals = [grad_of(0), grad_of(1), grad_of(2)]
        _, pull = jax.vjp(lambda *g: shape_values(list(g)), *[load(3 + n) for n in range(7)])
        for n, value in enumerate(pull([grad_of(3 + n) for n in range(6)])):
            save(3 + n, value)
        save(10, grad_of(9) / (1.0 + jnp.exp(load(10))))
        colour = [[grad_of(10 + 3 * w + c) for c in range(3)] for w in range(2)]
        bases, pulls = [], []
        for w in range(2):
            anchor = anchors[w]
            basis, pull = jax.vjp(lambda *m: colour_basis(list(m), anchor)[1:], *mean)
            bases.append(basis)
            pulls.append(pull)
        slopes = [[None] * 15, [None] * 15]
        for c in range(3):
            save(11 + 16 * c, HARMONIC_ZERO * (colour[0][c] + colour[1][c]))
            for k in range(15):
                coef = load(12 + 16 * c + k)
                save(12 + 16 * c + k, bases[0][k] * colour[0][c] + bases[1][k] * colour[1][c])
                for w in range(2):
                    term = coef * colour[w][c]
                    slopes[w][k] = term if c == 0 else slopes[w][k] + term
        for w in range(2):
            totals = [a + b for a, b in zip(totals, pulls[w](slopes[w]))]
        for n in range(3):
            save(n, totals[n])
        for n in range(8):
            result_copy(outs, out, q * 8 + n, sems).start()
        return carry

    lax.fori_loop(0, 8, compute, 0)

    def finish(row, carry):
        result_copy(outs, out, row, sems).wait()
        return carry

    lax.fori_loop(0, 64, finish, 0)


def splat_kernel(
    cam_v, cam_s, params, slist, counts, lens, lists, true, out,
    blocks, outs, group, chosen, hot, stab, pos, val, tab_s, stack_s,
    send, recv, tab_d, stack_0, stack_1, feats, alpha, keep, pair, left, right, frame,
    shown, truth, mean, map_m, map_q, map_x, rows_out, acc_d, pack, back, acc_s,
    in_sems, out_sems, send_sems, early_sems, late_sems, shown_sems, truth_sems,
):
    me = own_number()
    tile_row = lax.axis_index("tile")
    barrier = pltpu.get_barrier_semaphore()
    loads = param_copies(params, blocks, in_sems)
    for load in loads:
        load.start()
    own = own_cameras(cam_s, lax.axis_index("view"))
    table = all_anchors(cam_v)
    choose_slots(barrier, me, slist, counts, group, chosen, hot, stab, pos, val)
    true_rows(true, truth, frame)
    for load in loads:
        load.wait()
    source_tables(table, group, blocks, tab_s, stack_s)
    pl.semaphore_wait(barrier, 127)
    send_halo(truth, tile_row, truth_sems)
    send_slots(me, chosen, hot, stack_s, send, recv, send_sems)
    take_halo(truth, tile_row, truth_sems)
    true_means(truth, mean, 0, FIRST_MEANS)
    finish_blocks(send, recv, me, send_sems)
    stacks = [stack_0, stack_1]
    band_tables(own, recv, tab_d, stacks)
    list_features(lists, lens, stacks, feats)
    render_tiles(tile_row, feats, alpha, keep, pair, left, right)
    shown_rows(left, right, frame, shown)
    send_halo(shown, tile_row, shown_sems)
    true_means(truth, mean, FIRST_MEANS, 26 - FIRST_MEANS)
    take_halo(shown, tile_row, shown_sems)
    loss_slopes(tile_row, shown, truth, mean, map_m, map_q, map_x, frame)
    tile_slopes(frame, left, right)
    feature_slopes(tile_row, feats, alpha, keep, pair, left, right, rows_out)
    acc_s[...] = jnp.zeros((1024, 128), F32)
    early = first_part(me)
    scatter_features(lists, rows_out, acc_d, early)
    return_slots(me, own, recv, acc_d, pack, back, early_sems, early)
    scatter_features(lists, rows_out, acc_d, 1 - early)
    return_slots(me, own, recv, acc_d, pack, back, late_sems, 1 - early)
    start = pl.multiple_of(me * 8, 8)
    back[pl.ds(start, 8), :] = pack[pl.ds(start, 8), :]
    finish_part(pack, back, me, early_sems, True)
    scatter_slots(chosen, hot, back, acc_s, own_part(me))
    finish_part(pack, back, me, late_sems, False)
    scatter_slots(chosen, hot, back, acc_s, 1 - own_part(me))
    param_slopes(table, group, blocks, acc_s, outs, out, out_sems)


def struct(shape, dtype=F32):
    return jax.ShapeDtypeStruct(shape, dtype)


VM = pl.BlockSpec(memory_space=pltpu.VMEM)
SM = pl.BlockSpec(memory_space=pltpu.SMEM)
ANY = pl.BlockSpec(memory_space=pl.ANY)


def vm(*shape, dtype=F32):
    return pltpu.VMEM(shape, dtype)


def shards(params, send_list, send_counts, camera, ground_truth, tile_lists, list_lengths):
    lists = tile_lists.reshape(64, 128)
    true = ground_truth.reshape(96, 512)
    dma = pltpu.SemaphoreType.DMA
    return pl.pallas_call(
        splat_kernel,
        out_shape=struct((59, 8192)),
        in_specs=[VM, SM, ANY, VM, VM, SM, VM, VM],
        out_specs=ANY,
        scratch_shapes=[
            vm(4096, 128),
            vm(4096, 128),
            vm(32, 256),
            vm(32, 256, dtype=I32),
            vm(8192, 256, dtype=BF16),
            vm(64, 256),
            vm(32, 256, dtype=I32),
            vm(32, 256),
            vm(512, 256),
            vm(1312, 256, dtype=BF16),
            vm(1024, 128),
            vm(1024, 128),
            vm(576, 256),
            vm(736, 256, dtype=BF16),
            vm(736, 256, dtype=BF16),
            vm(1024, 128),
            vm(16384, 128),
            vm(16384, 128),
            vm(GROUP * 256, 256, dtype=BF16),
            vm(512, 128),
            vm(512, 128),
            vm(512, 128),
            vm(288, 512),
            vm(288, 512),
            vm(26, 8, 512),
            vm(26, 8, 512),
            vm(26, 8, 512),
            vm(26, 8, 512),
            vm(1024, 128),
            vm(576, 128),
            vm(1024, 128),
            vm(1024, 128),
            vm(1024, 128),
            dma((64,)),
            dma((64,)),
            dma((2,)),
            dma((2,)),
            dma((2,)),
            dma((4,)),
            dma((4,)),
        ],
        compiler_params=pltpu.CompilerParams(
            vmem_limit_bytes=VMEM_BYTES, collective_id=0, has_side_effects=True
        ),
        name="splat_gradient",
    )(camera, camera, params, send_list, send_counts, list_lengths, lists, true)


def solution(mesh):
    in_specs = (
        P(None, ("view", "tile")),
        P(("view", "tile"), None),
        P(("view", "tile"), None),
        P(),
        P("view", None, "tile", None),
        P("view", "tile", None, None),
        P("view", "tile", None),
    )
    out_specs = P(None, ("view", "tile"))
    return jax.shard_map(shards, mesh=mesh, in_specs=in_specs, out_specs=out_specs, check_vma=False)
```

```python
import jax
import jax.numpy as jnp
import numpy as np
from jax import lax
from jax.experimental import pallas as pl
from jax.experimental.pallas import tpu as pltpu
from jax.sharding import PartitionSpec as P

F32 = jnp.float32
BF16 = jnp.bfloat16
I32 = jnp.int32

TILE = 16
GROUP = 8
FOCAL = 1000.0
LOW_PASS = 0.3
SSIM_SHARE = 0.2
SMOOTH_EPS = 1e-06
SSIM_ONE = 0.0001
SSIM_TWO = 0.0009
LOG2E = 1.4426950408889634
HARMONIC_ZERO = 0.28209479177387814
HARMONIC_ONE = 0.4886025119029199
HARMONIC_TWO = (
    1.0925484305920792,
    -1.0925484305920792,
    0.31539156525252005,
    -1.0925484305920792,
    0.5462742152960396,
)
HARMONIC_THREE = (
    -0.5900435899266435,
    2.890611442640554,
    -0.4570457994644658,
    0.3731763325901154,
    -0.4570457994644658,
    1.445305721320277,
    -0.5900435899266435,
)
VMEM_BYTES = 56 * 1024 * 1024
CHOOSE = 16
GATHER = 8
LOOKUP = 16
SCAT = 16
BACK = 16
MESH = pl.DeviceIdType.MESH
FIRST_MEANS = 10
NT = (((1,), (1,)), ((), ()))
NN = (((1,), (0,)), ((), ()))
TN = (((0,), (0,)), ((), ()))


def window_taps():
    offsets_np = np.arange(11) - 5.0
    weights = np.exp(-offsets_np * offsets_np / 4.5)
    weights = weights / weights.sum()
    return [float(weight) for weight in weights]


TAPS = window_taps()


def matrix_product(left_side, right_side):
    return [
        [
            left_side[row_idx][0] * right_side[0][col_idx]
            + left_side[row_idx][1] * right_side[1][col_idx]
            + left_side[row_idx][2] * right_side[2][col_idx]
            for col_idx in range(3)
        ]
        for row_idx in range(3)
    ]


def rotation(angles):
    cos_a, sin_a = (jnp.cos(angles[0]), jnp.sin(angles[0]))
    cos_b, sin_b = (jnp.cos(angles[1]), jnp.sin(angles[1]))
    cos_c, sin_c = (jnp.cos(angles[2]), jnp.sin(angles[2]))
    zero, one = jnp.zeros_like(cos_a), jnp.ones_like(cos_a)
    about_x = [[one, zero, zero], [zero, cos_a, -sin_a], [zero, sin_a, cos_a]]
    about_y = [[cos_b, zero, sin_b], [zero, one, zero], [-sin_b, zero, cos_b]]
    about_z = [[cos_c, -sin_c, zero], [sin_c, cos_c, zero], [zero, zero, one]]
    return matrix_product(about_z, matrix_product(about_y, about_x))


def camera_values(numbers):
    rot = rotation(numbers[0:3])
    move = list(numbers[3:6])
    anchor = [
        -(rot[0][c] * move[0] + rot[1][c] * move[1] + rot[2][c] * move[2]) for c in range(3)
    ]
    return rot[0] + rot[1] + rot[2] + move, anchor


def own_cameras(cam, group):
    return [
        camera_values([jnp.full((8, 128), cam[2 * group + w, n], F32) for n in range(6)])[0]
        for w in range(2)
    ]


def all_anchors(cam):
    numbers = [jnp.broadcast_to(cam[:, n : n + 1], (8, 128)) for n in range(6)]
    anchor = camera_values(numbers)[1]
    return [[jnp.broadcast_to(a[n : n + 1, :], (8, 128)) for a in anchor] for n in range(8)]


def own_number():
    return lax.axis_index("view") * 32 + lax.axis_index("tile")


def device_of(number):
    return (lax.div(number, 32), lax.rem(number, 32))


def greet(barrier, me, o):
    pl.semaphore_signal(
        barrier, inc=1, device_id=device_of(lax.rem(me + o, 128)), device_id_type=MESH
    )


def block_copy(pack, recv, me, number, sems):
    return pltpu.make_async_remote_copy(
        src_ref=pack.at[pl.ds(pl.multiple_of(number * 8, 8), 8)],
        dst_ref=recv.at[pl.ds(pl.multiple_of(me * 8, 8), 8)],
        send_sem=sems.at[0],
        recv_sem=sems.at[1],
        device_id=device_of(number),
        device_id_type=MESH,
    )


def push_blocks(pack, recv, me, first, count, sems):
    def push(n, carry):
        number = first + n

        @pl.when(number != me)
        def _():
            block_copy(pack, recv, me, number, sems).start()

        return carry

    lax.fori_loop(0, count, push, 0)


def finish_blocks(pack, recv, me, sems):
    start = pl.multiple_of(me * 8, 8)
    recv[pl.ds(start, 8), :] = pack[pl.ds(start, 8), :]
    whole = pltpu.make_async_remote_copy(
        src_ref=pack.at[pl.ds(0, 1016)],
        dst_ref=recv.at[pl.ds(0, 1016)],
        send_sem=sems.at[0],
        recv_sem=sems.at[1],
        device_id=device_of(lax.rem(me + 1, 128)),
        device_id_type=MESH,
    )
    whole.wait()


def harmonics(dir_x, dir_y, dir_z):
    sq_x, sq_y, sq_z = (dir_x * dir_x, dir_y * dir_y, dir_z * dir_z)
    prod_xy, prod_yz, prod_xz = (dir_x * dir_y, dir_y * dir_z, dir_x * dir_z)
    return [
        None,
        -HARMONIC_ONE * dir_y,
        HARMONIC_ONE * dir_z,
        -HARMONIC_ONE * dir_x,
        HARMONIC_TWO[0] * prod_xy,
        HARMONIC_TWO[1] * prod_yz,
        HARMONIC_TWO[2] * (2.0 * sq_z - sq_x - sq_y),
        HARMONIC_TWO[3] * prod_xz,
        HARMONIC_TWO[4] * (sq_x - sq_y),
        HARMONIC_THREE[0] * dir_y * (3.0 * sq_x - sq_y),
        HARMONIC_THREE[1] * prod_xy * dir_z,
        HARMONIC_THREE[2] * dir_y * (4.0 * sq_z - sq_x - sq_y),
        HARMONIC_THREE[3] * dir_z * (2.0 * sq_z - 3.0 * sq_x - 3.0 * sq_y),
        HARMONIC_THREE[4] * dir_x * (4.0 * sq_z - sq_x - sq_y),
        HARMONIC_THREE[5] * dir_z * (sq_x - sq_y),
        HARMONIC_THREE[6] * dir_x * (sq_x - 3.0 * sq_y),
    ]


def shape_values(gauss):
    scales = [jnp.exp(gauss[axis]) for axis in range(3)]
    norm_inv = 1.0 / jnp.sqrt(
        gauss[3] * gauss[3] + gauss[4] * gauss[4] + gauss[5] * gauss[5] + gauss[6] * gauss[6]
    )
    quat_w, quat_x, quat_y, quat_z = [gauss[3 + n] * norm_inv for n in range(4)]
    quat_rot = [
        [
            1.0 - 2.0 * (quat_y * quat_y + quat_z * quat_z),
            2.0 * (quat_x * quat_y - quat_w * quat_z),
            2.0 * (quat_x * quat_z + quat_w * quat_y),
        ],
        [
            2.0 * (quat_x * quat_y + quat_w * quat_z),
            1.0 - 2.0 * (quat_x * quat_x + quat_z * quat_z),
            2.0 * (quat_y * quat_z - quat_w * quat_x),
        ],
        [
            2.0 * (quat_x * quat_z - quat_w * quat_y),
            2.0 * (quat_y * quat_z + quat_w * quat_x),
            1.0 - 2.0 * (quat_x * quat_x + quat_y * quat_y),
        ],
    ]
    spread = [[quat_rot[r][c] * scales[c] for c in range(3)] for r in range(3)]

    def dot_rows(one, two):
        return (
            spread[one][0] * spread[two][0]
            + spread[one][1] * spread[two][1]
            + spread[one][2] * spread[two][2]
        )

    return [
        dot_rows(0, 0),
        dot_rows(0, 1),
        dot_rows(0, 2),
        dot_rows(1, 1),
        dot_rows(1, 2),
        dot_rows(2, 2),
    ]


def colour_basis(mean, anchor):
    ray_x, ray_y, ray_z = (mean[0] - anchor[0], mean[1] - anchor[1], mean[2] - anchor[2])
    len_inv = 1.0 / jnp.sqrt(ray_x * ray_x + ray_y * ray_y + ray_z * ray_z)
    return harmonics(ray_x * len_inv, ray_y * len_inv, ray_z * len_inv)


def image_values(gauss, cam):
    point = [
        cam[3 * r] * gauss[0] + cam[3 * r + 1] * gauss[1] + cam[3 * r + 2] * gauss[2] + cam[9 + r]
        for r in range(3)
    ]
    inv_depth = 1.0 / point[2]
    jac = FOCAL * inv_depth
    jac_xz = -FOCAL * point[0] * inv_depth * inv_depth
    jac_yz = -FOCAL * point[1] * inv_depth * inv_depth
    row_x = [jac * cam[c] + jac_xz * cam[6 + c] for c in range(3)]
    row_y = [jac * cam[3 + c] + jac_yz * cam[6 + c] for c in range(3)]
    s_xx, s_xy, s_xz, s_yy, s_yz, s_zz = gauss[3:9]
    by_x = [
        s_xx * row_x[0] + s_xy * row_x[1] + s_xz * row_x[2],
        s_xy * row_x[0] + s_yy * row_x[1] + s_yz * row_x[2],
        s_xz * row_x[0] + s_yz * row_x[1] + s_zz * row_x[2],
    ]
    by_y = [
        s_xx * row_y[0] + s_xy * row_y[1] + s_xz * row_y[2],
        s_xy * row_y[0] + s_yy * row_y[1] + s_yz * row_y[2],
        s_xz * row_y[0] + s_yz * row_y[1] + s_zz * row_y[2],
    ]
    cov_xx = row_x[0] * by_x[0] + row_x[1] * by_x[1] + row_x[2] * by_x[2] + LOW_PASS
    cov_xy = row_y[0] * by_x[0] + row_y[1] * by_x[1] + row_y[2] * by_x[2]
    cov_yy = row_y[0] * by_y[0] + row_y[1] * by_y[1] + row_y[2] * by_y[2] + LOW_PASS
    det_inv = 1.0 / (cov_xx * cov_yy - cov_xy * cov_xy)
    return [
        FOCAL * point[0] * inv_depth + 256.0,
        FOCAL * point[1] * inv_depth + 256.0,
        cov_yy * det_inv,
        -cov_xy * det_inv,
        cov_xx * det_inv,
    ]


def split3(value):
    one = value.astype(BF16)
    rest = value - one.astype(F32)
    two = rest.astype(BF16)
    three = (rest - two.astype(F32)).astype(BF16)
    return one, two, three


def split2(value):
    one = value.astype(BF16)
    return one, (value - one.astype(F32)).astype(BF16)


def dot(left, right, dims):
    return lax.dot_general(left, right, dims, preferred_element_type=F32)


def iota(shape, dim):
    return lax.broadcasted_iota(I32, shape, dim)


def high_onehot(idx):
    high = ((idx >> 12) << 7) | (idx & 127)
    return jnp.where(iota((256, idx.shape[1]), 0) == high, 1.0, 0.0).astype(BF16)


def low_mask(idx):
    return iota((32, idx.shape[1]), 0) == ((idx >> 7) & 31)


def stack_tables(tab, stack, rows, exact):
    one, two, three = split3(tab)
    stack[0 : rows * 32, :] = one
    stack[rows * 32 : rows * 64, :] = two
    stack[rows * 64 : rows * 64 + exact * 32, :] = three[0 : exact * 32]


def pick(stack, rows, exact, onehot, mask):
    found = dot(stack, onehot, NN)
    total = found[0 : rows * 32] + found[rows * 32 : rows * 64]
    fine = total[0 : exact * 32] + found[rows * 64 : rows * 64 + exact * 32]

    def low_sum(part, count):
        picked = jnp.where(mask[None], part.reshape(count, 32, mask.shape[1]), 0.0)
        return jnp.sum(picked, axis=1)

    return jnp.concatenate(
        [low_sum(fine, exact), low_sum(total[exact * 32 :], rows - exact)], axis=0
    )


def spread_rows(rows, mask):
    count = rows.shape[0]
    return jnp.where(mask[None], rows[:, None, :], 0.0).reshape(count * mask.shape[0], rows.shape[1])


def add_up(left, onehot):
    size = left.shape[0]
    found = dot(jnp.concatenate(split2(left), axis=0), onehot, NT)
    return found[0:size] + found[size:]


def half_roll(value):
    return pltpu.roll(value, 64, 1)


def first_half():
    return iota((8, 128), 1) < 64


def param_copies(params, blocks, sems):
    return [
        pltpu.make_async_copy(
            params.at[:, pl.ds(row * 128, 128)], blocks.at[pl.ds(row * 64, 59)], sems.at[row]
        )
        for row in range(64)
    ]


def result_copy(outs, out, row, sems):
    return pltpu.make_async_copy(
        outs.at[pl.ds(pl.multiple_of(row * 64, 64), 59)],
        out.at[:, pl.ds(pl.multiple_of(row * 128, 128), 128)],
        sems.at[row],
    )


def group_anchors(table, group):
    anchors = []
    for slot in range(2):
        triple = []
        for c in range(3):
            value = table[slot][c]
            for number in range(1, 4):
                value = jnp.where(group > number + 0.5, table[2 * number + slot][c], value)
            triple.append(value)
        anchors.append(triple)
    return anchors


def choose_slots(barrier, me, slist, counts, group_out, chosen, hot, stab, pos, val):
    def greet_next(o, carry):
        greet(barrier, me, o)
        return carry

    lax.fori_loop(1, 128, greet_next, 0)
    cnt = counts[...].astype(F32)
    lanes = iota((32, 128), 1)
    first = iota((32, 128), 0) * 4
    slot_lane = iota((32, 256), 1)
    off = jnp.zeros((32, 256), F32)
    own = jnp.zeros((32, 256), F32)
    for j in range(4):
        off_j = jnp.sum(jnp.where(lanes < first + j, cnt, 0.0), axis=1, keepdims=True)
        own_j = jnp.sum(jnp.where(lanes == first + j, cnt, 0.0), axis=1, keepdims=True)
        here = (slot_lane >> 6) == j
        off = jnp.where(here, off_j, off)
        own = jnp.where(here, own_j, own)
    place = (slot_lane & 63).astype(F32)
    pos[...] = jnp.minimum(off + place, 8191.0).astype(I32)
    group = (iota((32, 256), 0) >> 3).astype(F32) + 1.0
    val[...] = jnp.where(place < own, group, 0.0)
    for row in range(64):
        piece = slist[:, row * 128 : (row + 1) * 128]
        half = slice((row // 32) * 128, (row // 32) * 128 + 128)
        stab[row % 32 : row % 32 + 1, half] = (piece >> 6).astype(F32)
        stab[32 + row % 32 : 33 + row % 32, half] = (piece & 63).astype(F32)
    group_out[...] = jnp.zeros((32, 256), F32)
    stab_b = stab[...].astype(BF16)

    def choose(step, carry):
        rows = [step * CHOOSE + g for g in range(CHOOSE)]
        places = [pos[pl.ds(p, 1), :] for p in rows]
        found = [dot(stab_b, high_onehot(idx), NN) for idx in places]
        total = None
        for g, p in enumerate(rows):
            both = found[g][0:32] * 64.0 + found[g][32:64]
            ids = jnp.sum(jnp.where(low_mask(places[g]), both, 0.0), axis=0, keepdims=True).astype(I32)
            chosen[pl.ds(p, 1), :] = ids
            onehot = high_onehot(ids)
            hot[pl.ds(pl.multiple_of(p * 256, 256), 256), :] = onehot
            left = jnp.where(low_mask(ids), val[pl.ds(p, 1), :], 0.0).astype(BF16)
            part = dot(left, onehot, NT)
            total = part if g == 0 else total + part
        group_out[...] += total
        return carry

    lax.fori_loop(0, 32 // CHOOSE, choose, 0)


def source_tables(table, group_out, blocks, tab, stack):
    for high in range(2):
        lane_part = slice(high * 128, high * 128 + 128)

        def compute(low, carry):
            base = (high * 4 + low) * 512
            row0 = pl.multiple_of(low * 8, 8)

            def load(p):
                return blocks[pl.ds(base + p, 8, stride=64), :]

            anchors = group_anchors(table, group_out[pl.ds(row0, 8), lane_part])
            mean = [load(0), load(1), load(2)]
            values = mean + shape_values([load(3 + n) for n in range(7)])
            values += [0.99 / (1.0 + jnp.exp(-load(10)))]
            bases = [colour_basis(mean, anchor) for anchor in anchors]
            sums = [[None] * 3, [None] * 3]
            for c in range(3):
                flat = 0.5 + HARMONIC_ZERO * load(11 + 16 * c)
                sums[0][c] = flat
                sums[1][c] = flat
                for k in range(1, 16):
                    coef = load(11 + 16 * c + k)
                    sums[0][c] = sums[0][c] + bases[0][k] * coef
                    sums[1][c] = sums[1][c] + bases[1][k] * coef
            values += sums[0] + sums[1]
            for f in range(16):
                tab[pl.ds(f * 32 + row0, 8), lane_part] = values[f]
            return carry

        lax.fori_loop(0, 4, compute, 0, unroll=2)
    stack_tables(tab[...], stack, 16, 9)


def send_slots(me, chosen, hot, stack, send, recv, sems):
    is_first = first_half()
    shift = lax.div(me, 4) + 1

    def group_at(step, g):
        return lax.rem(step * GATHER + g + shift, 32)

    def gather(step, carry):
        for g in range(GATHER):
            p = group_at(step, g)
            onehot = hot[pl.ds(pl.multiple_of(p * 256, 256), 256), :]
            rows = pick(stack[...], 16, 9, onehot, low_mask(chosen[pl.ds(p, 1), :]))
            for b in range(2):
                one = rows[0:8, b * 128 : b * 128 + 128]
                two = rows[8:16, b * 128 : b * 128 + 128]
                start = pl.multiple_of(p * 32 + b * 16, 16)
                send[pl.ds(start, 8), :] = jnp.where(is_first, one, half_roll(two))
                send[pl.ds(start + 8, 8), :] = jnp.where(is_first, half_roll(one), two)
        for g in range(GATHER):
            push_blocks(send, recv, me, group_at(step, g) * 4, 4, sems)
        return carry

    lax.fori_loop(0, 32 // GATHER, gather, 0)


def unpack_slots(recv, q):
    is_first = first_half()
    low, high = [], []
    for f in range(8):
        even = recv[pl.ds(q * 128 + f, 8, stride=16), :]
        odd = recv[pl.ds(q * 128 + 8 + f, 8, stride=16), :]
        low.append(jnp.where(is_first, even, half_roll(odd)))
        high.append(jnp.where(is_first, half_roll(even), odd))
    return low + high


def block_transpose(value):
    turn = (iota((8, 128), 0) - (iota((8, 128), 1) >> 4)) & 7
    result = value
    for d in range(1, 8):
        moved = pltpu.roll(pltpu.roll(value, d, 0), 128 - 16 * d, 1)
        result = jnp.where(turn == d, moved, result)
    return result


def triangle(keep):
    return jnp.where(keep, 1.0, 0.0).astype(BF16)


def pixel_rows(feat, column, tile_row):
    def row(f):
        return jnp.broadcast_to(feat[f : f + 1, :], (16, 128))

    shift = iota((16, 128), 0).astype(F32) + (column * 16).astype(F32)
    delta_x = row(0) - shift
    square = (-0.5 * LOG2E) * row(2) * delta_x * delta_x
    cross = -LOG2E * row(3) * delta_x
    quad = (-0.5 * LOG2E) * row(4)
    delta_v = row(1) - (tile_row * 16).astype(F32)
    return delta_x, delta_v, square, cross, quad, row(5)


def tile_weights(feats, columns, bases, tile_row, tri, alpha, pair):
    for g, feat in enumerate(feats):
        delta_x, delta_v, square, cross, quad, opacity = pixel_rows(feat, columns[g], tile_row)
        for j in range(16):
            delta_y = delta_v - float(j)
            value = opacity * jnp.exp2(square + delta_y * (cross + quad * delta_y))
            rows = slice(g * 256 + j * 16, g * 256 + j * 16 + 16)
            alpha[pl.ds(pl.multiple_of(bases[g] + j * 16, 16), 16), :] = value
            one, two = split2(jnp.log(1.0 - value))
            pair[rows, 0:128] = one
            pair[rows, 128:256] = two
    weights = []
    for g in range(len(feats)):
        rows = slice(g * 256, g * 256 + 256)
        weights.append(jnp.exp(dot(pair[rows, :], tri, NN)) * alpha[pl.ds(bases[g], 256), :])
    return weights


def stack_splits(value, order):
    one, two, three = split3(value)
    parts = [one.astype(F32), two.astype(F32), three.astype(F32)]
    return jnp.concatenate([parts[n] for n in order], axis=0).astype(BF16)


def greet_bands(tile_row):
    barrier = pltpu.get_barrier_semaphore()
    for step in (1, 31):
        other = lax.rem(tile_row + step, 32)
        pl.semaphore_signal(barrier, inc=1, device_id={"tile": other}, device_id_type=MESH)
    pl.semaphore_wait(barrier, 2)


def halo_copies(rows, tile_row, sems):
    def copy(source, target, step, n):
        return pltpu.make_async_remote_copy(
            src_ref=rows.at[pl.ds(source, 80)],
            dst_ref=rows.at[pl.ds(target, 80)],
            send_sem=sems.at[2 * n],
            recv_sem=sems.at[2 * n + 1],
            device_id={"tile": lax.rem(tile_row + step, 32)},
            device_id_type=MESH,
        )

    return copy(128, 0, 1, 0), copy(80, 208, 31, 1)


def send_halo(rows, tile_row, sems):
    down, up = halo_copies(rows, tile_row, sems)

    @pl.when(tile_row < 31)
    def _():
        down.start()

    @pl.when(tile_row > 0)
    def _():
        up.start()


def take_halo(rows, tile_row, sems):
    down, up = halo_copies(rows, tile_row, sems)

    @pl.when(tile_row < 31)
    def _():
        down.wait_send()
        up.wait_recv()

    @pl.when(tile_row > 0)
    def _():
        up.wait_send()
        down.wait_recv()

    @pl.when(tile_row == 0)
    def _():
        rows[0:80, :] = jnp.zeros((80, 512), F32)

    @pl.when(tile_row == 31)
    def _():
        rows[208:288, :] = jnp.zeros((80, 512), F32)


def true_rows(true, truth, frame):
    frame[...] = jnp.zeros((512, 128), F32)
    for n in range(6):
        for b in range(4):
            for half in range(2):
                rows = true[n * 16 + half * 8 : n * 16 + half * 8 + 8, b * 128 : b * 128 + 128]
                frame[pl.ds(b * 128 + half * 64 + n, 8, stride=8), :] = rows
    for b in range(4):
        truth[80:208, b * 128 : b * 128 + 128] = frame[b * 128 : b * 128 + 128, :]


def band_tables(own, recv, tab, stacks):
    for high in range(2):
        lane_part = slice(high * 128, high * 128 + 128)

        def compute(low, carry):
            row0 = pl.multiple_of(low * 8, 8)
            values = unpack_slots(recv, high * 4 + low)
            for w in range(2):
                seen = image_values(values[0:9], own[w])
                seen = seen + [values[9]] + values[10 + 3 * w : 13 + 3 * w]
                for f in range(9):
                    tab[pl.ds((w * 9 + f) * 32 + row0, 8), lane_part] = seen[f]
            return carry

        lax.fori_loop(0, 4, compute, 0, unroll=2)
    for w in range(2):
        stack_tables(tab[w * 288 : w * 288 + 288, :], stacks[w], 9, 5)


def list_features(lists, lens, tables, feats):
    lane = iota((1, 256), 1)
    for w in range(2):

        def look_up(step, carry):
            for g in range(LOOKUP):
                tile = w * 32 + (step * LOOKUP + g) * 2
                idx = jnp.concatenate([lists[pl.ds(tile, 1), :], lists[pl.ds(tile + 1, 1), :]], axis=1)
                rows = pick(tables[w][...], 9, 5, high_onehot(idx), low_mask(idx))
                length = jnp.where(lane < 128, lens[w, 0, tile - w * 32], lens[w, 0, tile - w * 32 + 1])
                rows = jnp.where((lane & 127) < length, rows, 0.0)
                start = pl.multiple_of(tile * 16, 32)
                for b in range(2):
                    part = rows[:, b * 128 : b * 128 + 128]
                    feats[pl.ds(start + b * 16, 6), :] = part[0:6]
                    feats[pl.ds(start + b * 16 + 6, 2), :] = jnp.zeros((2, 128), F32)
                    feats[pl.ds(start + b * 16 + 8, 3), :] = part[6:9]
                    feats[pl.ds(start + b * 16 + 11, 5), :] = jnp.zeros((5, 128), F32)
            return carry

        lax.fori_loop(0, 16 // LOOKUP, look_up, 0)


def render_tiles(tile_row, feats, alpha, keep, pair, left, right):
    tri = triangle((iota((256, 128), 0) & 127) < iota((256, 128), 1))

    def composite(step, carry):
        tiles = [step * GROUP + g for g in range(GROUP)]
        given = [feats[pl.ds(pl.multiple_of(tile * 16, 16), 16), :] for tile in tiles]
        bases = [pl.multiple_of(tile * 256, 256) for tile in tiles]
        weights = tile_weights(
            given, [tile & 31 for tile in tiles], bases, tile_row, tri, alpha, pair
        )
        for g, tile in enumerate(tiles):
            keep[pl.ds(bases[g], 256), :] = weights[g]
            one, two = split2(weights[g])
            colours = stack_splits(given[g][8:16], (0, 1, 2))
            big = dot(colours, one, NT)
            small = dot(colours, two, NT)
            result = (big[0:8] + big[8:16]) + (small[0:8] + small[8:16]) + big[16:24]
            start = pl.multiple_of(tile * 8, 8)
            left[pl.ds(start, 8), :] = result[:, 0:128]
            right[pl.ds(start, 8), :] = result[:, 128:256]
        return carry

    lax.fori_loop(0, 64 // GROUP, composite, 0)


def shown_rows(left, right, frame, shown):
    for w in range(2):
        for c in range(3):
            for b in range(4):
                for half, source in enumerate((left, right)):
                    block = source[pl.ds((w * 32 + b * 8) * 8 + c, 8, stride=8), :]
                    start = b * 128 + half * 64 + w * 3 + c
                    frame[pl.ds(start, 8, stride=8), :] = block_transpose(block)
    for b in range(4):
        shown[80:208, b * 128 : b * 128 + 128] = frame[b * 128 : b * 128 + 128, :]


def blur_lanes(value):
    padded = jnp.concatenate([value, jnp.zeros((8, 128), F32)], axis=1)
    moved = [pltpu.roll(padded, 639, 1), padded, pltpu.roll(padded, 1, 1), pltpu.roll(padded, 2, 1)]

    def part(far):
        total = None
        for near in range(-1, 3):
            tap = 4 * far + near
            if -5 <= tap <= 5:
                term = TAPS[5 + tap] * moved[near + 1]
                total = term if total is None else total + term
        return total

    total = part(0) + pltpu.roll(part(1), 4, 1) + pltpu.roll(part(-1), 636, 1)
    return total[:, 0:512]


def blur_rows(rows):
    total = TAPS[5] * rows[5]
    for k in range(1, 6):
        total = total + TAPS[5 + k] * (rows[5 - k] + rows[5 + k])
    return total


def at(y):
    return pl.ds(pl.multiple_of(y * 8, 8), 8)


def true_means(truth, mean, first, count):
    def one_row(n, carry):
        y = first + n
        mean[y] = blur_lanes(blur_rows([truth[at(y + k), :] for k in range(11)]))
        return carry

    lax.fori_loop(0, count, one_row, 0, unroll=count // 2)


def loss_slopes(tile_row, shown, truth, mean, map_m, map_q, map_x, frame):
    def similarity(y, carry):
        ones = [shown[at(y + k), :] for k in range(11)]
        twos = [truth[at(y + k), :] for k in range(11)]
        mean_one = blur_lanes(blur_rows(ones))
        mean_two = mean[y]
        squares = blur_lanes(blur_rows([a * a + b * b for a, b in zip(ones, twos)]))
        cross = blur_lanes(blur_rows([a * b for a, b in zip(ones, twos)]))
        num_one = 2.0 * mean_one * mean_two + SSIM_ONE
        num_two = 2.0 * (cross - mean_one * mean_two) + SSIM_TWO
        power = mean_one * mean_one + mean_two * mean_two
        den_one_inv = 1.0 / (power + SSIM_ONE)
        den_two_inv = 1.0 / (squares - power + SSIM_TWO)
        both_inv = den_one_inv * den_two_inv
        value = num_one * num_two * both_inv
        row = tile_row * 16 - 5 + y
        scale = jnp.where((row >= 0) & (row < 512), -SSIM_SHARE, 0.0)
        by_mean = 2.0 * mean_two * (num_two - num_one) * both_inv + 2.0 * mean_one * value * (
            den_two_inv - den_one_inv
        )
        map_m[y] = scale * by_mean
        map_q[y] = (-2.0 * scale) * value * den_two_inv
        map_x[y] = (2.0 * scale) * num_one * both_inv
        return carry

    lax.fori_loop(0, 26, similarity, 0, unroll=2)

    def image_grad(y, carry):
        by_mean = blur_lanes(blur_rows([map_m[y + k] for k in range(11)]))
        by_sq = blur_lanes(blur_rows([map_q[y + k] for k in range(11)]))
        by_cross = blur_lanes(blur_rows([map_x[y + k] for k in range(11)]))
        one = shown[at(y + 10), :]
        two = truth[at(y + 10), :]
        gap = one - two
        result = by_mean + one * by_sq + two * by_cross
        result = result + (1.0 - SSIM_SHARE) * gap / jnp.sqrt(gap * gap + SMOOTH_EPS)
        start = pl.multiple_of(y * 8, 8)
        for b in range(4):
            frame[pl.ds(b * 128 + start, 8), :] = result[:, b * 128 : b * 128 + 128]
        return carry

    lax.fori_loop(0, 16, image_grad, 0, unroll=2)


def tile_slopes(frame, left, right):
    left[...] = jnp.zeros((512, 128), F32)
    right[...] = jnp.zeros((512, 128), F32)
    for w in range(2):
        for c in range(3):
            for b in range(4):
                for half, target in enumerate((left, right)):
                    start = b * 128 + half * 64 + w * 3 + c
                    block = block_transpose(frame[pl.ds(start, 8, stride=8), :])
                    target[pl.ds((w * 32 + b * 8) * 8 + c, 8, stride=8), :] = block


def feature_slopes(tile_row, feats, alpha, keep, pair, left, right, rows_out):
    suf = triangle((iota((256, 128), 0) & 127) > iota((256, 128), 1))

    def total(terms):
        return jnp.sum(terms, axis=0, keepdims=True)

    def composite(step, carry):
        tiles = [step * GROUP + g for g in range(GROUP)]
        given = [feats[pl.ds(pl.multiple_of(tile * 16, 16), 16), :] for tile in tiles]
        bases = [pl.ds(pl.multiple_of(tile * 256, 256), 256) for tile in tiles]
        slopes, gains = [], []
        for g, tile in enumerate(tiles):
            rows = slice(g * 256, g * 256 + 256)
            start = pl.multiple_of(tile * 8, 8)
            grad = jnp.concatenate([left[pl.ds(start, 8), :], right[pl.ds(start, 8), :]], axis=1)
            slopes.append(grad)
            colours = stack_splits(given[g][8:16], (0, 1, 0, 2, 0, 1))
            gain = dot(stack_splits(grad, (0, 0, 1, 0, 2, 1)), colours, TN) * keep[bases[g], :]
            one, two = split2(gain)
            gains.append(gain)
            pair[rows, 0:128] = one
            pair[rows, 128:256] = two
        for g, tile in enumerate(tiles):
            rows = slice(g * 256, g * 256 + 256)
            w_one, w_two = split2(keep[bases[g], :])
            three = stack_splits(slopes[g], (0, 1, 2))
            big = dot(three, w_one, NN)
            small = dot(three, w_two, NN)
            by_colour = (big[0:8] + big[8:16]) + (small[0:8] + small[8:16]) + big[16:24]
            behind = dot(pair[rows, :], suf, NN)
            value = alpha[bases[g], :]
            feat = given[g]
            delta_x = jnp.broadcast_to(feat[0:1, :], (16, 128)) - (
                iota((16, 128), 0).astype(F32) + ((tile & 31) * 16).astype(F32)
            )
            delta_v = jnp.broadcast_to(feat[1:2, :], (16, 128)) - (tile_row * 16).astype(F32)
            cost = gains[g] - behind * (value / (1.0 - value))
            sum_0 = jnp.zeros((16, 128), F32)
            sum_1 = jnp.zeros((16, 128), F32)
            sum_2 = jnp.zeros((16, 128), F32)
            for j in range(16):
                delta_y = delta_v - float(j)
                part = cost[j * 16 : j * 16 + 16, :]
                sum_0 = sum_0 + part
                part = part * delta_y
                sum_1 = sum_1 + part
                sum_2 = sum_2 + part * delta_y
            e_0 = total(sum_0)
            e_x = total(sum_0 * delta_x)
            e_y = total(sum_1)
            e_xx = total(sum_0 * delta_x * delta_x)
            e_xy = total(sum_1 * delta_x)
            e_yy = total(sum_2)
            conic_0, conic_1, conic_2 = feat[2:3], feat[3:4], feat[4:5]
            rows_out[pl.ds(pl.multiple_of(tile * 16, 16), 16), :] = jnp.concatenate(
                [
                    -conic_0 * e_x - conic_1 * e_y,
                    -conic_2 * e_y - conic_1 * e_x,
                    -0.5 * e_xx,
                    -e_xy,
                    -0.5 * e_yy,
                    e_0,
                    by_colour[0:3],
                    jnp.zeros((7, 128), F32),
                ],
                axis=0,
            )
        return carry

    lax.fori_loop(0, 64 // GROUP, composite, 0)


def scatter_features(lists, rows_out, acc, half):
    acc[...] = jnp.zeros((576, 128), F32)
    for w in range(2):

        def scatter(step, carry):
            total = None
            for g in range(SCAT):
                tile = w * 32 + (step * SCAT + g) * 2
                idx = jnp.concatenate([lists[pl.ds(tile, 1), :], lists[pl.ds(tile + 1, 1), :]], axis=1)
                both = rows_out[pl.ds(pl.multiple_of(tile * 16, 32), 32), :]
                rows = jnp.concatenate([both[0:9], both[16:25]], axis=1)
                mask = iota((16, 256), 0) + half * 16 == ((idx >> 7) & 31)
                part = add_up(spread_rows(rows, mask), high_onehot(idx))
                total = part if g == 0 else total + part
            acc[w * 144 : w * 144 + 144, :] += total[:, 0:128]
            acc[288 + w * 144 : 288 + w * 144 + 144, :] += total[:, 128:256]
            return carry

        lax.fori_loop(0, 16 // SCAT, scatter, 0)


def return_slots(me, own, recv, acc, pack, back, sems, half):
    is_first = first_half()

    def project_back(step, carry):
        turn = lax.rem(step + lax.div(me, 8), 4)
        high = lax.div(turn, 2)
        low = lax.rem(turn, 2)
        q = high * 4 + half * 2 + low
        values = unpack_slots(recv, q)
        row0 = high * 288 + low * 8

        def grad_of(w, f):
            return acc[pl.ds(pl.multiple_of((w * 9 + f) * 16 + row0, 8), 8), :]

        totals = None
        for w in range(2):
            cam_w = own[w]
            _, pull = jax.vjp(lambda *g: image_values(list(g), cam_w), *values[0:9])
            parts = pull([grad_of(w, f) for f in range(5)])
            totals = parts if totals is None else [a + b for a, b in zip(totals, parts)]
        result = list(totals) + [grad_of(0, 5) + grad_of(1, 5)]
        result += [grad_of(w, 6 + c) for w in range(2) for c in range(3)]
        for f in range(8):
            even = jnp.where(is_first, result[f], half_roll(result[f + 8]))
            odd = jnp.where(is_first, half_roll(result[f]), result[f + 8])
            pack[pl.ds(q * 128 + f, 8, stride=16), :] = even
            pack[pl.ds(q * 128 + 8 + f, 8, stride=16), :] = odd
        push_blocks(pack, back, me, q * 16, 16, sems)
        return carry

    lax.fori_loop(0, 4, project_back, 0)


def first_part(number):
    return lax.rem(lax.div(number, 4), 2)


def own_part(number):
    return lax.rem(lax.div(number, 32), 2)


def finish_part(pack, back, me, sems, early):
    def wait(rows):
        pltpu.make_async_remote_copy(
            src_ref=pack.at[pl.ds(0, rows)],
            dst_ref=back.at[pl.ds(0, rows)],
            send_sem=sems.at[0],
            recv_sem=sems.at[1],
            device_id=device_of(lax.rem(me + 1, 128)),
            device_id_type=MESH,
        ).wait()

    with_own = (first_part(me) == own_part(me)) if early else (first_part(me) != own_part(me))

    @pl.when(with_own)
    def _():
        wait(504)

    @pl.when(jnp.logical_not(with_own))
    def _():
        wait(512)


def scatter_slots(chosen, hot, recv, acc, part_no):
    is_first = first_half()

    def scatter(step, carry):
        totals = [None, None]
        for g in range(BACK):
            p = (step * BACK + g) * 2 + part_no
            onehot = hot[pl.ds(pl.multiple_of(p * 256, 256), 256), :]
            mask = low_mask(chosen[pl.ds(p, 1), :])
            lows, highs = [], []
            for b in range(2):
                start = pl.multiple_of(p * 32 + b * 16, 16)
                even = recv[pl.ds(start, 8), :]
                odd = recv[pl.ds(start + 8, 8), :]
                lows.append(jnp.where(is_first, even, half_roll(odd)))
                highs.append(jnp.where(is_first, half_roll(even), odd))
            for part, pieces in enumerate((lows, highs)):
                rows = jnp.concatenate(pieces, axis=1)
                term = add_up(spread_rows(rows, mask), onehot)
                totals[part] = term if g == 0 else totals[part] + term
        for part in range(2):
            for high in range(2):
                start = high * 512 + part * 256
                acc[start : start + 256, :] += totals[part][:, high * 128 : high * 128 + 128]
        return carry

    lax.fori_loop(0, 16 // BACK, scatter, 0)


def param_slopes(table, group_in, blocks, acc, outs, out, sems):
    def compute(q, carry):
        base = q * 512
        row0 = lax.rem(q, 4) * 8
        high = lax.div(q, 4)

        def load(p):
            return blocks[pl.ds(base + p, 8, stride=64), :]

        def save(p, value):
            outs[pl.ds(base + p, 8, stride=64), :] = value

        def grad_of(f):
            return acc[pl.ds(pl.multiple_of(high * 512 + f * 32 + row0, 8), 8), :]

        group = group_in[pl.ds(pl.multiple_of(row0, 8), 8), pl.ds(pl.multiple_of(high * 128, 128), 128)]
        anchors = group_anchors(table, group)
        mean = [load(0), load(1), load(2)]
        totals = [grad_of(0), grad_of(1), grad_of(2)]
        _, pull = jax.vjp(lambda *g: shape_values(list(g)), *[load(3 + n) for n in range(7)])
        for n, value in enumerate(pull([grad_of(3 + n) for n in range(6)])):
            save(3 + n, value)
        save(10, grad_of(9) / (1.0 + jnp.exp(load(10))))
        colour = [[grad_of(10 + 3 * w + c) for c in range(3)] for w in range(2)]
        bases, pulls = [], []
        for w in range(2):
            anchor = anchors[w]
            basis, pull = jax.vjp(lambda *m: colour_basis(list(m), anchor)[1:], *mean)
            bases.append(basis)
            pulls.append(pull)
        slopes = [[None] * 15, [None] * 15]
        for c in range(3):
            save(11 + 16 * c, HARMONIC_ZERO * (colour[0][c] + colour[1][c]))
            for k in range(15):
                coef = load(12 + 16 * c + k)
                save(12 + 16 * c + k, bases[0][k] * colour[0][c] + bases[1][k] * colour[1][c])
                for w in range(2):
                    term = coef * colour[w][c]
                    slopes[w][k] = term if c == 0 else slopes[w][k] + term
        for w in range(2):
            totals = [a + b for a, b in zip(totals, pulls[w](slopes[w]))]
        for n in range(3):
            save(n, totals[n])
        for n in range(8):
            result_copy(outs, out, q * 8 + n, sems).start()
        return carry

    lax.fori_loop(0, 8, compute, 0, unroll=2)

    def finish(row, carry):
        result_copy(outs, out, row, sems).wait()
        return carry

    lax.fori_loop(0, 64, finish, 0)


def splat_kernel(
    cam_v, cam_s, params, slist, counts, lens, lists, true, out,
    blocks, outs, group, chosen, hot, stab, pos, val, tab_s, stack_s,
    send, recv, tab_d, stack_0, stack_1, feats, alpha, keep, pair, left, right, frame,
    shown, truth, mean, map_m, map_q, map_x, rows_out, acc_d, pack, back, acc_s,
    in_sems, out_sems, send_sems, early_sems, late_sems, shown_sems, truth_sems,
):
    me = own_number()
    tile_row = lax.axis_index("tile")
    barrier = pltpu.get_barrier_semaphore()
    loads = param_copies(params, blocks, in_sems)
    for load in loads:
        load.start()
    own = own_cameras(cam_s, lax.axis_index("view"))
    table = all_anchors(cam_v)
    choose_slots(barrier, me, slist, counts, group, chosen, hot, stab, pos, val)
    true_rows(true, truth, frame)
    for load in loads:
        load.wait()
    source_tables(table, group, blocks, tab_s, stack_s)
    pl.semaphore_wait(barrier, 127)
    send_halo(truth, tile_row, truth_sems)
    send_slots(me, chosen, hot, stack_s, send, recv, send_sems)
    take_halo(truth, tile_row, truth_sems)
    true_means(truth, mean, 0, FIRST_MEANS)
    finish_blocks(send, recv, me, send_sems)
    stacks = [stack_0, stack_1]
    band_tables(own, recv, tab_d, stacks)
    list_features(lists, lens, stacks, feats)
    render_tiles(tile_row, feats, alpha, keep, pair, left, right)
    shown_rows(left, right, frame, shown)
    send_halo(shown, tile_row, shown_sems)
    true_means(truth, mean, FIRST_MEANS, 26 - FIRST_MEANS)
    take_halo(shown, tile_row, shown_sems)
    loss_slopes(tile_row, shown, truth, mean, map_m, map_q, map_x, frame)
    tile_slopes(frame, left, right)
    feature_slopes(tile_row, feats, alpha, keep, pair, left, right, rows_out)
    acc_s[...] = jnp.zeros((1024, 128), F32)
    early = first_part(me)
    scatter_features(lists, rows_out, acc_d, early)
    return_slots(me, own, recv, acc_d, pack, back, early_sems, early)
    scatter_features(lists, rows_out, acc_d, 1 - early)
    return_slots(me, own, recv, acc_d, pack, back, late_sems, 1 - early)
    start = pl.multiple_of(me * 8, 8)
    back[pl.ds(start, 8), :] = pack[pl.ds(start, 8), :]
    finish_part(pack, back, me, early_sems, True)
    scatter_slots(chosen, hot, back, acc_s, own_part(me))
    finish_part(pack, back, me, late_sems, False)
    scatter_slots(chosen, hot, back, acc_s, 1 - own_part(me))
    param_slopes(table, group, blocks, acc_s, outs, out, out_sems)


def struct(shape, dtype=F32):
    return jax.ShapeDtypeStruct(shape, dtype)


VM = pl.BlockSpec(memory_space=pltpu.VMEM)
SM = pl.BlockSpec(memory_space=pltpu.SMEM)
ANY = pl.BlockSpec(memory_space=pl.ANY)


def vm(*shape, dtype=F32):
    return pltpu.VMEM(shape, dtype)


def shards(params, send_list, send_counts, camera, ground_truth, tile_lists, list_lengths):
    lists = tile_lists.reshape(64, 128)
    true = ground_truth.reshape(96, 512)
    dma = pltpu.SemaphoreType.DMA
    return pl.pallas_call(
        splat_kernel,
        out_shape=struct((59, 8192)),
        in_specs=[VM, SM, ANY, VM, VM, SM, VM, VM],
        out_specs=ANY,
        scratch_shapes=[
            vm(4096, 128),
            vm(4096, 128),
            vm(32, 256),
            vm(32, 256, dtype=I32),
            vm(8192, 256, dtype=BF16),
            vm(64, 256),
            vm(32, 256, dtype=I32),
            vm(32, 256),
            vm(512, 256),
            vm(1312, 256, dtype=BF16),
            vm(1024, 128),
            vm(1024, 128),
            vm(576, 256),
            vm(736, 256, dtype=BF16),
            vm(736, 256, dtype=BF16),
            vm(1024, 128),
            vm(16384, 128),
            vm(16384, 128),
            vm(GROUP * 256, 256, dtype=BF16),
            vm(512, 128),
            vm(512, 128),
            vm(512, 128),
            vm(288, 512),
            vm(288, 512),
            vm(26, 8, 512),
            vm(26, 8, 512),
            vm(26, 8, 512),
            vm(26, 8, 512),
            vm(1024, 128),
            vm(576, 128),
            vm(1024, 128),
            vm(1024, 128),
            vm(1024, 128),
            dma((64,)),
            dma((64,)),
            dma((2,)),
            dma((2,)),
            dma((2,)),
            dma((4,)),
            dma((4,)),
        ],
        compiler_params=pltpu.CompilerParams(
            vmem_limit_bytes=VMEM_BYTES, collective_id=0, has_side_effects=True
        ),
        name="splat_gradient",
    )(camera, camera, params, send_list, send_counts, list_lengths, lists, true)


def solution(mesh):
    in_specs = (
        P(None, ("view", "tile")),
        P(("view", "tile"), None),
        P(("view", "tile"), None),
        P(),
        P("view", None, "tile", None),
        P("view", "tile", None, None),
        P("view", "tile", None),
    )
    out_specs = P(None, ("view", "tile"))
    return jax.shard_map(shards, mesh=mesh, in_specs=in_specs, out_specs=out_specs, check_vma=False)
```
